32 devices in a mesh: rows: 8 (over y, x, core), cols: 4 (over z).
Axes of the slice: x: 2, y: 2, z: 4, core: 2. Of those that a mesh axis runs over, the one named last changes fastest.
Arguments:
- cross_kernel: float32 [8192, 512], P('rows', 'cols'), may hold values from -6 to 6
- factor_panels: float32 [2, 512, 8192], P(None, 'cols', 'rows'), may hold values from -0.25 to 0.25
- block_inverses: float32 [2, 512, 512], P(None, 'cols'), may hold values from -0.5 to 1.5, as said below
Outputs:
- solved: float32 [8192, 512], P('rows', 'cols')
The draws below stay inside these ranges and needn't reach their ends.
Inputs may be any that keep to these rules, and one draw needn't show every extreme that they name: `block_inverses`: each block is lower triangular, with diagonal entries from 0.5 to 1.5.
All inputs are finite; a program needn't handle non-finite values.
Results may differ from the reference program's by a relative error of at most 0.000084.
Values sent between devices are 32-bit elements; how exact they have to be, the bound alone decides.
No kernel may reach another device: no remote copies, remote signals or barrier semaphores. Data moves between devices by JAX's collectives and lax.ppermute only.
A program may use at most 64 MiB of HBM per device.

```python
import math
import jax
import jax.numpy as jnp
from jax import lax

PANEL = 512
ROWS = 8192
CANDS = 512


def draw_block_inverses(key, part):
    key_lower = jax.random.fold_in(key, 11)
    key_diag = jax.random.fold_in(key, 12)
    spread = 0.6 / math.sqrt(PANEL)
    lower = jax.random.normal(key_lower, (2, PANEL, PANEL), jnp.float32) * spread
    lower = jnp.clip(lower, -0.45, 0.45)
    diag = jax.random.uniform(key_diag, (2, PANEL, 1), jnp.float32, 0.5, 1.5)
    row_ids = lax.broadcasted_iota(jnp.int32, (2, PANEL, PANEL), 1)
    col_ids = lax.broadcasted_iota(jnp.int32, (2, PANEL, PANEL), 2)
    zeros = jnp.zeros((2, PANEL, PANEL), jnp.float32)
    return jnp.where(col_ids < row_ids, lower, zeros) + jnp.where(col_ids == row_ids, diag + zeros, zeros)


def steps_of(key, shape, pieces, least, top_value):
    def one(axis_at, parts):
        draws = jax.random.uniform(jax.random.fold_in(jax.random.fold_in(key, 6), axis_at), (parts,), jnp.float32, least / len(pieces), top_value / len(pieces))
        return jnp.repeat(jnp.exp(draws), shape[axis_at] // parts).reshape((-1,) + (1,) * (len(shape) - axis_at - 1))

    factor_of = one(*pieces[0])
    for cut in pieces[1:]:
        factor_of = factor_of * one(*cut)
    return factor_of


def normal_values(key, extent, deviation, most, shards=(), dtype=jnp.bfloat16):
    values = jax.random.normal(key, extent, jnp.float32) * deviation
    if len(shards) > 0:
        values = steps_of(key, extent, shards, -0.22, 0.18) * values
    return jnp.clip(values, min=-most, max=most).astype(dtype)


def setup_inputs(seed: int = 0) -> dict:
    key_list = jax.random.split(jax.random.key(seed), 4)
    cross_kernel = normal_values(key_list[0], (ROWS, CANDS), 1.0, 6.0, ((0, 8), (1, 4)), jnp.float32)
    factor_panels = normal_values(key_list[1], (2, PANEL, ROWS), PANEL ** -0.5, 0.25, ((1, 4), (2, 8)), jnp.float32)
    block_inverses = draw_block_inverses(jax.random.fold_in(key_list[3], 71), 0)
    return dict(cross_kernel=cross_kernel, factor_panels=factor_panels, block_inverses=block_inverses)


def reference(cross_kernel, factor_panels, block_inverses):
    highest = lax.Precision.HIGHEST
    width = PANEL
    first = jnp.dot(block_inverses[0], cross_kernel[:width], precision=highest, preferred_element_type=jnp.float32)
    update = lax.dot_general(factor_panels[0][:, width:], first, (((0,), (0,)), ((), ())), precision=highest, preferred_element_type=jnp.float32)
    rest = cross_kernel[width:] - update
    second = jnp.dot(block_inverses[1], rest[:width], precision=highest, preferred_element_type=jnp.float32)
    update = lax.dot_general(factor_panels[1][:, 2 * width:], second, (((0,), (0,)), ((), ())), precision=highest, preferred_element_type=jnp.float32)
    remain = rest[width:] - update
    return jnp.concatenate([first, second, remain], axis=0)
```

```python
import jax
import jax.numpy as jnp
from jax import lax
from jax.sharding import PartitionSpec as P

AXES = ("rows", "cols")


def dot(left, right, left_dim):
    return lax.dot_general(
        left,
        right,
        (((left_dim,), (0,)), ((), ())),
        precision=lax.Precision.HIGH,
        preferred_element_type=jnp.float32,
    )


def make_on_device(n_rows, n_cols):
    groups = n_cols // 2

    def swap(array, flip, rows):
        pairs = [
            (row * n_cols + col, row * n_cols + (col ^ flip))
            for row in rows
            for col in range(n_cols)
        ]
        return lax.ppermute(array, AXES, pairs)

    def step_down(array, bit, have):
        pairs = [
            (row * n_cols + col, (row | bit) * n_cols + col) for row in have for col in range(n_cols)
        ]
        return lax.ppermute(array, AXES, pairs)

    def broadcast(array, row_id, bits):
        have = [0]
        for bit in bits:
            got = step_down(array, bit, have)
            array = jnp.where((row_id & bit) != 0, got, array)
            have = have + [row | bit for row in have]
        return array

    def broadcast_halves(array, row_id):
        bits = []
        bit = 1
        while bit < n_rows:
            bits.append(bit)
            bit *= 2
        outer, inner = bits[1:], bits[:1]
        half = array.shape[0] // 2
        upper = broadcast(array[:half], row_id, outer + inner)
        lower = broadcast(array[half:], row_id, outer[::-1] + inner)
        return jnp.concatenate([upper, lower], axis=0)

    def on_device(cross_kernel, factor_panels, block_inverses):
        row_id = lax.axis_index("rows")
        col_id = lax.axis_index("cols")
        width = block_inverses.shape[2]
        cands = cross_kernel.shape[1]
        top = [0]
        below = range(1, n_rows)

        inverse = block_inverses[0]
        inverse_pair = jnp.concatenate([inverse, swap(inverse, 1, top)], axis=0)
        rhs = cross_kernel[:width]
        rhs_blocks = jnp.concatenate(
            [rhs] + [swap(rhs, 2 * step, top) for step in range(1, groups)], axis=1
        )
        first_pair = dot(inverse_pair, rhs_blocks, 1)
        first_all = [first_pair]
        for step in range(1, groups):
            got = swap(first_pair, 2 * step, top)
            order = [place ^ step for place in range(groups)]
            first_all.append(
                jnp.concatenate([got[:, at * cands : (at + 1) * cands] for at in order], axis=1)
            )
        first_all = jnp.concatenate(first_all, axis=0)
        corner = factor_panels[0, :, width : 2 * width]
        corner_all = jnp.concatenate(
            [corner] + [swap(corner, flip, top) for flip in range(1, n_cols)], axis=0
        )
        rhs = cross_kernel[width : 2 * width]
        rhs_blocks = jnp.concatenate(
            [rhs] + [swap(rhs, 2 * step, top) for step in range(1, groups)], axis=1
        )
        inverse = block_inverses[1]
        inverse_pair = jnp.concatenate([inverse, swap(inverse, 1, top)], axis=0)
        second_pair = dot(inverse_pair, rhs_blocks - dot(corner_all, first_all, 0), 1)

        solved_pair = jnp.concatenate(
            [broadcast_halves(first_pair, row_id), broadcast_halves(second_pair, row_id)], axis=0
        )
        factors = factor_panels
        factors_other = swap(factors, 1, below)
        stacked = jnp.concatenate(
            [factors[0], factors_other[0], factors[1], factors_other[1]], axis=0
        )
        fresh = cross_kernel
        partials = []
        for step in range(1, groups):
            block = solved_pair[:, step * cands : (step + 1) * cands]
            partials.append(swap(dot(stacked, block, 0), 2 * step, below))
        fresh = fresh - dot(stacked, solved_pair[:, :cands], 0)
        for partial in partials:
            fresh = fresh - partial

        second_all = jnp.concatenate(
            [second_pair[:, :cands]]
            + [
                swap(second_pair[:, step * cands : (step + 1) * cands], 2 * step, top)
                for step in range(1, groups)
            ],
            axis=0,
        )
        order = jnp.arange(n_cols) ^ col_id
        both = jnp.stack([first_all[:, :cands], second_all])
        both = both.reshape(2, n_cols, width // n_cols, cands)
        both = jnp.take(both, order, axis=1).reshape(2 * width, cands)
        head = jnp.where(row_id == 0, both, fresh[: 2 * width])
        return jnp.concatenate([head, fresh[2 * width :]], axis=0)

    return on_device


def solution(mesh):
    in_specs = (P("rows", "cols"), P(None, "cols", "rows"), P(None, "cols", None))
    out_specs = P("rows", "cols")
    return jax.shard_map(
        make_on_device(mesh.shape["rows"], mesh.shape["cols"]),
        mesh=mesh,
        in_specs=in_specs,
        out_specs=out_specs,
        check_vma=False,
    )
```

```python
import jax
import jax.numpy as jnp
from jax import lax
from jax.sharding import PartitionSpec as P

AXES = ("rows", "cols")
CHUNKS = 4


def dot(left, right, left_dim):
    return lax.dot_general(
        left,
        right,
        (((left_dim,), (0,)), ((), ())),
        precision=lax.Precision.HIGH,
        preferred_element_type=jnp.float32,
    )


def make_on_device(n_rows, n_cols):
    half = n_cols // 2

    def swap(array, flip, rows):
        pairs = [
            (row * n_cols + col, row * n_cols + (col ^ flip))
            for row in rows
            for col in range(n_cols)
        ]
        return lax.ppermute(array, AXES, pairs)

    def send_down(array, offset, have):
        pairs = [
            (row * n_cols + col, (row + offset) * n_cols + col) for row in have for col in range(n_cols)
        ]
        return lax.ppermute(array, AXES, pairs)

    def spread(array, row_id, stages, have):
        for low, radix in stages:
            digit = (row_id // low) % radix
            result = array
            for step in range(radix - 1, 0, -1):
                result = jnp.where(digit == step, send_down(array, step * low, have), result)
            array = result
            have = [row + step * low for row in have for step in range(radix)]
        return array

    def broadcast_outer(array, row_id):
        stages = []
        low = 2
        while low < n_rows:
            radix = min(4, n_rows // low)
            stages.append((low, radix))
            low *= radix
        return spread(array, row_id, stages[::-1], [0])

    def broadcast_inner(array, row_id):
        return spread(array, row_id, [(1, 2)], range(0, n_rows, 2))

    def block(array, place, cands):
        return array[:, place * cands : (place + 1) * cands]

    def shuffle(array, flip, cands):
        return jnp.concatenate([block(array, at ^ flip, cands) for at in range(half)], axis=1)

    def in_order(pieces, col_id):
        offsets = [at for step in range(half) for at in (step, step ^ half)]
        pieces = [pieces[offsets.index(at)] for at in range(n_cols)]
        bit = 1
        while bit < n_cols:
            flipped = (col_id & bit) != 0
            pieces = [
                jnp.where(flipped, pieces[at ^ bit], pieces[at]) for at in range(n_cols)
            ]
            bit *= 2
        return pieces

    def on_device(cross_kernel, factor_panels, block_inverses):
        row_id = lax.axis_index("rows")
        col_id = lax.axis_index("cols")
        width = block_inverses.shape[2]
        depth = block_inverses.shape[1]
        n_design, cands = cross_kernel.shape
        piece = n_design // CHUNKS
        top = [0]
        below = range(1, n_rows)

        def with_other(array, rows):
            return jnp.concatenate([array, swap(array, half, rows)], axis=0)

        def with_blocks(array):
            return jnp.concatenate(
                [array] + [swap(array, step, top) for step in range(1, half)], axis=1
            )

        def others(pair):
            got = [swap(block(pair, step, cands), step, top) for step in range(1, half)]
            return [block(pair, 0, cands)] + got

        arrived = []
        for at in range(CHUNKS):
            mine = factor_panels[:, :, at * piece : (at + 1) * piece]
            arrived.append(swap(mine, half, below))

        rhs = with_blocks(cross_kernel[: 2 * width])
        lead = jnp.concatenate(
            [block_inverses[0], factor_panels[0, :, width : 2 * width]], axis=1
        )
        lead = with_other(lead, top)
        inverse = with_other(block_inverses[1], top)
        first = dot(lead[:, :width], rhs[:width], 1)
        update = dot(lead[:, width:], first, 0)
        update, arrived[0] = lax.optimization_barrier((update, arrived[0]))
        bit = 1
        while bit < half:
            update = update + shuffle(swap(update, bit, top), bit, cands)
            bit *= 2
        first_half = broadcast_outer(first, row_id)
        rest = rhs[width:] - update
        rest, first_half, arrived[1] = lax.optimization_barrier((rest, first_half, arrived[1]))
        second = dot(inverse, rest, 1)
        second_half = broadcast_outer(second, row_id)
        second_half, arrived[2] = lax.optimization_barrier((second_half, arrived[2]))
        solved = jnp.concatenate(
            [broadcast_inner(first_half, row_id), broadcast_inner(second_half, row_id)], axis=0
        )

        pair = jnp.concatenate([first, second], axis=0)
        pieces = [[], []]
        for got in others(pair):
            for at in range(4):
                pieces[at // 2].append(got[at * depth : (at + 1) * depth])
        top_rows = jnp.concatenate(
            in_order(pieces[0], col_id) + in_order(pieces[1], col_id), axis=0
        )

        fresh = []
        for at in range(CHUNKS):
            part = slice(at * piece, (at + 1) * piece)
            mine = factor_panels[:, :, part]
            other, solved = lax.optimization_barrier((arrived[at], solved))
            stacked = jnp.concatenate([mine[0], other[0], mine[1], other[1]], axis=0)
            partial = dot(stacked, solved, 0)
            total = cross_kernel[part] - block(partial, 0, cands)
            for step in range(1, half):
                total = total - swap(block(partial, step, cands), step, below)
            fresh.append(total)
        fresh = jnp.concatenate(fresh, axis=0)
        head = jnp.where(row_id == 0, top_rows, fresh[: 2 * width])
        return jnp.concatenate([head, fresh[2 * width :]], axis=0)

    return on_device


def solution(mesh):
    in_specs = (P("rows", "cols"), P(None, "cols", "rows"), P(None, "cols", None))
    out_specs = P("rows", "cols")
    return jax.shard_map(
        make_on_device(mesh.shape["rows"], mesh.shape["cols"]),
        mesh=mesh,
        in_specs=in_specs,
        out_specs=out_specs,
        check_vma=False,
    )
```

```python
import jax
import jax.numpy as jnp
from jax import lax
from jax.sharding import PartitionSpec as P

AXES = ("rows", "cols")


def dot(left, right, left_dim):
    return lax.dot_general(
        left,
        right,
        (((left_dim,), (0,)), ((), ())),
        precision=lax.Precision.HIGH,
        preferred_element_type=jnp.float32,
    )


def make_on_device(n_rows, n_cols):
    half = n_cols // 2

    def swap(array, flip, rows):
        pairs = [
            (row * n_cols + col, row * n_cols + (col ^ flip))
            for row in rows
            for col in range(n_cols)
        ]
        return lax.ppermute(array, AXES, pairs)

    def send_down(array, offset, have):
        pairs = [
            (row * n_cols + col, (row + offset) * n_cols + col) for row in have for col in range(n_cols)
        ]
        return lax.ppermute(array, AXES, pairs)

    def spread(array, row_id, stages, have):
        for low, radix in stages:
            digit = (row_id // low) % radix
            result = array
            for step in range(radix - 1, 0, -1):
                result = jnp.where(digit == step, send_down(array, step * low, have), result)
            array = result
            have = [row + step * low for row in have for step in range(radix)]
        return array

    def broadcast_outer(array, row_id):
        stages = []
        low = 2
        while low < n_rows:
            radix = min(4, n_rows // low)
            stages.append((low, radix))
            low *= radix
        return spread(array, row_id, stages[::-1], [0])

    def broadcast_inner(array, row_id):
        return spread(array, row_id, [(1, 2)], range(0, n_rows, 2))

    def block(array, place, cands):
        return array[:, place * cands : (place + 1) * cands]

    def shuffle(array, flip, cands):
        return jnp.concatenate([block(array, at ^ flip, cands) for at in range(half)], axis=1)

    def in_order(pieces, col_id):
        offsets = [at for step in range(half) for at in (step, step ^ half)]
        pieces = [pieces[offsets.index(at)] for at in range(n_cols)]
        bit = 1
        while bit < n_cols:
            flipped = (col_id & bit) != 0
            pieces = [
                jnp.where(flipped, pieces[at ^ bit], pieces[at]) for at in range(n_cols)
            ]
            bit *= 2
        return pieces

    def on_device(cross_kernel, factor_panels, block_inverses):
        row_id = lax.axis_index("rows")
        col_id = lax.axis_index("cols")
        width = block_inverses.shape[2]
        depth = block_inverses.shape[1]
        n_design, cands = cross_kernel.shape
        cuts = [0, 3 * n_design // 8, 5 * n_design // 8, n_design]
        parts = [slice(start, stop) for start, stop in zip(cuts, cuts[1:])]
        top = [0]
        below = range(1, n_rows)

        def with_other(array, rows):
            return jnp.concatenate([array, swap(array, half, rows)], axis=0)

        def with_blocks(array):
            return jnp.concatenate(
                [array] + [swap(array, step, top) for step in range(1, half)], axis=1
            )

        def others(pair):
            got = [swap(block(pair, step, cands), step, top) for step in range(1, half)]
            return [block(pair, 0, cands)] + got

        flat = factor_panels.reshape(2 * depth, n_design)

        inverses = block_inverses.reshape(2 * depth, width)
        inverses_other = swap(inverses, half, top)
        corner = factor_panels[0, :, width : 2 * width]
        rhs, corner = lax.optimization_barrier((cross_kernel, corner))
        rhs = with_blocks(rhs[: 2 * width])
        corner = with_other(corner, top)
        arrived = [swap(flat[:, parts[0]], half, range(2, n_rows))]
        arrived += [swap(flat[:, part], half, below) for part in parts[1:]]

        inverse = jnp.concatenate([inverses[:depth], inverses_other[:depth]], axis=0)
        first = dot(inverse, rhs[:width], 1)
        first, late = lax.optimization_barrier((first, flat[:, parts[0]]))
        late = swap(late, half, range(1, min(2, n_rows)))
        update = dot(corner, first, 0)
        update, arrived[0] = lax.optimization_barrier((update, arrived[0]))
        bit = 1
        while bit < half:
            update = update + shuffle(swap(update, bit, top), bit, cands)
            bit *= 2
        first_half = broadcast_outer(first, row_id)
        rest = rhs[width:] - update
        rest, first_half, arrived[1] = lax.optimization_barrier((rest, first_half, arrived[1]))
        inverse = jnp.concatenate([inverses[depth:], inverses_other[depth:]], axis=0)
        second = dot(inverse, rest, 1)
        second_half = broadcast_outer(second, row_id)
        halves = [broadcast_inner(first_half, row_id), broadcast_inner(second_half, row_id)]
        solved = jnp.concatenate(
            [got[at : at + depth] for at in (0, depth) for got in halves], axis=0
        )

        pair = jnp.concatenate([first, second], axis=0)
        pieces = [[], []]
        for got in others(pair):
            for at in range(4):
                pieces[at // 2].append(got[at * depth : (at + 1) * depth])
        top_rows = jnp.concatenate(
            in_order(pieces[0], col_id) + in_order(pieces[1], col_id), axis=0
        )

        fresh = []
        arrived[0], late, solved = lax.optimization_barrier((arrived[0], late, solved))
        arrived[0] = jnp.where(row_id == 1, late, arrived[0])
        for part, other in zip(parts, arrived):
            stacked = jnp.concatenate([flat[:, part], other], axis=0)
            partial = dot(stacked, solved, 0)
            partial, solved = lax.optimization_barrier((partial, solved))
            total = cross_kernel[part] - block(partial, 0, cands)
            for step in range(1, half):
                total = total - swap(block(partial, step, cands), step, below)
            fresh.append(total)
        fresh = jnp.concatenate(fresh, axis=0)
        head = jnp.where(row_id == 0, top_rows, fresh[: 2 * width])
        return jnp.concatenate([head, fresh[2 * width :]], axis=0)

    return on_device


def solution(mesh):
    in_specs = (P("rows", "cols"), P(None, "cols", "rows"), P(None, "cols", None))
    out_specs = P("rows", "cols")
    return jax.shard_map(
        make_on_device(mesh.shape["rows"], mesh.shape["cols"]),
        mesh=mesh,
        in_specs=in_specs,
        out_specs=out_specs,
        check_vma=False,
    )
```

```python
import functools
import jax
import jax.numpy as jnp
from jax import lax
from jax.experimental import pallas as pl
from jax.experimental.pallas import tpu as pltpu
from jax.sharding import PartitionSpec as P

AXES = ("rows", "cols")
EIGHTHS = (0, 2, 3, 5, 8)
PARAMS = pltpu.CompilerParams(vmem_limit_bytes=24 * 1024 * 1024)


def split(array):
    high = array.astype(jnp.bfloat16)
    return high, (array - high.astype(jnp.float32)).astype(jnp.bfloat16)


def dot(left, right, left_dim):
    def one(a, b):
        return lax.dot_general(
            a, b, (((left_dim,), (0,)), ((), ())), preferred_element_type=jnp.float32
        )

    left_high, left_low = split(left)
    right_high, right_low = split(right)
    return one(left_high, right_high) + (one(left_high, right_low) + one(left_low, right_high))


def call(kernel, shapes, n_in, flops, *args):
    return pl.pallas_call(
        kernel,
        out_shape=[jax.ShapeDtypeStruct(shape, jnp.float32) for shape in shapes],
        in_specs=[pl.BlockSpec(memory_space=pltpu.VMEM)] * n_in
        + [pl.BlockSpec(memory_space=pltpu.SMEM)] * (len(args) - n_in),
        out_specs=[pl.BlockSpec(memory_space=pltpu.VMEM)] * len(shapes),
        compiler_params=PARAMS,
        cost_estimate=pl.CostEstimate(flops=flops, bytes_accessed=0, transcendentals=0),
    )(*args)


def first_kernel(places, width, lead, lead_other, rhs, *refs):
    others, (low, solved, update, shuffled) = refs[:-4], refs[-4:]
    cands = rhs.shape[1]
    blocks = [rhs[...]] + [other[...] for other in others]
    blocks = jnp.concatenate(blocks, axis=1)
    inverse = jnp.concatenate([lead[:, :width], lead_other[:, :width]], axis=0)
    first = dot(inverse, blocks, 1)
    solved[...] = first
    corner = jnp.concatenate([lead[:, width:], lead_other[:, width:]], axis=0)
    total = dot(corner, first, 0)
    pieces = [total[:, at * cands : (at + 1) * cands] for at in range(len(places))]
    pieces[0] = pieces[0] - low[...]
    for at, place in enumerate(places):
        update[:, at * cands : (at + 1) * cands] = pieces[at]
        shuffled[:, at * cands : (at + 1) * cands] = pieces[place]


def second_kernel(inverse, inverse_other, update, got, solved):
    both = jnp.concatenate([inverse[...], inverse_other[...]], axis=0)
    solved[...] = dot(both, -(update[...] + got[...]), 1)


def chunk_kernel(part, mine, other, late, first, second, base, beside, own, send):
    cands = base.shape[1]
    depth = first.shape[0] // 2
    other = other[...]
    if late is not None:
        other = jnp.where(beside[0] == 1, late[:, part], other)
    factors = jnp.concatenate([mine[...], other], axis=0)
    solved = jnp.concatenate(
        [first[:depth], second[:depth], first[depth:], second[depth:]], axis=0
    )
    partial = dot(factors, solved, 0)
    own[...] = base[...] - partial[:, :cands]
    send[...] = partial[:, cands:]


def chunk_kernel_plain(part, mine, other, first, second, base, beside, own, send):
    chunk_kernel(part, mine, other, None, first, second, base, beside, own, send)


def make_on_device(n_rows, n_cols):
    half = n_cols // 2

    def swap(array, flip, rows):
        pairs = [
            (row * n_cols + col, row * n_cols + (col ^ flip))
            for row in rows
            for col in range(n_cols)
        ]
        return lax.ppermute(array, AXES, pairs)

    def send_down(array, offset, have):
        pairs = [
            (row * n_cols + col, (row + offset) * n_cols + col) for row in have for col in range(n_cols)
        ]
        return lax.ppermute(array, AXES, pairs)

    def spread(array, row_id, stages, have):
        for low, radix in stages:
            digit = (row_id // low) % radix
            result = array
            for step in range(radix - 1, 0, -1):
                result = jnp.where(digit == step, send_down(array, step * low, have), result)
            array = result
            have = [row + step * low for row in have for step in range(radix)]
        return array

    def broadcast_outer(array, row_id):
        stages = []
        low = 2
        while low < n_rows:
            radix = min(4, n_rows // low)
            stages.append((low, radix))
            low *= radix
        return spread(array, row_id, stages[::-1], [0])

    def broadcast_inner(array, row_id):
        return spread(array, row_id, [(1, 2)], range(0, n_rows, 2))

    def block(array, place, cands):
        return array[:, place * cands : (place + 1) * cands]

    def shuffle(array, flip, cands):
        return jnp.concatenate([block(array, at ^ flip, cands) for at in range(half)], axis=1)

    def in_order(pieces, col_id):
        offsets = [at for step in range(half) for at in (step, step ^ half)]
        pieces = [pieces[offsets.index(at)] for at in range(n_cols)]
        bit = 1
        while bit < n_cols:
            flipped = (col_id & bit) != 0
            pieces = [
                jnp.where(flipped, pieces[at ^ bit], pieces[at]) for at in range(n_cols)
            ]
            bit *= 2
        return pieces

    def on_device(cross_kernel, factor_panels, block_inverses):
        row_id = lax.axis_index("rows")
        col_id = lax.axis_index("cols")
        width = block_inverses.shape[2]
        depth = block_inverses.shape[1]
        n_design, cands = cross_kernel.shape
        cuts = [n_design * at // 8 for at in EIGHTHS]
        parts = [slice(start, stop) for start, stop in zip(cuts, cuts[1:])]
        early = slice(0, cuts[-2])
        top = [0]
        beside = range(1, min(2, n_rows))
        below = range(2, n_rows)
        flat = factor_panels.reshape(2 * depth, n_design)
        mine = [flat[:, part] for part in parts]

        lead = jnp.concatenate(
            [block_inverses[0], factor_panels[0, :, width : 2 * width]], axis=1
        )
        lead, rhs = lax.optimization_barrier((lead, cross_kernel[:width]))
        lead_other = swap(lead, half, top)
        rhs_others = [swap(rhs, step, top) for step in range(1, half)]
        arrived = [swap(piece, half, below) for piece in mine[:-1]]
        arrived.append(swap(mine[-1], half, range(1, n_rows)))

        first, update, shuffled = call(
            functools.partial(first_kernel, [at ^ 1 for at in range(half)], width),
            [(2 * depth, half * cands)] + [(width, half * cands)] * 2,
            4 + len(rhs_others),
            6 * width * half * cands * (2 * depth + 2 * depth),
            lead,
            lead_other,
            rhs,
            *rhs_others,
            cross_kernel[width : 2 * width],
        )
        first, inverse, late = lax.optimization_barrier((first, block_inverses[1], flat[:, early]))
        late = swap(late, half, beside)
        inverse_other = swap(inverse, half, top)
        shuffled, arrived[0] = lax.optimization_barrier((shuffled, arrived[0]))
        got = swap(shuffled, 1, top)
        bit = 2
        while bit < half:
            update = update + got
            got = swap(shuffle(update, bit, cands), bit, top)
            bit *= 2
        first_half = broadcast_outer(first, row_id)
        got, first_half, arrived[1] = lax.optimization_barrier((got, first_half, arrived[1]))
        (second,) = call(
            second_kernel,
            [(2 * depth, half * cands)],
            4,
            6 * 2 * depth * width * half * cands,
            inverse,
            inverse_other,
            update,
            got,
        )
        second_half = broadcast_outer(second, row_id)
        second_half, arrived[2] = lax.optimization_barrier((second_half, arrived[2]))
        solved = [broadcast_inner(first_half, row_id), broadcast_inner(second_half, row_id)]

        pair = jnp.concatenate([first, second], axis=0)
        others = [block(pair, 0, cands)]
        others += [swap(block(pair, step, cands), step, top) for step in range(1, half)]
        pieces = [[], []]
        for got in others:
            for at in range(4):
                pieces[at // 2].append(got[at * depth : (at + 1) * depth])
        top_rows = jnp.concatenate(
            in_order(pieces[0], col_id) + in_order(pieces[1], col_id), axis=0
        )

        is_beside = (row_id == 1).astype(jnp.int32).reshape(1)
        fresh = []
        for at, part in enumerate(parts):
            last = at == len(parts) - 1
            args = [mine[at], arrived[at]] + ([] if last else [late])
            args += [*solved, cross_kernel[part]]
            count = part.stop - part.start
            own, send = call(
                functools.partial(chunk_kernel_plain if last else chunk_kernel, part),
                [(count, cands), (count, (half - 1) * cands)],
                len(args),
                6 * count * 4 * depth * half * cands,
                *args,
                is_beside,
            )
            own, send, solved[0], solved[1] = lax.optimization_barrier((own, send, *solved))
            for step in range(1, half):
                own = own - swap(block(send, step - 1, cands), step, range(1, n_rows))
            fresh.append(own)
        fresh = jnp.concatenate(fresh, axis=0)
        head = jnp.where(row_id == 0, top_rows, fresh[: 2 * width])
        return jnp.concatenate([head, fresh[2 * width :]], axis=0)

    return on_device


def solution(mesh):
    in_specs = (P("rows", "cols"), P(None, "cols", "rows"), P(None, "cols", None))
    out_specs = P("rows", "cols")
    return jax.shard_map(
        make_on_device(mesh.shape["rows"], mesh.shape["cols"]),
        mesh=mesh,
        in_specs=in_specs,
        out_specs=out_specs,
        check_vma=False,
    )
```

```python
import functools
import jax
import jax.numpy as jnp
from jax import lax
from jax.experimental import pallas as pl
from jax.experimental.pallas import tpu as pltpu
from jax.sharding import PartitionSpec as P

AXES = ("rows", "cols")
EIGHTHS = (0, 4, 5, 8)
PARAMS = pltpu.CompilerParams(vmem_limit_bytes=24 * 1024 * 1024)


def split(array):
    high = array.astype(jnp.bfloat16)
    return high, (array - high.astype(jnp.float32)).astype(jnp.bfloat16)


def dot(left, right, left_dim):
    def one(a, b):
        return lax.dot_general(
            a, b, (((left_dim,), (0,)), ((), ())), preferred_element_type=jnp.float32
        )

    left_high, left_low = split(left)
    right_high, right_low = split(right)
    return one(left_high, right_high) + (one(left_high, right_low) + one(left_low, right_high))


def call(kernel, shapes, n_in, flops, *args):
    return pl.pallas_call(
        kernel,
        out_shape=[jax.ShapeDtypeStruct(shape, jnp.float32) for shape in shapes],
        in_specs=[pl.BlockSpec(memory_space=pltpu.VMEM)] * n_in
        + [pl.BlockSpec(memory_space=pltpu.SMEM)] * (len(args) - n_in),
        out_specs=[pl.BlockSpec(memory_space=pltpu.VMEM)] * len(shapes),
        compiler_params=PARAMS,
        cost_estimate=pl.CostEstimate(flops=flops, bytes_accessed=0, transcendentals=0),
    )(*args)


def first_kernel(places, width, lead, lead_other, rhs, *refs):
    others, (low, solved, update, shuffled) = refs[:-4], refs[-4:]
    cands = rhs.shape[1]
    blocks = [rhs[...]] + [other[...] for other in others]
    blocks = jnp.concatenate(blocks, axis=1)
    inverse = jnp.concatenate([lead[:, :width], lead_other[:, :width]], axis=0)
    first = dot(inverse, blocks, 1)
    solved[...] = first
    corner = jnp.concatenate([lead[:, width : 2 * width], lead_other[:, width : 2 * width]], axis=0)
    total = dot(corner, first, 0)
    pieces = [total[:, at * cands : (at + 1) * cands] for at in range(len(places))]
    pieces[0] = pieces[0] - low[...]
    for at, place in enumerate(places):
        update[:, at * cands : (at + 1) * cands] = pieces[at]
        shuffled[:, at * cands : (at + 1) * cands] = pieces[place]


def second_kernel(start, lead, lead_other, update, got, solved):
    both = jnp.concatenate([lead[:, start:], lead_other[:, start:]], axis=0)
    solved[...] = dot(both, -(update[...] + got[...]), 1)


def chunk_kernel(mine, others, late, first, second, base, beside, own, send):
    cands = base.shape[1]
    depth = first.shape[0] // 2
    other = jnp.concatenate([piece[...] for piece in others], axis=1)
    if late is not None:
        other = jnp.where(beside[0] == 1, late[...], other)
    factors = jnp.concatenate([mine[...], other], axis=0)
    solved = jnp.concatenate(
        [first[:depth], second[:depth], first[depth:], second[depth:]], axis=0
    )
    partial = dot(factors, solved, 0)
    own[...] = base[...] - partial[:, :cands]
    send[...] = partial[:, cands:]


def early_kernel(mine, one, two, late, *refs):
    chunk_kernel(mine, [one, two], late, *refs)


def late_kernel(mine, one, *refs):
    chunk_kernel(mine, [one], None, *refs)


def make_on_device(n_rows, n_cols):
    half = n_cols // 2

    def swap(array, flip, rows):
        pairs = [
            (row * n_cols + col, row * n_cols + (col ^ flip))
            for row in rows
            for col in range(n_cols)
        ]
        return lax.ppermute(array, AXES, pairs)

    def send_down(array, offset, have):
        pairs = [
            (row * n_cols + col, (row + offset) * n_cols + col) for row in have for col in range(n_cols)
        ]
        return lax.ppermute(array, AXES, pairs)

    def spread(array, row_id, low, radix, have):
        digit = (row_id // low) % radix
        result = array
        for step in range(radix - 1, 0, -1):
            result = jnp.where(digit == step, send_down(array, step * low, have), result)
        return result, [row + step * low for row in have for step in range(radix)]

    def broadcast_outer(array, row_id):
        low = n_rows
        have = [0]
        while low > 2:
            radix = min(4, low // 2)
            low //= radix
            array, have = spread(array, row_id, low, radix, have)
        return array

    def broadcast_inner(array, row_id, start=0):
        return jnp.where(row_id % 2 == 1, send_down(array, 1, range(start, n_rows, 2)), array)

    def block(array, place, cands):
        return array[:, place * cands : (place + 1) * cands]

    def shuffle(array, flip, cands):
        return jnp.concatenate([block(array, at ^ flip, cands) for at in range(half)], axis=1)

    def in_order(pieces, col_id):
        offsets = [at for step in range(half) for at in (step, step ^ half)]
        pieces = [pieces[offsets.index(at)] for at in range(n_cols)]
        bit = 1
        while bit < n_cols:
            flipped = (col_id & bit) != 0
            pieces = [
                jnp.where(flipped, pieces[at ^ bit], pieces[at]) for at in range(n_cols)
            ]
            bit *= 2
        return pieces

    def on_device(cross_kernel, factor_panels, block_inverses):
        row_id = lax.axis_index("rows")
        col_id = lax.axis_index("cols")
        width = block_inverses.shape[2]
        depth = block_inverses.shape[1]
        n_design, cands = cross_kernel.shape
        cuts = [n_design * at // 8 for at in EIGHTHS]
        parts = [slice(start, stop) for start, stop in zip(cuts, cuts[1:])]
        early = slice(0, cuts[-2])
        top = [0]
        beside = range(1, min(2, n_rows))
        below = range(2, n_rows)
        flat = factor_panels.reshape(2 * depth, n_design)

        lead = jnp.concatenate(
            [block_inverses[0], factor_panels[0, :, width : 2 * width], block_inverses[1]], axis=1
        )
        lead, rhs = lax.optimization_barrier((lead, cross_kernel[:width]))
        lead_other = swap(lead, half, top)
        rhs_others = [swap(rhs, step, top) for step in range(1, half)]
        mine = [flat[:, part] for part in parts]
        arrived = [swap(mine[0], half, below)]
        lead_other, mine_early, mine[1], mine[2] = lax.optimization_barrier(
            (lead_other, flat[:, early], mine[1], mine[2])
        )
        arrived.append(swap(mine[1], half, below))

        first, update, shuffled = call(
            functools.partial(first_kernel, [at ^ 1 for at in range(half)], width),
            [(2 * depth, half * cands)] + [(width, half * cands)] * 2,
            4 + len(rhs_others),
            6 * width * half * cands * (2 * depth + 2 * depth),
            lead,
            lead_other,
            rhs,
            *rhs_others,
            cross_kernel[width : 2 * width],
        )
        shuffled, arrived[0] = lax.optimization_barrier((shuffled, arrived[0]))
        got = swap(shuffled, 1, top)
        bit = 2
        while bit < half:
            update = update + got
            got = swap(shuffle(update, bit, cands), bit, top)
            bit *= 2
        first_beside = first
        late = mine_early
        if n_rows > 1:
            first_beside = send_down(first, 1, top)
            first_beside, late = lax.optimization_barrier((first_beside, late))
        late = swap(late, half, beside)
        first_half = broadcast_outer(first, row_id)
        got, first_half = lax.optimization_barrier((got, first_half))
        (second,) = call(
            functools.partial(second_kernel, 2 * width),
            [(2 * depth, half * cands)],
            4,
            6 * 2 * depth * width * half * cands,
            lead,
            lead_other,
            update,
            got,
        )
        second_half = broadcast_outer(second, row_id)
        second_half, second, arrived[1], late = lax.optimization_barrier(
            (second_half, second, arrived[1], late)
        )
        first_full = jnp.where(
            row_id == 1, first_beside, broadcast_inner(first_half, row_id, 2)
        )
        solved = [first_full, broadcast_inner(second_half, row_id)]
        arrived.append(swap(mine[2], half, range(1, n_rows)))

        pair = jnp.concatenate([first, second], axis=0)
        others = [block(pair, 0, cands)]
        others += [swap(block(pair, step, cands), step, top) for step in range(1, half)]
        pieces = [[], []]
        for got in others:
            for at in range(4):
                pieces[at // 2].append(got[at * depth : (at + 1) * depth])
        top_rows = jnp.concatenate(
            in_order(pieces[0], col_id) + in_order(pieces[1], col_id), axis=0
        )

        is_beside = (row_id == 1).astype(jnp.int32).reshape(1)
        fresh = []
        work = [
            (early, early_kernel, [mine_early, arrived[0], arrived[1], late]),
            (parts[2], late_kernel, [mine[2], arrived[2]]),
        ]
        for part, kernel, args in work:
            args = args + [*solved, cross_kernel[part]]
            count = part.stop - part.start
            own, send = call(
                kernel,
                [(count, cands), (count, (half - 1) * cands)],
                len(args),
                6 * count * 4 * depth * half * cands,
                *args,
                is_beside,
            )
            own, send, solved[0], solved[1] = lax.optimization_barrier((own, send, *solved))
            for step in range(1, half):
                own = own - swap(block(send, step - 1, cands), step, range(1, n_rows))
            fresh.append(own)
        fresh = jnp.concatenate(fresh, axis=0)
        head = jnp.where(row_id == 0, top_rows, fresh[: 2 * width])
        return jnp.concatenate([head, fresh[2 * width :]], axis=0)

    return on_device


def solution(mesh):
    in_specs = (P("rows", "cols"), P(None, "cols", "rows"), P(None, "cols", None))
    out_specs = P("rows", "cols")
    return jax.shard_map(
        make_on_device(mesh.shape["rows"], mesh.shape["cols"]),
        mesh=mesh,
        in_specs=in_specs,
        out_specs=out_specs,
        check_vma=False,
    )
```

```python
import functools
import jax
import jax.numpy as jnp
from jax import lax
from jax.experimental import pallas as pl
from jax.experimental.pallas import tpu as pltpu
from jax.sharding import PartitionSpec as P

AXES = ("rows", "cols")
LIMIT = 20 * 1024 * 1024


def split(array):
    high = array.astype(jnp.bfloat16)
    return high, (array - high.astype(jnp.float32)).astype(jnp.bfloat16)


def dot(left, right, left_dim):
    def one(a, b):
        return lax.dot_general(
            a, b, (((left_dim,), (0,)), ((), ())), preferred_element_type=jnp.float32
        )

    left_high, left_low = split(left)
    right_high, right_low = split(right)
    return one(left_high, right_high) + (one(left_high, right_low) + one(left_low, right_high))


def call(kernel, shapes, flops, operands):
    def spec(shape, place):
        return pl.BlockSpec(shape, lambda step: place)

    arrays, specs = [], []
    for operand in operands:
        array, shape, place = operand if isinstance(operand, tuple) else (operand, None, (0, 0))
        arrays.append(array)
        specs.append(spec(shape or array.shape, place))
    return pl.pallas_call(
        kernel,
        grid=(1,),
        out_shape=[jax.ShapeDtypeStruct(shape, jnp.float32) for shape in shapes],
        in_specs=specs,
        out_specs=[spec(shape, (0, 0)) for shape in shapes],
        compiler_params=pltpu.CompilerParams(vmem_limit_bytes=LIMIT),
        cost_estimate=pl.CostEstimate(flops=flops, bytes_accessed=0, transcendentals=0),
    )(*arrays)


def first_kernel(places, width, lead, lead_other, rhs, *refs):
    others, (low, solved, update, shuffled) = refs[:-4], refs[-4:]
    cands = rhs.shape[1]
    blocks = [rhs[...]] + [other[...] for other in others]
    blocks = jnp.concatenate(blocks, axis=1)
    inverse = jnp.concatenate([lead[:, :width], lead_other[:, :width]], axis=0)
    first = dot(inverse, blocks, 1)
    solved[...] = first
    corner = jnp.concatenate([lead[:, width : 2 * width], lead_other[:, width : 2 * width]], axis=0)
    total = dot(corner, first, 0)
    pieces = [total[:, at * cands : (at + 1) * cands] for at in range(len(places))]
    pieces[0] = pieces[0] - low[...]
    for at, place in enumerate(places):
        update[:, at * cands : (at + 1) * cands] = pieces[at]
        shuffled[:, at * cands : (at + 1) * cands] = pieces[place]


def second_kernel(inverse, inverse_other, update, got, solved):
    both = jnp.concatenate([inverse[...], inverse_other[...]], axis=0)
    solved[...] = dot(both, -(update[...] + got[...]), 1)


def chunk_kernel(mine, whole, late, piece, first, second, base, own, send):
    cands = base.shape[1]
    depth = first.shape[0] // 2
    other = piece[...] + (whole[...] + late[...])
    factors = jnp.concatenate([mine[...], other], axis=0)
    solved = jnp.concatenate(
        [first[:depth], second[:depth], first[depth:], second[depth:]], axis=0
    )
    partial = dot(factors, solved, 0)
    own[...] = base[...] - partial[:, :cands]
    send[...] = partial[:, cands:]


def make_on_device(n_rows, n_cols):
    half = n_cols // 2

    def swap(array, flip, rows):
        pairs = [
            (row * n_cols + col, row * n_cols + (col ^ flip))
            for row in rows
            for col in range(n_cols)
        ]
        return lax.ppermute(array, AXES, pairs)

    def send_down(array, offset, have):
        pairs = [
            (row * n_cols + col, (row + offset) * n_cols + col) for row in have for col in range(n_cols)
        ]
        return lax.ppermute(array, AXES, pairs)

    def spread(array, row_id, low, radix, have):
        digit = (row_id // low) % radix
        result = array
        for step in range(radix - 1, 0, -1):
            result = jnp.where(digit == step, send_down(array, step * low, have), result)
        return result, [row + step * low for row in have for step in range(radix)]

    def broadcast_outer(array, row_id):
        low = n_rows
        have = [0]
        while low > 2:
            radix = min(4, low // 2)
            low //= radix
            array, have = spread(array, row_id, low, radix, have)
        return array

    def broadcast_inner(array, row_id, start=0):
        return jnp.where(row_id % 2 == 1, send_down(array, 1, range(start, n_rows, 2)), array)

    def block(array, place, cands):
        return array[:, place * cands : (place + 1) * cands]

    def shuffle(array, flip, cands):
        return jnp.concatenate([block(array, at ^ flip, cands) for at in range(half)], axis=1)

    def in_order(pieces, col_id):
        offsets = [at for step in range(half) for at in (step, step ^ half)]
        pieces = [pieces[offsets.index(at)] for at in range(n_cols)]
        bit = 1
        while bit < n_cols:
            flipped = (col_id & bit) != 0
            pieces = [
                jnp.where(flipped, pieces[at ^ bit], pieces[at]) for at in range(n_cols)
            ]
            bit *= 2
        return pieces

    def on_device(cross_kernel, factor_panels, block_inverses):
        row_id = lax.axis_index("rows")
        col_id = lax.axis_index("cols")
        width = block_inverses.shape[2]
        depth = block_inverses.shape[1]
        n_design, cands = cross_kernel.shape
        count = n_design // 2
        top = [0]
        beside = range(1, min(2, n_rows))
        evens, odds = range(2, n_rows, 2), range(3, n_rows, 2)
        flat = factor_panels.reshape(2 * depth, n_design)

        lead = jnp.concatenate(
            [block_inverses[0], factor_panels[0, :, width : 2 * width], block_inverses[1]], axis=1
        )
        lead, rhs = lax.optimization_barrier((lead, cross_kernel[:width]))
        lead_other = swap(lead, half, top)
        rhs_others = [swap(rhs, step, top) for step in range(1, half)]
        whole = swap(flat, half, odds)
        arrived = [swap(flat[:, :count], half, evens)]
        lead_other, rest = lax.optimization_barrier((lead_other, flat[:, count:]))
        arrived.append(swap(rest, half, evens))

        first, update, shuffled = call(
            functools.partial(first_kernel, [at ^ 1 for at in range(half)], width),
            [(2 * depth, half * cands)] + [(width, half * cands)] * 2,
            6 * width * half * cands * (2 * depth + 2 * depth),
            [lead, lead_other, rhs, *rhs_others, cross_kernel[width : 2 * width]],
        )
        shuffled, first, arrived[0], whole = lax.optimization_barrier(
            (shuffled, first, arrived[0], whole)
        )
        got = swap(shuffled, 1, top)
        bit = 2
        while bit < half:
            update = update + got
            got = swap(shuffle(update, bit, cands), bit, top)
            bit *= 2
        first_beside = first
        late = flat
        if n_rows > 1:
            first_beside = send_down(first, 1, top)
            first_beside, late = lax.optimization_barrier((first_beside, late))
        late = swap(late, half, beside)
        first_half = broadcast_outer(first, row_id)
        got, first_half = lax.optimization_barrier((got, first_half))
        inverse = ((depth, width), (0, 2))
        (second,) = call(
            second_kernel,
            [(2 * depth, half * cands)],
            6 * 2 * depth * width * half * cands,
            [(lead, *inverse), (lead_other, *inverse), update, got],
        )
        second_half = broadcast_outer(second, row_id)
        second_half, second, late = lax.optimization_barrier((second_half, second, late))
        first_full = jnp.where(
            row_id == 1, first_beside, broadcast_inner(first_half, row_id, 2)
        )
        solved = [first_full, broadcast_inner(second_half, row_id)]

        pair = jnp.concatenate([first, second], axis=0)
        others = [block(pair, 0, cands)]
        others += [swap(block(pair, step, cands), step, top) for step in range(1, half)]
        pieces = [[], []]
        for got in others:
            for at in range(4):
                pieces[at // 2].append(got[at * depth : (at + 1) * depth])
        top_rows = jnp.concatenate(
            in_order(pieces[0], col_id) + in_order(pieces[1], col_id), axis=0
        )

        fresh = []
        for at, piece in enumerate(arrived):
            window = ((2 * depth, count), (0, at))
            own, send = call(
                chunk_kernel,
                [(count, cands), (count, (half - 1) * cands)],
                6 * count * 4 * depth * half * cands,
                [(flat, *window), (whole, *window), (late, *window)]
                + [piece, *solved, (cross_kernel, (count, cands), (at, 0))],
            )
            own, send, solved[0], solved[1] = lax.optimization_barrier((own, send, *solved))
            for step in range(1, half):
                own = own - swap(block(send, step - 1, cands), step, range(1, n_rows))
            fresh.append(own)
        fresh = jnp.concatenate(fresh, axis=0)
        head = jnp.where(row_id == 0, top_rows, fresh[: 2 * width])
        return jnp.concatenate([head, fresh[2 * width :]], axis=0)

    return on_device


def solution(mesh):
    in_specs = (P("rows", "cols"), P(None, "cols", "rows"), P(None, "cols", None))
    out_specs = P("rows", "cols")
    return jax.shard_map(
        make_on_device(mesh.shape["rows"], mesh.shape["cols"]),
        mesh=mesh,
        in_specs=in_specs,
        out_specs=out_specs,
        check_vma=False,
    )
```

```python
import functools
import jax
import jax.numpy as jnp
from jax import lax
from jax.experimental import pallas as pl
from jax.experimental.pallas import tpu as pltpu
from jax.sharding import PartitionSpec as P

AXES = ("rows", "cols")
FIRST = 3
LIMIT = 16 * 1024 * 1024


def split(array):
    high = array.astype(jnp.bfloat16)
    return high, (array - high.astype(jnp.float32)).astype(jnp.bfloat16)


def dot(left, right, left_dim):
    def one(a, b):
        return lax.dot_general(
            a, b, (((left_dim,), (0,)), ((), ())), preferred_element_type=jnp.float32
        )

    left_high, left_low = split(left)
    right_high, right_low = split(right)
    return one(left_high, right_high) + (one(left_high, right_low) + one(left_low, right_high))


def call(kernel, shapes, flops, operands):
    def spec(shape, place):
        return pl.BlockSpec(shape, lambda step: place)

    arrays, specs = [], []
    for operand in operands:
        array, shape, place = operand if isinstance(operand, tuple) else (operand, None, (0, 0))
        arrays.append(array)
        specs.append(spec(shape or array.shape, place))
    return pl.pallas_call(
        kernel,
        grid=(1,),
        out_shape=[jax.ShapeDtypeStruct(shape, jnp.float32) for shape in shapes],
        in_specs=specs,
        out_specs=[spec(shape, (0, 0)) for shape in shapes],
        compiler_params=pltpu.CompilerParams(vmem_limit_bytes=LIMIT),
        cost_estimate=pl.CostEstimate(flops=flops, bytes_accessed=0, transcendentals=0),
    )(*arrays)


def first_kernel(places, width, lead, lead_other, rhs, *refs):
    others, (low, solved, update, shuffled) = refs[:-4], refs[-4:]
    cands = rhs.shape[1]
    blocks = [rhs[...]] + [other[...] for other in others]
    blocks = jnp.concatenate(blocks, axis=1)
    inverse = jnp.concatenate([lead[:, :width], lead_other[:, :width]], axis=0)
    first = dot(inverse, blocks, 1)
    solved[...] = first
    corner = jnp.concatenate([lead[:, width : 2 * width], lead_other[:, width : 2 * width]], axis=0)
    total = dot(corner, first, 0)
    pieces = [total[:, at * cands : (at + 1) * cands] for at in range(len(places))]
    pieces[0] = pieces[0] - low[...]
    for at, place in enumerate(places):
        update[:, at * cands : (at + 1) * cands] = pieces[at]
        shuffled[:, at * cands : (at + 1) * cands] = pieces[place]


def second_kernel(inverse, inverse_other, update, got, solved):
    both = jnp.concatenate([inverse[...], inverse_other[...]], axis=0)
    solved[...] = dot(both, -(update[...] + got[...]), 1)


def chunk_kernel(*refs):
    tiles, (piece, first, second, own, send) = refs[:-5], refs[-5:]
    each = len(tiles) // 4
    mine, whole, late = [
        jnp.concatenate([ref[...] for ref in tiles[at * each : (at + 1) * each]], axis=1)
        for at in range(3)
    ]
    base = jnp.concatenate([ref[...] for ref in tiles[3 * each :]], axis=0)
    cands = base.shape[1]
    depth = first.shape[0] // 2
    factors = jnp.concatenate([mine, piece[...] + (whole + late)], axis=0)
    solved = jnp.concatenate(
        [first[:depth], second[:depth], first[depth:], second[depth:]], axis=0
    )
    partial = dot(factors, solved, 0)
    own[...] = base - partial[:, :cands]
    send[...] = partial[:, cands:]


def make_on_device(n_rows, n_cols):
    half = n_cols // 2

    def swap(array, flip, rows):
        pairs = [
            (row * n_cols + col, row * n_cols + (col ^ flip))
            for row in rows
            for col in range(n_cols)
        ]
        return lax.ppermute(array, AXES, pairs)

    def send_down(array, offset, have):
        pairs = [
            (row * n_cols + col, (row + offset) * n_cols + col) for row in have for col in range(n_cols)
        ]
        return lax.ppermute(array, AXES, pairs)

    def spread(array, row_id, low, radix, have):
        digit = (row_id // low) % radix
        result = array
        for step in range(radix - 1, 0, -1):
            result = jnp.where(digit == step, send_down(array, step * low, have), result)
        return result, [row + step * low for row in have for step in range(radix)]

    def broadcast_outer(array, row_id):
        low = n_rows
        have = [0]
        while low > 2:
            radix = min(4, low // 2)
            low //= radix
            array, have = spread(array, row_id, low, radix, have)
        return array

    def broadcast_inner(array, row_id, start=0):
        return jnp.where(row_id % 2 == 1, send_down(array, 1, range(start, n_rows, 2)), array)

    def block(array, place, cands):
        return array[:, place * cands : (place + 1) * cands]

    def shuffle(array, flip, cands):
        return jnp.concatenate([block(array, at ^ flip, cands) for at in range(half)], axis=1)

    def in_order(pieces, col_id):
        offsets = [at for step in range(half) for at in (step, step ^ half)]
        pieces = [pieces[offsets.index(at)] for at in range(n_cols)]
        bit = 1
        while bit < n_cols:
            flipped = (col_id & bit) != 0
            pieces = [
                jnp.where(flipped, pieces[at ^ bit], pieces[at]) for at in range(n_cols)
            ]
            bit *= 2
        return pieces

    def on_device(cross_kernel, factor_panels, block_inverses):
        row_id = lax.axis_index("rows")
        col_id = lax.axis_index("cols")
        width = block_inverses.shape[2]
        depth = block_inverses.shape[1]
        n_design, cands = cross_kernel.shape
        tile = n_design // 8
        cuts = [0, FIRST * tile, n_design]
        top = [0]
        beside = range(1, min(2, n_rows))
        evens, odds = range(2, n_rows, 2), range(3, n_rows, 2)
        flat = factor_panels.reshape(2 * depth, n_design)

        lead = jnp.concatenate(
            [block_inverses[0], factor_panels[0, :, width : 2 * width], block_inverses[1]], axis=1
        )
        lead, rhs = lax.optimization_barrier((lead, cross_kernel[:width]))
        lead_other = swap(lead, half, top)
        rhs_others = [swap(rhs, step, top) for step in range(1, half)]
        whole = swap(flat, half, odds)
        arrived = [swap(flat[:, : cuts[1]], half, evens)]
        lead_other, piece = lax.optimization_barrier((lead_other, flat[:, cuts[1] :]))
        arrived.append(swap(piece, half, evens))

        first, update, shuffled = call(
            functools.partial(first_kernel, [at ^ 1 for at in range(half)], width),
            [(2 * depth, half * cands)] + [(width, half * cands)] * 2,
            6 * width * half * cands * (2 * depth + 2 * depth),
            [lead, lead_other, rhs, *rhs_others, cross_kernel[width : 2 * width]],
        )
        shuffled, arrived[0], whole = lax.optimization_barrier((shuffled, arrived[0], whole))
        got = swap(shuffled, 1, top)
        bit = 2
        while bit < half:
            update = update + got
            got = swap(shuffle(update, bit, cands), bit, top)
            bit *= 2
        first_beside = first
        late = flat
        if n_rows > 1:
            first_beside = send_down(first, 1, top)
            first_beside, late = lax.optimization_barrier((first_beside, late))
        late = swap(late, half, beside)
        first_half = broadcast_outer(first, row_id)
        got, first_half = lax.optimization_barrier((got, first_half))
        inverse = ((depth, width), (0, 2))
        (second,) = call(
            second_kernel,
            [(2 * depth, half * cands)],
            6 * 2 * depth * width * half * cands,
            [(lead, *inverse), (lead_other, *inverse), update, got],
        )
        second_half = broadcast_outer(second, row_id)
        second_half, second, late = lax.optimization_barrier((second_half, second, late))
        first_full = jnp.where(
            row_id == 1, first_beside, broadcast_inner(first_half, row_id, 2)
        )
        solved = [first_full, broadcast_inner(second_half, row_id)]

        pair = jnp.concatenate([first, second], axis=0)
        others = [block(pair, 0, cands)]
        others += [swap(block(pair, step, cands), step, top) for step in range(1, half)]
        pieces = [[], []]
        for got in others:
            for at in range(4):
                pieces[at // 2].append(got[at * depth : (at + 1) * depth])
        top_rows = jnp.concatenate(
            in_order(pieces[0], col_id) + in_order(pieces[1], col_id), axis=0
        )

        fresh = []
        for start, stop, piece in zip(cuts, cuts[1:], arrived):
            count = stop - start
            tiles = range(start // tile, stop // tile)
            windows = [
                (array, (2 * depth, tile), (0, at)) for array in (flat, whole, late) for at in tiles
            ]
            windows += [(cross_kernel, (tile, cands), (at, 0)) for at in tiles]
            own, send = call(
                chunk_kernel,
                [(count, cands), (count, (half - 1) * cands)],
                6 * count * 4 * depth * half * cands,
                windows + [piece, *solved],
            )
            own, send, solved[0], solved[1] = lax.optimization_barrier((own, send, *solved))
            for step in range(1, half):
                own = own - swap(block(send, step - 1, cands), step, range(1, n_rows))
            fresh.append(own)
        fresh = jnp.concatenate(fresh, axis=0)
        head = jnp.where(row_id == 0, top_rows, fresh[: 2 * width])
        return jnp.concatenate([head, fresh[2 * width :]], axis=0)

    return on_device


def solution(mesh):
    in_specs = (P("rows", "cols"), P(None, "cols", "rows"), P(None, "cols", None))
    out_specs = P("rows", "cols")
    return jax.shard_map(
        make_on_device(mesh.shape["rows"], mesh.shape["cols"]),
        mesh=mesh,
        in_specs=in_specs,
        out_specs=out_specs,
        check_vma=False,
    )
```

```python
import functools
import jax
import jax.numpy as jnp
from jax import lax
from jax.experimental import pallas as pl
from jax.experimental.pallas import tpu as pltpu
from jax.sharding import PartitionSpec as P

AXES = ("rows", "cols")
LIMIT = 36 * 1024 * 1024


def split(array):
    high = array.astype(jnp.bfloat16)
    return high, (array - high.astype(jnp.float32)).astype(jnp.bfloat16)


def dot(left, right, left_dim):
    def one(a, b):
        return lax.dot_general(
            a, b, (((left_dim,), (0,)), ((), ())), preferred_element_type=jnp.float32
        )

    left_high, left_low = split(left)
    right_high, right_low = split(right)
    return one(left_high, right_high) + (one(left_high, right_low) + one(left_low, right_high))


def call(kernel, shapes, flops, operands, flag=None):
    def spec(shape, place):
        return pl.BlockSpec(shape, lambda step: place)

    arrays, specs = [], []
    for operand in operands:
        array, shape, place = operand if isinstance(operand, tuple) else (operand, None, (0, 0))
        arrays.append(array)
        specs.append(spec(shape or array.shape, place))
    if flag is not None:
        arrays.insert(0, flag.astype(jnp.int32).reshape(1))
        specs.insert(0, pl.BlockSpec(memory_space=pltpu.SMEM))
    return pl.pallas_call(
        kernel,
        grid=(1,),
        out_shape=[jax.ShapeDtypeStruct(shape, jnp.float32) for shape in shapes],
        in_specs=specs,
        out_specs=[spec(shape, (0, 0)) for shape in shapes],
        compiler_params=pltpu.CompilerParams(vmem_limit_bytes=LIMIT),
        cost_estimate=pl.CostEstimate(flops=flops, bytes_accessed=0, transcendentals=0),
    )(*arrays)


def first_kernel(places, width, lead, lead_other, rhs, *refs):
    others, (low, solved, update, shuffled) = refs[:-4], refs[-4:]
    cands = rhs.shape[1]
    blocks = [rhs[...]] + [other[...] for other in others]
    blocks = jnp.concatenate(blocks, axis=1)
    inverse = jnp.concatenate([lead[:, :width], lead_other[:, :width]], axis=0)
    first = dot(inverse, blocks, 1)
    solved[...] = first
    corner = jnp.concatenate([lead[:, width : 2 * width], lead_other[:, width : 2 * width]], axis=0)
    total = dot(corner, first, 0)
    pieces = [total[:, at * cands : (at + 1) * cands] for at in range(len(places))]
    pieces[0] = pieces[0] - low[...]
    for at, place in enumerate(places):
        update[:, at * cands : (at + 1) * cands] = pieces[at]
        shuffled[:, at * cands : (at + 1) * cands] = pieces[place]


def second_kernel(beside, inverse, inverse_other, update, got, first, solved, bundle):
    both = jnp.concatenate([inverse[...], inverse_other[...]], axis=0)
    second = dot(both, -(update[...] + got[...]), 1)
    solved[...] = second
    bundle[...] = jnp.where(beside[0] == 1, first[...], second)


def rows_kernel(odd, mine, whole, early, beside, tail, base, held, got, own, send):
    n_design, cands = base.shape
    depth = held.shape[0] // 2
    is_odd = odd[0] == 1
    first = jnp.where(is_odd, held[...], got[...])
    second = jnp.where(is_odd, got[...], held[...])
    solved = jnp.concatenate(
        [first[:depth], second[:depth], first[depth:], second[depth:]], axis=0
    )
    count = n_design // 2
    for at, parts in enumerate(([early, beside], [tail])):
        part = slice(at * count, (at + 1) * count)
        other = whole[:, part]
        for array in parts:
            other = other + array[...]
        factors = jnp.concatenate([mine[:, part], other], axis=0)
        partial = dot(factors, solved, 0)
        own[part] = base[part] - partial[:, :cands]
        send[part] = partial[:, cands:]


def make_on_device(n_rows, n_cols):
    half = n_cols // 2

    def swap(array, flip, rows):
        pairs = [
            (row * n_cols + col, row * n_cols + (col ^ flip))
            for row in rows
            for col in range(n_cols)
        ]
        return lax.ppermute(array, AXES, pairs)

    def send_down(array, offset, have):
        pairs = [
            (row * n_cols + col, (row + offset) * n_cols + col) for row in have for col in range(n_cols)
        ]
        return lax.ppermute(array, AXES, pairs)

    def spread(array, row_id, low, radix, have):
        digit = (row_id // low) % radix
        result = array
        for step in range(radix - 1, 0, -1):
            result = jnp.where(digit == step, send_down(array, step * low, have), result)
        return result, [row + step * low for row in have for step in range(radix)]

    def broadcast_outer(array, row_id):
        low = n_rows
        have = [0, 1]
        while low > 2:
            radix = min(4, low // 2)
            low //= radix
            array, have = spread(array, row_id, low, radix, have)
        return array

    def swap_cores(array):
        pairs = [
            (row * n_cols + col, (row ^ 1) * n_cols + col)
            for row in range(n_rows)
            for col in range(n_cols)
        ]
        return lax.ppermute(array, AXES, pairs)

    def block(array, place, cands):
        return array[:, place * cands : (place + 1) * cands]

    def shuffle(array, flip, cands):
        return jnp.concatenate([block(array, at ^ flip, cands) for at in range(half)], axis=1)

    def in_order(pieces, col_id):
        offsets = [at for step in range(half) for at in (step, step ^ half)]
        pieces = [pieces[offsets.index(at)] for at in range(n_cols)]
        bit = 1
        while bit < n_cols:
            flipped = (col_id & bit) != 0
            pieces = [
                jnp.where(flipped, pieces[at ^ bit], pieces[at]) for at in range(n_cols)
            ]
            bit *= 2
        return pieces

    def on_device(cross_kernel, factor_panels, block_inverses):
        row_id = lax.axis_index("rows")
        col_id = lax.axis_index("cols")
        width = block_inverses.shape[2]
        depth = block_inverses.shape[1]
        n_design, cands = cross_kernel.shape
        count = n_design // 2
        top = [0]
        beside = [1]
        evens, odds = range(2, n_rows, 2), range(3, n_rows, 2)
        flat = factor_panels.reshape(2 * depth, n_design)

        lead = jnp.concatenate(
            [block_inverses[0], factor_panels[0, :, width : 2 * width], block_inverses[1]], axis=1
        )
        lead, rhs = lax.optimization_barrier((lead, cross_kernel[:width]))
        lead_other = swap(lead, half, top)
        rhs_others = [swap(rhs, step, top) for step in range(1, half)]
        whole = swap(flat, half, odds)
        head = flat[:, :count]
        arrived = swap(head, half, evens)
        lead_other, head, tail = lax.optimization_barrier((lead_other, head, flat[:, count:]))

        first, update, shuffled = call(
            functools.partial(first_kernel, [at ^ 1 for at in range(half)], width),
            [(2 * depth, half * cands)] + [(width, half * cands)] * 2,
            6 * width * half * cands * (2 * depth + 2 * depth),
            [lead, lead_other, rhs, *rhs_others, cross_kernel[width : 2 * width]],
        )
        shuffled, arrived, whole = lax.optimization_barrier((shuffled, arrived, whole))
        got = swap(shuffled, 1, top)
        bit = 2
        while bit < half:
            update = update + got
            got = swap(shuffle(update, bit, cands), bit, top)
            bit *= 2
        first_beside = send_down(first, 1, top)
        inverse = ((depth, width), (0, 2))
        second, bundle = call(
            second_kernel,
            [(2 * depth, half * cands)] * 2,
            6 * 2 * depth * width * half * cands,
            [(lead, *inverse), (lead_other, *inverse), update, got, first_beside],
            row_id == 1,
        )
        first_beside, head = lax.optimization_barrier((first_beside, head))
        late = swap(head, half, beside)
        held = broadcast_outer(bundle, row_id)
        held, second, late = lax.optimization_barrier((held, second, late))
        tail = swap(tail, half, [*beside, *evens])
        solved = [held, swap_cores(held)]

        pair = jnp.concatenate([first, second], axis=0)
        others = [block(pair, 0, cands)]
        others += [swap(block(pair, step, cands), step, top) for step in range(1, half)]
        pieces = [[], []]
        for got in others:
            for at in range(4):
                pieces[at // 2].append(got[at * depth : (at + 1) * depth])
        top_rows = jnp.concatenate(
            in_order(pieces[0], col_id) + in_order(pieces[1], col_id), axis=0
        )

        fresh, send = call(
            rows_kernel,
            [(n_design, cands), (n_design, (half - 1) * cands)],
            6 * n_design * 4 * depth * half * cands,
            [flat, whole, arrived, late, tail, cross_kernel, *solved],
            row_id % 2 == 1,
        )
        for step in range(1, half):
            fresh = fresh - swap(block(send, step - 1, cands), step, range(1, n_rows))
        head = jnp.where(row_id == 0, top_rows, fresh[: 2 * width])
        return jnp.concatenate([head, fresh[2 * width :]], axis=0)

    return on_device


def solution(mesh):
    in_specs = (P("rows", "cols"), P(None, "cols", "rows"), P(None, "cols", None))
    out_specs = P("rows", "cols")
    return jax.shard_map(
        make_on_device(mesh.shape["rows"], mesh.shape["cols"]),
        mesh=mesh,
        in_specs=in_specs,
        out_specs=out_specs,
        check_vma=False,
    )
```

```python
import functools
import jax
import jax.numpy as jnp
from jax import lax
from jax.experimental import pallas as pl
from jax.experimental.pallas import tpu as pltpu
from jax.sharding import PartitionSpec as P

AXES = ("rows", "cols")
LIMIT = 12 * 1024 * 1024


def split(array):
    high = array.astype(jnp.bfloat16)
    return high, (array - high.astype(jnp.float32)).astype(jnp.bfloat16)


def dot(left, right, left_dim):
    def one(a, b):
        return lax.dot_general(
            a, b, (((left_dim,), (0,)), ((), ())), preferred_element_type=jnp.float32
        )

    left_high, left_low = split(left)
    right_high, right_low = split(right)
    return one(left_high, right_high) + (one(left_high, right_low) + one(left_low, right_high))


def call(kernel, shapes, flops, operands, flag=None):
    def spec(shape, place):
        return pl.BlockSpec(shape, lambda step: place)

    arrays, specs = [], []
    for operand in operands:
        array, shape, place = operand if isinstance(operand, tuple) else (operand, None, (0, 0))
        arrays.append(array)
        specs.append(spec(shape or array.shape, place))
    if flag is not None:
        arrays.insert(0, flag.astype(jnp.int32).reshape(1))
        specs.insert(0, pl.BlockSpec(memory_space=pltpu.SMEM))
    return pl.pallas_call(
        kernel,
        grid=(1,),
        out_shape=[jax.ShapeDtypeStruct(shape, jnp.float32) for shape in shapes],
        in_specs=specs,
        out_specs=[spec(shape, (0, 0)) for shape in shapes],
        compiler_params=pltpu.CompilerParams(vmem_limit_bytes=LIMIT),
        cost_estimate=pl.CostEstimate(flops=flops, bytes_accessed=0, transcendentals=0),
    )(*arrays)


def first_kernel(places, width, lead, lead_other, rhs, *refs):
    others, (low, solved, update, shuffled) = refs[:-4], refs[-4:]
    cands = rhs.shape[1]
    blocks = [rhs[...]] + [other[...] for other in others]
    blocks = jnp.concatenate(blocks, axis=1)
    inverse = jnp.concatenate([lead[:, :width], lead_other[:, :width]], axis=0)
    first = dot(inverse, blocks, 1)
    solved[...] = first
    corner = jnp.concatenate([lead[:, width : 2 * width], lead_other[:, width : 2 * width]], axis=0)
    total = dot(corner, first, 0)
    pieces = [total[:, at * cands : (at + 1) * cands] for at in range(len(places))]
    pieces[0] = pieces[0] - low[...]
    for at, place in enumerate(places):
        update[:, at * cands : (at + 1) * cands] = pieces[at]
        shuffled[:, at * cands : (at + 1) * cands] = pieces[place]


def second_kernel(beside, inverse, inverse_other, update, got, first, solved, bundle):
    both = jnp.concatenate([inverse[...], inverse_other[...]], axis=0)
    second = dot(both, -(update[...] + got[...]), 1)
    solved[...] = second
    bundle[...] = jnp.where(beside[0] == 1, first[...], second)


def rows_kernel(odd, mine, whole, early, beside, tail, base, held, got, own, send):
    n_design, cands = base.shape
    depth = held.shape[0] // 2
    is_odd = odd[0] == 1
    first = jnp.where(is_odd, held[...], got[...])
    second = jnp.where(is_odd, got[...], held[...])
    solved = jnp.concatenate(
        [first[:depth], second[:depth], first[depth:], second[depth:]], axis=0
    )
    count = n_design // 2
    for at, parts in enumerate(([early, beside], [tail])):
        part = slice(at * count, (at + 1) * count)
        other = whole[:, part]
        for array in parts:
            other = other + array[...]
        factors = jnp.concatenate([mine[:, part], other], axis=0)
        partial = dot(factors, solved, 0)
        own[part] = base[part] - partial[:, :cands]
        send[part] = partial[:, cands:]


def make_on_device(n_rows, n_cols):
    half = n_cols // 2

    def swap(array, flip, rows):
        pairs = [
            (row * n_cols + col, row * n_cols + (col ^ flip))
            for row in rows
            for col in range(n_cols)
        ]
        return lax.ppermute(array, AXES, pairs)

    def send_down(array, offset, have):
        pairs = [
            (row * n_cols + col, (row + offset) * n_cols + col) for row in have for col in range(n_cols)
        ]
        return lax.ppermute(array, AXES, pairs)

    def spread(array, row_id, low, radix, have):
        digit = (row_id // low) % radix
        result = array
        for step in range(1, radix):
            result = jnp.where(digit == step, send_down(array, step * low, have), result)
        return result, [row + step * low for row in have for step in range(radix)]

    def broadcast_outer(array, row_id):
        low = n_rows
        have = [0, 1]
        while low > 2:
            radix = min(4, low // 2)
            low //= radix
            array, have = spread(array, row_id, low, radix, have)
        return array

    def swap_cores(array):
        pairs = [
            (row * n_cols + col, (row ^ 1) * n_cols + col)
            for row in range(n_rows)
            for col in range(n_cols)
        ]
        return lax.ppermute(array, AXES, pairs)

    def block(array, place, cands):
        return array[:, place * cands : (place + 1) * cands]

    def shuffle(array, flip, cands):
        return jnp.concatenate([block(array, at ^ flip, cands) for at in range(half)], axis=1)

    def in_order(pieces, col_id):
        offsets = [at for step in range(half) for at in (step, step ^ half)]
        pieces = [pieces[offsets.index(at)] for at in range(n_cols)]
        bit = 1
        while bit < n_cols:
            flipped = (col_id & bit) != 0
            pieces = [
                jnp.where(flipped, pieces[at ^ bit], pieces[at]) for at in range(n_cols)
            ]
            bit *= 2
        return pieces

    def on_device(cross_kernel, factor_panels, block_inverses):
        row_id = lax.axis_index("rows")
        col_id = lax.axis_index("cols")
        width = block_inverses.shape[2]
        depth = block_inverses.shape[1]
        n_design, cands = cross_kernel.shape
        count = n_design // 2
        top = [0]
        beside = [1]
        evens, odds = range(2, n_rows, 2), range(3, n_rows, 2)
        flat = factor_panels.reshape(2 * depth, n_design)

        lead = jnp.concatenate(
            [block_inverses[0], factor_panels[0, :, width : 2 * width], block_inverses[1]], axis=1
        )
        lead, rhs = lax.optimization_barrier((lead, cross_kernel[:width]))
        lead_other = swap(lead, half, top)
        rhs_others = [swap(rhs, step, top) for step in range(1, half)]
        whole = swap(flat, half, odds)
        head = flat[:, :count]
        arrived = swap(head, half, evens)
        lead_other, head, tail = lax.optimization_barrier((lead_other, head, flat[:, count:]))

        first, update, shuffled = call(
            functools.partial(first_kernel, [at ^ 1 for at in range(half)], width),
            [(2 * depth, half * cands)] + [(width, half * cands)] * 2,
            6 * width * half * cands * (2 * depth + 2 * depth),
            [lead, lead_other, rhs, *rhs_others, cross_kernel[width : 2 * width]],
        )
        shuffled, arrived, whole = lax.optimization_barrier((shuffled, arrived, whole))
        got = swap(shuffled, 1, top)
        bit = 2
        while bit < half:
            update = update + got
            got = swap(shuffle(update, bit, cands), bit, top)
            bit *= 2
        first_beside = send_down(first, 1, top)
        inverse = ((depth, width), (0, 2))
        second, bundle = call(
            second_kernel,
            [(2 * depth, half * cands)] * 2,
            6 * 2 * depth * width * half * cands,
            [(lead, *inverse), (lead_other, *inverse), update, got, first_beside],
            row_id == 1,
        )
        first_beside, head = lax.optimization_barrier((first_beside, head))
        late = swap(head, half, beside)
        held = broadcast_outer(bundle, row_id)
        held, second, late = lax.optimization_barrier((held, second, late))
        tail = swap(tail, half, [*beside, *evens])
        solved = [held, swap_cores(held)]

        pair = jnp.concatenate([first, second], axis=0)
        others = [block(pair, 0, cands)]
        others += [swap(block(pair, step, cands), step, top) for step in range(1, half)]
        pieces = [[], []]
        for got in others:
            for at in range(4):
                pieces[at // 2].append(got[at * depth : (at + 1) * depth])
        top_rows = jnp.concatenate(
            in_order(pieces[0], col_id) + in_order(pieces[1], col_id), axis=0
        )

        fresh, send = call(
            rows_kernel,
            [(n_design, cands), (n_design, (half - 1) * cands)],
            6 * n_design * 4 * depth * half * cands,
            [flat, whole, arrived, late, tail, cross_kernel, *solved],
            row_id % 2 == 1,
        )
        for step in range(1, half):
            fresh = fresh - swap(block(send, step - 1, cands), step, range(1, n_rows))
        head = jnp.where(row_id == 0, top_rows, fresh[: 2 * width])
        return jnp.concatenate([head, fresh[2 * width :]], axis=0)

    return on_device


def solution(mesh):
    in_specs = (P("rows", "cols"), P(None, "cols", "rows"), P(None, "cols", None))
    out_specs = P("rows", "cols")
    return jax.shard_map(
        make_on_device(mesh.shape["rows"], mesh.shape["cols"]),
        mesh=mesh,
        in_specs=in_specs,
        out_specs=out_specs,
        check_vma=False,
    )
```

```python
import functools
import jax
import jax.numpy as jnp
from jax import lax
from jax.experimental import pallas as pl
from jax.experimental.pallas import tpu as pltpu
from jax.sharding import PartitionSpec as P

AXES = ("rows", "cols")
LIMIT = 12 * 1024 * 1024


def split(array):
    high = array.astype(jnp.bfloat16)
    return high, (array - high.astype(jnp.float32)).astype(jnp.bfloat16)


def dot(left, right, left_dim):
    def one(a, b):
        return lax.dot_general(
            a, b, (((left_dim,), (0,)), ((), ())), preferred_element_type=jnp.float32
        )

    left_high, left_low = split(left)
    right_high, right_low = split(right)
    return one(left_high, right_high) + (one(left_high, right_low) + one(left_low, right_high))


def call(kernel, shapes, flops, near, far=(), flag=None, scratch=()):
    flags = [] if flag is None else [flag.astype(jnp.int32).reshape(1)]
    spaces = [pltpu.SMEM] * len(flags) + [pltpu.VMEM] * len(near) + [pltpu.HBM] * len(far)
    return pl.pallas_call(
        kernel,
        out_shape=[jax.ShapeDtypeStruct(shape, jnp.float32) for shape in shapes],
        in_specs=[pl.BlockSpec(memory_space=space) for space in spaces],
        out_specs=[pl.BlockSpec(memory_space=pltpu.VMEM)] * len(shapes),
        scratch_shapes=[pltpu.VMEM(shape, jnp.float32) for shape in scratch]
        + [pltpu.SemaphoreType.DMA((6,))] * (1 if far else 0),
        compiler_params=pltpu.CompilerParams(vmem_limit_bytes=LIMIT),
        cost_estimate=pl.CostEstimate(flops=flops, bytes_accessed=0, transcendentals=0),
    )(*flags, *near, *far)


def first_kernel(places, width, row, lead, lead_other, rhs, *refs):
    others, (low, solved, shuffled) = refs[:-3], refs[-3:]
    cands = rhs.shape[1]

    @pl.when(row[0] == 0)
    def _():
        blocks = [rhs[...]] + [other[...] for other in others]
        blocks = jnp.concatenate(blocks, axis=1)
        inverse = jnp.concatenate([lead[:, :width], lead_other[:, :width]], axis=0)
        first = dot(inverse, blocks, 1)
        solved[...] = first
        middle = slice(width, 2 * width)
        corner = jnp.concatenate([lead[:, middle], lead_other[:, middle]], axis=0)
        total = dot(corner, first, 0)
        pieces = [total[:, at * cands : (at + 1) * cands] for at in range(len(places))]
        pieces[0] = pieces[0] - low[...]
        for at, place in enumerate(places):
            shuffled[:, at * cands : (at + 1) * cands] = pieces[place]


def second_kernel(places, row, lead, lead_other, sent, got, first, solved, bundle, *refs):
    sums, more, sems = refs
    width = sums.shape[0]
    cands = sums.shape[1] // len(places)

    @pl.when(row[0] == 0)
    def _():
        copies = [
            pltpu.make_async_copy(sent, sums, sems.at[0]),
            pltpu.make_async_copy(got, more, sems.at[1]),
        ]
        for copy in copies:
            copy.start()
        last = slice(2 * width, 3 * width)
        both = jnp.concatenate([lead[:, last], lead_other[:, last]], axis=0)
        for copy in copies:
            copy.wait()
        rest = [sums[:, place * cands : (place + 1) * cands] for place in places]
        second = dot(both, -(jnp.concatenate(rest, axis=1) + more[...]), 1)
        solved[...] = second
        bundle[...] = second

    @pl.when(row[0] == 1)
    def _():
        copy = pltpu.make_async_copy(first, bundle, sems.at[2])
        copy.start()
        copy.wait()


def rows_kernel(row, held, got, flat, whole, early, beside, tail, cross, own, send, *refs):
    mine, other, base, sems = refs
    n_design, cands = base.shape
    depth = held.shape[0] // 2
    count = n_design // 2
    parts = [slice(0, count), slice(count, n_design)]
    is_odd = row[0] % 2 == 1

    def fetch(at, source):
        return pltpu.make_async_copy(source, other.at[:, parts[at]], sems.at[at])

    @pl.when(row[0] > 0)
    def _():
        copies = []
        for at, part in enumerate(parts):
            copies += [
                pltpu.make_async_copy(flat.at[:, part], mine.at[:, part], sems.at[2 + at]),
                pltpu.make_async_copy(cross.at[part], base.at[part], sems.at[4 + at]),
            ]
        sources = [
            (row[0] == 1, [beside, tail]),
            ((row[0] > 1) & ~is_odd, [early, tail]),
            ((row[0] > 1) & is_odd, [whole.at[:, part] for part in parts]),
        ]
        for at in range(2):
            for chosen, pair in sources:
                pl.when(chosen)(lambda at=at, pair=pair: fetch(at, pair[at]).start())
            for copy in copies[2 * at : 2 * at + 2]:
                copy.start()
        first = jnp.where(is_odd, held[...], got[...])
        second = jnp.where(is_odd, got[...], held[...])
        solved = jnp.concatenate(
            [first[:depth], second[:depth], first[depth:], second[depth:]], axis=0
        )
        for at, part in enumerate(parts):
            fetch(at, tail).wait()
            for copy in copies[2 * at : 2 * at + 2]:
                copy.wait()
            factors = jnp.concatenate([mine[:, part], other[:, part]], axis=0)
            partial = dot(factors, solved, 0)
            own[part] = base[part] - partial[:, :cands]
            send[part] = partial[:, cands:]


def make_on_device(n_rows, n_cols):
    half = n_cols // 2

    def swap(array, flip, rows):
        pairs = [
            (row * n_cols + col, row * n_cols + (col ^ flip))
            for row in rows
            for col in range(n_cols)
        ]
        return lax.ppermute(array, AXES, pairs)

    def send_down(array, offset, have):
        pairs = [
            (row * n_cols + col, (row + offset) * n_cols + col) for row in have for col in range(n_cols)
        ]
        return lax.ppermute(array, AXES, pairs)

    def spread(array, row_id, low, radix, have):
        digit = (row_id // low) % radix
        result = array
        for step in range(1, radix):
            result = jnp.where(digit == step, send_down(array, step * low, have), result)
        return result, [row + step * low for row in have for step in range(radix)]

    def broadcast_outer(array, row_id):
        low = n_rows
        have = [0, 1]
        while low > 2:
            radix = min(4, low // 2)
            low //= radix
            array, have = spread(array, row_id, low, radix, have)
        return array

    def swap_cores(array):
        pairs = [
            (row * n_cols + col, (row ^ 1) * n_cols + col)
            for row in range(n_rows)
            for col in range(n_cols)
        ]
        return lax.ppermute(array, AXES, pairs)

    def block(array, place, cands):
        return array[:, place * cands : (place + 1) * cands]

    def shuffle(array, flip, cands):
        return jnp.concatenate([block(array, at ^ flip, cands) for at in range(half)], axis=1)

    def in_order(pieces, col_id):
        offsets = [at for step in range(half) for at in (step, step ^ half)]
        pieces = [pieces[offsets.index(at)] for at in range(n_cols)]
        bit = 1
        while bit < n_cols:
            flipped = (col_id & bit) != 0
            pieces = [
                jnp.where(flipped, pieces[at ^ bit], pieces[at]) for at in range(n_cols)
            ]
            bit *= 2
        return pieces

    def on_device(cross_kernel, factor_panels, block_inverses):
        row_id = lax.axis_index("rows")
        col_id = lax.axis_index("cols")
        width = block_inverses.shape[2]
        depth = block_inverses.shape[1]
        n_design, cands = cross_kernel.shape
        count = n_design // 2
        top = [0]
        beside = [1]
        evens, odds = range(2, n_rows, 2), range(3, n_rows, 2)
        flat = factor_panels.reshape(2 * depth, n_design)

        lead = jnp.concatenate(
            [block_inverses[0], factor_panels[0, :, width : 2 * width], block_inverses[1]], axis=1
        )
        lead, rhs = lax.optimization_barrier((lead, cross_kernel[:width]))
        lead_other = swap(lead, half, top)
        rhs_others = [swap(rhs, step, top) for step in range(1, half)]
        whole = swap(flat, half, odds)
        head = flat[:, :count]
        arrived = swap(head, half, evens)
        lead_other, head, tail = lax.optimization_barrier((lead_other, head, flat[:, count:]))

        places = [at ^ 1 for at in range(half)]
        first, shuffled = call(
            functools.partial(first_kernel, places, width),
            [(2 * depth, half * cands), (width, half * cands)],
            6 * width * half * cands * (2 * depth + 2 * depth),
            [lead, lead_other, rhs, *rhs_others, cross_kernel[width : 2 * width]],
            flag=row_id,
        )
        shuffled, arrived, whole = lax.optimization_barrier((shuffled, arrived, whole))
        sums = got = swap(shuffled, 1, top)
        bit = 2
        while bit < half:
            update = shuffle(shuffled, 1, cands) + sums
            got = swap(shuffle(update, bit, cands), bit, top)
            sums = sums + got
            bit *= 2
        first_beside = send_down(first, 1, top)
        second, bundle = call(
            functools.partial(second_kernel, places),
            [(2 * depth, half * cands)] * 2,
            6 * 2 * depth * width * half * cands,
            [lead, lead_other],
            [shuffled, sums, first_beside],
            row_id,
            [(width, half * cands)] * 2,
        )
        first_beside, head = lax.optimization_barrier((first_beside, head))
        late = swap(head, half, beside)
        held = broadcast_outer(bundle, row_id)
        held, second, late = lax.optimization_barrier((held, second, late))
        tail = swap(tail, half, [*beside, *evens])
        solved = [held, swap_cores(held)]

        pair = jnp.concatenate([first, second], axis=0)
        others = [block(pair, 0, cands)]
        others += [swap(block(pair, step, cands), step, top) for step in range(1, half)]
        pieces = [[], []]
        for got in others:
            for at in range(4):
                pieces[at // 2].append(got[at * depth : (at + 1) * depth])
        top_rows = jnp.concatenate(
            in_order(pieces[0], col_id) + in_order(pieces[1], col_id), axis=0
        )

        fresh, send = call(
            rows_kernel,
            [(n_design, cands), (n_design, (half - 1) * cands)],
            6 * n_design * 4 * depth * half * cands,
            solved,
            [flat, whole, arrived, late, tail, cross_kernel],
            row_id,
            [(2 * depth, n_design)] * 2 + [(n_design, cands)],
        )
        for step in range(1, half):
            fresh = fresh - swap(block(send, step - 1, cands), step, range(1, n_rows))
        return jnp.where(row_id == 0, top_rows, fresh)

    return on_device


def solution(mesh):
    in_specs = (P("rows", "cols"), P(None, "cols", "rows"), P(None, "cols", None))
    out_specs = P("rows", "cols")
    return jax.shard_map(
        make_on_device(mesh.shape["rows"], mesh.shape["cols"]),
        mesh=mesh,
        in_specs=in_specs,
        out_specs=out_specs,
        check_vma=False,
    )
```

```python
import functools
import jax
import jax.numpy as jnp
from jax import lax
from jax.experimental import pallas as pl
from jax.experimental.pallas import tpu as pltpu
from jax.sharding import PartitionSpec as P

AXES = ("rows", "cols")
LIMIT = 12 * 1024 * 1024


def split(array):
    high = array.astype(jnp.bfloat16)
    return high, (array - high.astype(jnp.float32)).astype(jnp.bfloat16)


def dot(left, right, left_dim):
    def one(a, b):
        return lax.dot_general(
            a, b, (((left_dim,), (0,)), ((), ())), preferred_element_type=jnp.float32
        )

    left_high, left_low = split(left)
    right_high, right_low = split(right)
    return one(left_high, right_high) + (one(left_high, right_low) + one(left_low, right_high))


def call(kernel, shapes, flops, near, far=(), flag=None, scratch=()):
    flags = [] if flag is None else [flag.astype(jnp.int32).reshape(1)]
    spaces = [pltpu.SMEM] * len(flags) + [pltpu.VMEM] * len(near) + [pltpu.HBM] * len(far)
    return pl.pallas_call(
        kernel,
        out_shape=[jax.ShapeDtypeStruct(shape, jnp.float32) for shape in shapes],
        in_specs=[pl.BlockSpec(memory_space=space) for space in spaces],
        out_specs=[pl.BlockSpec(memory_space=pltpu.VMEM)] * len(shapes),
        scratch_shapes=[pltpu.VMEM(shape, jnp.float32) for shape in scratch]
        + [pltpu.SemaphoreType.DMA((6,))] * (1 if far else 0),
        compiler_params=pltpu.CompilerParams(vmem_limit_bytes=LIMIT),
        cost_estimate=pl.CostEstimate(flops=flops, bytes_accessed=0, transcendentals=0),
    )(*flags, *near, *far)


def first_kernel(places, width, row, lead, lead_other, rhs, *refs):
    others, (solved, shuffled, *held, sems) = refs[: len(places) - 1], refs[len(places) - 1 :]
    cands = rhs.shape[1]

    @pl.when(row[0] == 0)
    def _():
        copies = [
            pltpu.make_async_copy(other.at[:width], place, sems.at[at])
            for at, (other, place) in enumerate(zip(others, held))
        ]
        for copy in copies:
            copy.start()
        for copy in copies:
            copy.wait()
        blocks = jnp.concatenate([rhs[:width]] + [place[...] for place in held], axis=1)
        inverse = jnp.concatenate([lead[:, :width], lead_other[:, :width]], axis=0)
        first = dot(inverse, blocks, 1)
        solved[...] = first
        middle = slice(width, 2 * width)
        corner = jnp.concatenate([lead[:, middle], lead_other[:, middle]], axis=0)
        total = dot(corner, first, 0)
        pieces = [total[:, at * cands : (at + 1) * cands] for at in range(len(places))]
        pieces[0] = pieces[0] - rhs[middle]
        for at, place in enumerate(places):
            shuffled[:, at * cands : (at + 1) * cands] = pieces[place]


def second_kernel(places, row, inverse, inverse_other, sent, got, first, solved, bundle, *refs):
    sums, more, sems = refs
    width = sums.shape[0]
    cands = sums.shape[1] // len(places)

    @pl.when(row[0] == 0)
    def _():
        copies = [
            pltpu.make_async_copy(sent, sums, sems.at[0]),
            pltpu.make_async_copy(got, more, sems.at[1]),
        ]
        for copy in copies:
            copy.start()
        both = jnp.concatenate([inverse[...], inverse_other[...]], axis=0)
        for copy in copies:
            copy.wait()
        rest = [sums[:, place * cands : (place + 1) * cands] for place in places]
        second = dot(both, -(jnp.concatenate(rest, axis=1) + more[...]), 1)
        solved[...] = second
        bundle[...] = second

    @pl.when(row[0] == 1)
    def _():
        copy = pltpu.make_async_copy(first, bundle, sems.at[2])
        copy.start()
        copy.wait()


def rows_kernel(row, held, got, flat, whole, early, beside, tail, cross, own, send, *refs):
    mine, other, base, sems = refs
    n_design, cands = base.shape
    depth = held.shape[0] // 2
    count = early.shape[1]
    parts = [slice(0, count), slice(count, n_design)]
    is_odd = row[0] % 2 == 1

    def fetch(at, source):
        return pltpu.make_async_copy(source, other.at[:, parts[at]], sems.at[at])

    @pl.when(row[0] > 0)
    def _():
        copies = []
        for at, part in enumerate(parts):
            copies += [
                pltpu.make_async_copy(flat.at[:, part], mine.at[:, part], sems.at[2 + at]),
                pltpu.make_async_copy(cross.at[part], base.at[part], sems.at[4 + at]),
            ]
        sources = [
            (row[0] == 1, [beside.at[:, parts[0]], tail]),
            ((row[0] > 1) & ~is_odd, [early, tail]),
            ((row[0] > 1) & is_odd, [whole.at[:, part] for part in parts]),
        ]
        for at in range(2):
            for chosen, pair in sources:
                pl.when(chosen)(lambda at=at, pair=pair: fetch(at, pair[at]).start())
            for copy in copies[2 * at : 2 * at + 2]:
                copy.start()
        first = jnp.where(is_odd, held[...], got[...])
        second = jnp.where(is_odd, got[...], held[...])
        solved = jnp.concatenate(
            [first[:depth], second[:depth], first[depth:], second[depth:]], axis=0
        )
        for at, part in enumerate(parts):
            fetch(at, whole.at[:, part]).wait()
            for copy in copies[2 * at : 2 * at + 2]:
                copy.wait()
            factors = jnp.concatenate([mine[:, part], other[:, part]], axis=0)
            partial = dot(factors, solved, 0)
            own[part] = base[part] - partial[:, :cands]
            send[part] = partial[:, cands:]


def make_on_device(n_rows, n_cols):
    half = n_cols // 2

    def swap(array, flip, rows):
        pairs = [
            (row * n_cols + col, row * n_cols + (col ^ flip))
            for row in rows
            for col in range(n_cols)
        ]
        return lax.ppermute(array, AXES, pairs)

    def send_down(array, offset, have):
        pairs = [
            (row * n_cols + col, (row + offset) * n_cols + col) for row in have for col in range(n_cols)
        ]
        return lax.ppermute(array, AXES, pairs)

    def spread(array, row_id, low, radix, have):
        digit = (row_id // low) % radix
        result = array
        for step in range(1, radix):
            result = jnp.where(digit == step, send_down(array, step * low, have), result)
        return result, [row + step * low for row in have for step in range(radix)]

    def broadcast_outer(array, row_id):
        low = n_rows
        have = [0, 1]
        while low > 2:
            radix = min(4, low // 2)
            low //= radix
            array, have = spread(array, row_id, low, radix, have)
        return array

    def swap_cores(array):
        pairs = [
            (row * n_cols + col, (row ^ 1) * n_cols + col)
            for row in range(n_rows)
            for col in range(n_cols)
        ]
        return lax.ppermute(array, AXES, pairs)

    def block(array, place, cands):
        return array[:, place * cands : (place + 1) * cands]

    def shuffle(array, flip, cands):
        return jnp.concatenate([block(array, at ^ flip, cands) for at in range(half)], axis=1)

    def in_order(pieces, col_id):
        offsets = [at for step in range(half) for at in (step, step ^ half)]
        pieces = [pieces[offsets.index(at)] for at in range(n_cols)]
        bit = 1
        while bit < n_cols:
            flipped = (col_id & bit) != 0
            pieces = [
                jnp.where(flipped, pieces[at ^ bit], pieces[at]) for at in range(n_cols)
            ]
            bit *= 2
        return pieces

    def on_device(cross_kernel, factor_panels, block_inverses):
        row_id = lax.axis_index("rows")
        col_id = lax.axis_index("cols")
        width = block_inverses.shape[2]
        depth = block_inverses.shape[1]
        n_design, cands = cross_kernel.shape
        count = n_design * 3 // 8
        top = [0]
        beside = [1]
        evens, odds = range(2, n_rows, 2), range(3, n_rows, 2)
        flat = factor_panels.reshape(2 * depth, n_design)

        lead = jnp.concatenate(
            [block_inverses[0], factor_panels[0, :, width : 2 * width]], axis=1
        )
        lead, rhs = lax.optimization_barrier((lead, cross_kernel))
        lead_other = swap(lead, half, top)
        rhs_others = [swap(rhs, step, top) for step in range(1, half)]
        whole = swap(flat, half, odds)
        arrived = swap(flat[:, :count], half, evens)
        lead_other, head, tail, inverse = lax.optimization_barrier(
            (lead_other, flat[:, : n_design // 2], flat[:, count:], block_inverses[1])
        )

        places = [at ^ 1 for at in range(half)]
        first, shuffled = call(
            functools.partial(first_kernel, places, width),
            [(2 * depth, half * cands), (width, half * cands)],
            6 * width * half * cands * (2 * depth + 2 * depth),
            [lead, lead_other, rhs],
            rhs_others,
            row_id,
            [(width, cands)] * len(rhs_others),
        )
        first, inverse = lax.optimization_barrier((first, inverse))
        inverse_other = swap(inverse, half, top)
        shuffled, arrived, whole = lax.optimization_barrier((shuffled, arrived, whole))
        sums = got = swap(shuffled, 1, top)
        bit = 2
        while bit < half:
            update = shuffle(shuffled, 1, cands) + sums
            got = swap(shuffle(update, bit, cands), bit, top)
            sums = sums + got
            bit *= 2
        first_beside = send_down(first, 1, top)
        second, bundle = call(
            functools.partial(second_kernel, places),
            [(2 * depth, half * cands)] * 2,
            6 * 2 * depth * width * half * cands,
            [inverse, inverse_other],
            [shuffled, sums, first_beside],
            row_id,
            [(width, half * cands)] * 2,
        )
        first_beside, head = lax.optimization_barrier((first_beside, head))
        late = swap(head, half, beside)
        held = broadcast_outer(bundle, row_id)
        held, second, late = lax.optimization_barrier((held, second, late))
        tail = swap(tail, half, [*beside, *evens])
        solved = [held, swap_cores(held)]

        pair = jnp.concatenate([first, second], axis=0)
        others = [block(pair, 0, cands)]
        others += [swap(block(pair, step, cands), step, top) for step in range(1, half)]
        pieces = [[], []]
        for got in others:
            for at in range(4):
                pieces[at // 2].append(got[at * depth : (at + 1) * depth])
        top_rows = jnp.concatenate(
            in_order(pieces[0], col_id) + in_order(pieces[1], col_id), axis=0
        )

        fresh, send = call(
            rows_kernel,
            [(n_design, cands), (n_design, (half - 1) * cands)],
            6 * n_design * 4 * depth * half * cands,
            solved,
            [flat, whole, arrived, late, tail, cross_kernel],
            row_id,
            [(2 * depth, n_design)] * 2 + [(n_design, cands)],
        )
        for step in range(1, half):
            fresh = fresh - swap(block(send, step - 1, cands), step, range(1, n_rows))
        return jnp.where(row_id == 0, top_rows, fresh)

    return on_device


def solution(mesh):
    in_specs = (P("rows", "cols"), P(None, "cols", "rows"), P(None, "cols", None))
    out_specs = P("rows", "cols")
    return jax.shard_map(
        make_on_device(mesh.shape["rows"], mesh.shape["cols"]),
        mesh=mesh,
        in_specs=in_specs,
        out_specs=out_specs,
        check_vma=False,
    )
```

```python
import functools
import jax
import jax.numpy as jnp
from jax import lax
from jax.experimental import pallas as pl
from jax.experimental.pallas import tpu as pltpu
from jax.sharding import PartitionSpec as P

AXES = ("rows", "cols")
LIMIT = 12 * 1024 * 1024


def split(array):
    high = array.astype(jnp.bfloat16)
    return high, (array - high.astype(jnp.float32)).astype(jnp.bfloat16)


def dot(left, right, left_dim):
    def one(a, b):
        return lax.dot_general(
            a, b, (((left_dim,), (0,)), ((), ())), preferred_element_type=jnp.float32
        )

    left_high, left_low = split(left)
    right_high, right_low = right if isinstance(right, tuple) else split(right)
    return one(left_high, right_high) + (one(left_high, right_low) + one(left_low, right_high))


def call(kernel, shapes, flops, near, far=(), flag=None, scratch=()):
    flags = [] if flag is None else [flag.astype(jnp.int32).reshape(1)]
    spaces = [pltpu.SMEM] * len(flags) + [pltpu.VMEM] * len(near) + [pltpu.HBM] * len(far)
    return pl.pallas_call(
        kernel,
        out_shape=[jax.ShapeDtypeStruct(shape, jnp.float32) for shape in shapes],
        in_specs=[pl.BlockSpec(memory_space=space) for space in spaces],
        out_specs=[pl.BlockSpec(memory_space=pltpu.VMEM)] * len(shapes),
        scratch_shapes=[pltpu.VMEM(shape, jnp.float32) for shape in scratch]
        + [pltpu.SemaphoreType.DMA((6,))] * (1 if far else 0),
        compiler_params=pltpu.CompilerParams(vmem_limit_bytes=LIMIT),
        cost_estimate=pl.CostEstimate(flops=flops, bytes_accessed=0, transcendentals=0),
    )(*flags, *near, *far)


def first_kernel(places, width, row, lead, rhs, far_lead, *refs):
    others, (solved, shuffled, lead_other, *held, sems) = (
        refs[: len(places) - 1],
        refs[len(places) - 1 :],
    )
    cands = rhs.shape[1]

    @pl.when(row[0] == 0)
    def _():
        copies = [
            pltpu.make_async_copy(other.at[:width], place, sems.at[at])
            for at, (other, place) in enumerate(zip(others, held))
        ]
        copies.append(
            pltpu.make_async_copy(
                far_lead.at[:, : 2 * width], lead_other, sems.at[len(copies)]
            )
        )
        for copy in copies:
            copy.start()
        for copy in copies:
            copy.wait()
        blocks = jnp.concatenate([rhs[:width]] + [place[...] for place in held], axis=1)
        inverse = jnp.concatenate([lead[:, :width], lead_other[:, :width]], axis=0)
        first = dot(inverse, blocks, 1)
        solved[...] = first
        middle = slice(width, 2 * width)
        corner = jnp.concatenate([lead[:, middle], lead_other[:, middle]], axis=0)
        total = dot(corner, first, 0)
        pieces = [total[:, at * cands : (at + 1) * cands] for at in range(len(places))]
        pieces[0] = pieces[0] - rhs[middle]
        for at, place in enumerate(places):
            shuffled[:, at * cands : (at + 1) * cands] = pieces[place]


def second_kernel(places, row, lead, far_lead, sent, got, first, solved, bundle, *refs):
    inverse_other, sums, more, sems = refs
    width = sums.shape[0]
    cands = sums.shape[1] // len(places)

    last = slice(2 * width, 3 * width)

    @pl.when(row[0] == 0)
    def _():
        copies = [
            pltpu.make_async_copy(sent, sums, sems.at[0]),
            pltpu.make_async_copy(got, more, sems.at[1]),
            pltpu.make_async_copy(far_lead.at[:, last], inverse_other, sems.at[2]),
        ]
        for copy in copies:
            copy.start()
        for copy in copies:
            copy.wait()
        both = jnp.concatenate([lead[:, last], inverse_other[...]], axis=0)
        rest = [sums[:, place * cands : (place + 1) * cands] for place in places]
        second = dot(both, -(jnp.concatenate(rest, axis=1) + more[...]), 1)
        solved[...] = second
        bundle[...] = second

    @pl.when(row[0] == 1)
    def _():
        copy = pltpu.make_async_copy(first, bundle, sems.at[3])
        copy.start()
        copy.wait()


def rows_kernel(row, held, got, flat, whole, early, beside, tail, cross, own, send, *refs):
    mine, other, base, sems = refs
    n_design, cands = base.shape
    depth = held.shape[0] // 2
    count = early.shape[1]
    parts = [slice(0, count), slice(count, n_design)]
    is_odd = row[0] % 2 == 1

    def fetch(at, source):
        return pltpu.make_async_copy(source, other.at[:, parts[at]], sems.at[at])

    @pl.when(row[0] > 0)
    def _():
        copies = []
        for at, part in enumerate(parts):
            copies += [
                pltpu.make_async_copy(flat.at[:, part], mine.at[:, part], sems.at[2 + at]),
                pltpu.make_async_copy(cross.at[part], base.at[part], sems.at[4 + at]),
            ]
        sources = [
            (row[0] == 1, [beside.at[:, parts[0]], tail]),
            ((row[0] > 1) & ~is_odd, [early, tail]),
            ((row[0] > 1) & is_odd, [whole.at[:, part] for part in parts]),
        ]
        for at in range(2):
            for chosen, pair in sources:
                pl.when(chosen)(lambda at=at, pair=pair: fetch(at, pair[at]).start())
            for copy in copies[2 * at : 2 * at + 2]:
                copy.start()
        has_first = (row[0] == 1) | ((row[0] > 1) & ~is_odd)
        first = jnp.where(has_first, held[...], got[...])
        second = jnp.where(has_first, got[...], held[...])
        solved = jnp.concatenate(
            [first[:depth], second[:depth], first[depth:], second[depth:]], axis=0
        )
        solved = split(solved)
        for at, part in enumerate(parts):
            fetch(at, whole.at[:, part]).wait()
            for copy in copies[2 * at : 2 * at + 2]:
                copy.wait()
            factors = jnp.concatenate([mine[:, part], other[:, part]], axis=0)
            partial = dot(factors, solved, 0)
            own[part] = base[part] - partial[:, :cands]
            send[part] = partial[:, cands:]


def top_kernel(offsets, col, pair, *refs):
    others, out = refs[:-1], refs[-1]
    cands = out.shape[1]
    depth = pair.shape[0] // 4
    n_cols = len(offsets)
    sources = [pair[:, :cands]] + [other[...] for other in others]
    for panel in range(2):
        pieces = []
        for source in sources:
            for at in (2 * panel, 2 * panel + 1):
                pieces.append(source[at * depth : (at + 1) * depth])
        pieces = [pieces[offsets.index(at)] for at in range(n_cols)]
        bit = 1
        while bit < n_cols:
            flipped = (col[0] & bit) != 0
            pieces = [jnp.where(flipped, pieces[at ^ bit], pieces[at]) for at in range(n_cols)]
            bit *= 2
        for at, piece in enumerate(pieces):
            place = (panel * n_cols + at) * depth
            out[place : place + depth] = piece


def make_on_device(n_rows, n_cols):
    half = n_cols // 2

    def swap(array, flip, rows):
        pairs = [
            (row * n_cols + col, row * n_cols + (col ^ flip))
            for row in rows
            for col in range(n_cols)
        ]
        return lax.ppermute(array, AXES, pairs)

    def send_down(array, offset, have):
        pairs = [
            (row * n_cols + col, target(row, offset) * n_cols + col)
            for row in have
            for col in range(n_cols)
        ]
        return lax.ppermute(array, AXES, pairs)

    def target(row, offset):
        return (row + offset) ^ (1 if row < 2 and offset > 1 else 0)

    def spread(array, row_id, low, radix, have):
        digit = (row_id // low) % radix
        result = array
        for step in (2, 1, 3) if radix == 4 else range(1, radix):
            result = jnp.where(digit == step, send_down(array, step * low, have), result)
        return result, [target(row, step * low) for row in have for step in range(radix)]

    def broadcast_outer(array, row_id):
        low = n_rows
        have = [0, 1]
        while low > 2:
            radix = min(4, low // 2)
            low //= radix
            array, have = spread(array, row_id, low, radix, have)
        return array

    def swap_cores(array):
        pairs = [
            (row * n_cols + col, (row ^ 1) * n_cols + col)
            for row in range(n_rows)
            for col in range(n_cols)
        ]
        return lax.ppermute(array, AXES, pairs)

    def block(array, place, cands):
        return array[:, place * cands : (place + 1) * cands]

    def shuffle(array, flip, cands):
        return jnp.concatenate([block(array, at ^ flip, cands) for at in range(half)], axis=1)

    def on_device(cross_kernel, factor_panels, block_inverses):
        row_id = lax.axis_index("rows")
        col_id = lax.axis_index("cols")
        width = block_inverses.shape[2]
        depth = block_inverses.shape[1]
        n_design, cands = cross_kernel.shape
        count = n_design * 3 // 8
        top = [0]
        beside = [1]
        evens, odds = range(2, n_rows, 2), range(3, n_rows, 2)
        flat = factor_panels.reshape(2 * depth, n_design)

        lead = jnp.concatenate(
            [block_inverses[0], factor_panels[0, :, width : 2 * width], block_inverses[1]], axis=1
        )
        lead, rhs = lax.optimization_barrier((lead, cross_kernel))
        lead_other = swap(lead, half, top)
        rhs_others = [swap(rhs, step, top) for step in range(1, half)]
        whole = swap(flat, half, odds)
        arrived = swap(flat[:, :count], half, evens)
        lead_other, head, tail = lax.optimization_barrier(
            (lead_other, flat[:, : n_design // 2], flat[:, count:])
        )

        places = [at ^ 1 for at in range(half)]
        first, shuffled = call(
            functools.partial(first_kernel, places, width),
            [(2 * depth, half * cands), (width, half * cands)],
            6 * width * half * cands * (2 * depth + 2 * depth),
            [lead, rhs],
            [lead_other, *rhs_others],
            row_id,
            [(depth, 2 * width)] + [(width, cands)] * len(rhs_others),
        )
        shuffled, arrived, whole = lax.optimization_barrier((shuffled, arrived, whole))
        sums = got = swap(shuffled, 1, top)
        bit = 2
        while bit < half:
            update = shuffle(shuffled, 1, cands) + sums
            got = swap(shuffle(update, bit, cands), bit, top)
            sums = sums + got
            bit *= 2
        first_beside = send_down(first, 1, top)
        second, bundle = call(
            functools.partial(second_kernel, places),
            [(2 * depth, half * cands)] * 2,
            6 * 2 * depth * width * half * cands,
            [lead],
            [lead_other, shuffled, sums, first_beside],
            row_id,
            [(depth, width)] + [(width, half * cands)] * 2,
        )
        first_beside, head = lax.optimization_barrier((first_beside, head))
        late = swap(head, half, beside)
        held = broadcast_outer(bundle, row_id)
        held, second, late = lax.optimization_barrier((held, second, late))
        tail = swap(tail, half, [*beside, *evens])
        solved = [held, swap_cores(held)]

        pair = jnp.concatenate([first, second], axis=0)
        others = [swap(block(pair, step, cands), step, top) for step in range(1, half)]
        offsets = [at for step in range(half) for at in (step, step ^ half)]
        (top_rows,) = call(
            functools.partial(top_kernel, offsets),
            [(2 * width, cands)],
            0,
            [pair, *others],
            flag=col_id,
        )

        fresh, send = call(
            rows_kernel,
            [(n_design, cands), (n_design, (half - 1) * cands)],
            6 * n_design * 4 * depth * half * cands,
            solved,
            [flat, whole, arrived, late, tail, cross_kernel],
            row_id,
            [(2 * depth, n_design)] * 2 + [(n_design, cands)],
        )
        for step in range(1, half):
            fresh = fresh - swap(block(send, step - 1, cands), step, range(1, n_rows))
        return jnp.where(row_id == 0, top_rows, fresh)

    return on_device


def solution(mesh):
    in_specs = (P("rows", "cols"), P(None, "cols", "rows"), P(None, "cols", None))
    out_specs = P("rows", "cols")
    return jax.shard_map(
        make_on_device(mesh.shape["rows"], mesh.shape["cols"]),
        mesh=mesh,
        in_specs=in_specs,
        out_specs=out_specs,
        check_vma=False,
    )
```

```python
import functools
import jax
import jax.numpy as jnp
from jax import lax
from jax.experimental import pallas as pl
from jax.experimental.pallas import tpu as pltpu
from jax.sharding import PartitionSpec as P

AXES = ("rows", "cols")
LIMIT = 12 * 1024 * 1024


def split(array):
    high = array.astype(jnp.bfloat16)
    return high, (array - high.astype(jnp.float32)).astype(jnp.bfloat16)


def dot(left, right, left_dim):
    def one(a, b):
        return lax.dot_general(
            a, b, (((left_dim,), (0,)), ((), ())), preferred_element_type=jnp.float32
        )

    left_high, left_low = split(left)
    right_high, right_low = right if isinstance(right, tuple) else split(right)
    return one(left_high, right_high) + (one(left_high, right_low) + one(left_low, right_high))


def call(kernel, shapes, flops, near, far=(), flag=None, scratch=()):
    flags = [] if flag is None else [flag.astype(jnp.int32).reshape(1)]
    spaces = [pltpu.SMEM] * len(flags) + [pltpu.VMEM] * len(near) + [pltpu.HBM] * len(far)
    return pl.pallas_call(
        kernel,
        out_shape=[jax.ShapeDtypeStruct(shape, jnp.float32) for shape in shapes],
        in_specs=[pl.BlockSpec(memory_space=space) for space in spaces],
        out_specs=[pl.BlockSpec(memory_space=pltpu.VMEM)] * len(shapes),
        scratch_shapes=[pltpu.VMEM(shape, jnp.float32) for shape in scratch]
        + [pltpu.SemaphoreType.DMA((12,))] * (1 if far else 0),
        compiler_params=pltpu.CompilerParams(vmem_limit_bytes=LIMIT),
        cost_estimate=pl.CostEstimate(flops=flops, bytes_accessed=0, transcendentals=0),
    )(*flags, *near, *far)


def first_kernel(places, width, row, lead, rhs, far_lead, *refs):
    others, (solved, shuffled, lead_other, *held, sems) = (
        refs[: len(places) - 1],
        refs[len(places) - 1 :],
    )
    cands = rhs.shape[1]

    @pl.when(row[0] == 0)
    def _():
        copies = [
            pltpu.make_async_copy(other.at[:width], place, sems.at[at])
            for at, (other, place) in enumerate(zip(others, held))
        ]
        copies.append(
            pltpu.make_async_copy(
                far_lead.at[:, : 2 * width], lead_other, sems.at[len(copies)]
            )
        )
        for copy in copies:
            copy.start()
        for copy in copies:
            copy.wait()
        blocks = jnp.concatenate([rhs[:width]] + [place[...] for place in held], axis=1)
        inverse = jnp.concatenate([lead[:, :width], lead_other[:, :width]], axis=0)
        first = dot(inverse, blocks, 1)
        solved[...] = first
        middle = slice(width, 2 * width)
        corner = jnp.concatenate([lead[:, middle], lead_other[:, middle]], axis=0)
        total = dot(corner, first, 0)
        pieces = [total[:, at * cands : (at + 1) * cands] for at in range(len(places))]
        pieces[0] = pieces[0] - rhs[middle]
        for at, place in enumerate(places):
            shuffled[:, at * cands : (at + 1) * cands] = pieces[place]


def second_kernel(places, row, lead, far_lead, sent, got, first, bundle, *refs):
    inverse_other, sums, more, sems = refs
    width = sums.shape[0]
    cands = sums.shape[1] // len(places)

    last = slice(2 * width, 3 * width)

    @pl.when(row[0] == 0)
    def _():
        copies = [
            pltpu.make_async_copy(sent, sums, sems.at[0]),
            pltpu.make_async_copy(got, more, sems.at[1]),
            pltpu.make_async_copy(far_lead.at[:, last], inverse_other, sems.at[2]),
        ]
        for copy in copies:
            copy.start()
        for copy in copies:
            copy.wait()
        both = jnp.concatenate([lead[:, last], inverse_other[...]], axis=0)
        rest = [sums[:, place * cands : (place + 1) * cands] for place in places]
        second = dot(both, -(jnp.concatenate(rest, axis=1) + more[...]), 1)
        bundle[...] = second

    @pl.when(row[0] == 1)
    def _():
        copy = pltpu.make_async_copy(first, bundle, sems.at[3])
        copy.start()
        copy.wait()


def rows_kernel(row, held, got, flat, whole, early, beside, tail, cross, own, send, *refs):
    mine, other, base, sems = refs
    n_design, cands = base.shape
    depth = held.shape[0] // 2
    parts = [slice(at * n_design // 4, (at + 1) * n_design // 4) for at in range(4)]
    is_odd = row[0] % 2 == 1

    def fetch(at, source):
        return pltpu.make_async_copy(source, other.at[:, parts[at]], sems.at[at])

    @pl.when(row[0] > 0)
    def _():
        copies = []
        for at, part in enumerate(parts):
            copies.append(
                [
                    pltpu.make_async_copy(flat.at[:, part], mine.at[:, part], sems.at[4 + at]),
                    pltpu.make_async_copy(cross.at[part], base.at[part], sems.at[8 + at]),
                ]
            )
        sources = [
            (row[0] == 1, [array.at[:, part] for array in (beside, tail) for part in parts[:2]]),
            (
                (row[0] > 1) & ~is_odd,
                [array.at[:, part] for array in (early, tail) for part in parts[:2]],
            ),
            ((row[0] > 1) & is_odd, [whole.at[:, part] for part in parts]),
        ]
        for at in range(4):
            for chosen, pieces in sources:
                pl.when(chosen)(lambda at=at, pieces=pieces: fetch(at, pieces[at]).start())
            for copy in copies[at]:
                copy.start()
        has_first = (row[0] == 1) | ((row[0] > 1) & ~is_odd)
        first = jnp.where(has_first, held[...], got[...])
        second = jnp.where(has_first, got[...], held[...])
        solved = jnp.concatenate(
            [first[:depth], second[:depth], first[depth:], second[depth:]], axis=0
        )
        solved = split(solved)
        for at, part in enumerate(parts):
            fetch(at, whole.at[:, part]).wait()
            for copy in copies[at]:
                copy.wait()
            factors = jnp.concatenate([mine[:, part], other[:, part]], axis=0)
            partial = dot(factors, solved, 0)
            own[part] = base[part] - partial[:, :cands]
            send[part] = partial[:, cands:]


def top_kernel(offsets, col, pair, *refs):
    others, out = refs[:-1], refs[-1]
    cands = out.shape[1]
    depth = pair.shape[0] // 4
    n_cols = len(offsets)
    sources = [pair[:, :cands]] + [other[...] for other in others]
    for panel in range(2):
        pieces = []
        for source in sources:
            for at in (2 * panel, 2 * panel + 1):
                pieces.append(source[at * depth : (at + 1) * depth])
        pieces = [pieces[offsets.index(at)] for at in range(n_cols)]
        bit = 1
        while bit < n_cols:
            flipped = (col[0] & bit) != 0
            pieces = [jnp.where(flipped, pieces[at ^ bit], pieces[at]) for at in range(n_cols)]
            bit *= 2
        for at, piece in enumerate(pieces):
            place = (panel * n_cols + at) * depth
            out[place : place + depth] = piece


def make_on_device(n_rows, n_cols):
    half = n_cols // 2

    def swap(array, flip, rows):
        pairs = [
            (row * n_cols + col, row * n_cols + (col ^ flip))
            for row in rows
            for col in range(n_cols)
        ]
        return lax.ppermute(array, AXES, pairs)

    def send_down(array, offset, have):
        pairs = [
            (row * n_cols + col, target(row, offset) * n_cols + col)
            for row in have
            for col in range(n_cols)
        ]
        return lax.ppermute(array, AXES, pairs)

    def target(row, offset):
        return (row + offset) ^ (1 if row < 2 and offset > 1 else 0)

    def spread(array, row_id, low, radix, have):
        digit = (row_id // low) % radix
        result = array
        for step in (2, 1, 3) if radix == 4 else range(1, radix):
            result = jnp.where(digit == step, send_down(array, step * low, have), result)
        return result, [target(row, step * low) for row in have for step in range(radix)]

    def broadcast_outer(array, row_id):
        low = n_rows
        have = [0, 1]
        while low > 2:
            radix = min(4, low // 2)
            low //= radix
            array, have = spread(array, row_id, low, radix, have)
        return array

    def swap_cores(array):
        pairs = [
            (row * n_cols + col, (row ^ 1) * n_cols + col)
            for row in range(n_rows)
            for col in range(n_cols)
        ]
        return lax.ppermute(array, AXES, pairs)

    def block(array, place, cands):
        return array[:, place * cands : (place + 1) * cands]

    def shuffle(array, flip, cands):
        return jnp.concatenate([block(array, at ^ flip, cands) for at in range(half)], axis=1)

    def on_device(cross_kernel, factor_panels, block_inverses):
        row_id = lax.axis_index("rows")
        col_id = lax.axis_index("cols")
        width = block_inverses.shape[2]
        depth = block_inverses.shape[1]
        n_design, cands = cross_kernel.shape
        count = n_design // 2
        top = [0]
        beside = [1]
        evens, odds = range(2, n_rows, 2), range(3, n_rows, 2)
        flat = factor_panels.reshape(2 * depth, n_design)

        lead = jnp.concatenate(
            [block_inverses[0], factor_panels[0, :, width : 2 * width], block_inverses[1]], axis=1
        )
        lead, rhs = lax.optimization_barrier((lead, cross_kernel))
        lead_other = swap(lead, half, top)
        rhs_others = [swap(rhs, step, top) for step in range(1, half)]
        whole = swap(flat, half, odds)
        arrived = swap(flat[:, :count], half, evens)
        lead_other, head, tail = lax.optimization_barrier(
            (lead_other, flat[:, : n_design // 2], flat[:, count:])
        )

        places = [at ^ 1 for at in range(half)]
        first, shuffled = call(
            functools.partial(first_kernel, places, width),
            [(2 * depth, half * cands), (width, half * cands)],
            6 * width * half * cands * (2 * depth + 2 * depth),
            [lead, rhs],
            [lead_other, *rhs_others],
            row_id,
            [(depth, 2 * width)] + [(width, cands)] * len(rhs_others),
        )
        shuffled, arrived, whole = lax.optimization_barrier((shuffled, arrived, whole))
        sums = got = swap(shuffled, 1, top)
        bit = 2
        while bit < half:
            update = shuffle(shuffled, 1, cands) + sums
            got = swap(shuffle(update, bit, cands), bit, top)
            sums = sums + got
            bit *= 2
        first_beside = send_down(first, 1, top)
        (bundle,) = call(
            functools.partial(second_kernel, places),
            [(2 * depth, half * cands)],
            6 * 2 * depth * width * half * cands,
            [lead],
            [lead_other, shuffled, sums, first_beside],
            row_id,
            [(depth, width)] + [(width, half * cands)] * 2,
        )
        first_beside, head = lax.optimization_barrier((first_beside, head))
        late = swap(head, half, beside)
        held = broadcast_outer(bundle, row_id)
        held, late = lax.optimization_barrier((held, late))
        tail = swap(tail, half, [*beside, *evens])
        solved = [held, swap_cores(held)]

        pair = jnp.concatenate([first, held], axis=0)
        others = [swap(block(pair, step, cands), step, top) for step in range(1, half)]
        offsets = [at for step in range(half) for at in (step, step ^ half)]
        (top_rows,) = call(
            functools.partial(top_kernel, offsets),
            [(2 * width, cands)],
            0,
            [pair, *others],
            flag=col_id,
        )

        fresh, send = call(
            rows_kernel,
            [(n_design, cands), (n_design, (half - 1) * cands)],
            6 * n_design * 4 * depth * half * cands,
            solved,
            [flat, whole, arrived, late, tail, cross_kernel],
            row_id,
            [(2 * depth, n_design)] * 2 + [(n_design, cands)],
        )
        for step in range(1, half):
            fresh = fresh - swap(block(send, step - 1, cands), step, range(1, n_rows))
        return jnp.where(row_id == 0, top_rows, fresh)

    return on_device


def solution(mesh):
    in_specs = (P("rows", "cols"), P(None, "cols", "rows"), P(None, "cols", None))
    out_specs = P("rows", "cols")
    return jax.shard_map(
        make_on_device(mesh.shape["rows"], mesh.shape["cols"]),
        mesh=mesh,
        in_specs=in_specs,
        out_specs=out_specs,
        check_vma=False,
    )
```

```python
import functools
import jax
import jax.numpy as jnp
from jax import lax
from jax.experimental import pallas as pl
from jax.experimental.pallas import tpu as pltpu
from jax.sharding import PartitionSpec as P

AXES = ("rows", "cols")
LIMIT = 12 * 1024 * 1024


def split(array):
    high = array.astype(jnp.bfloat16)
    return high, (array - high.astype(jnp.float32)).astype(jnp.bfloat16)


def dot(left, right, left_dim):
    def one(a, b):
        return lax.dot_general(
            a, b, (((left_dim,), (0,)), ((), ())), preferred_element_type=jnp.float32
        )

    left_high, left_low = split(left)
    right_high, right_low = right if isinstance(right, tuple) else split(right)
    return one(left_high, right_high) + (one(left_high, right_low) + one(left_low, right_high))


def call(kernel, shapes, flops, near, far=(), flag=None, scratch=()):
    flags = [] if flag is None else [flag.astype(jnp.int32).reshape(1)]
    spaces = [pltpu.SMEM] * len(flags) + [pltpu.VMEM] * len(near) + [pltpu.HBM] * len(far)
    return pl.pallas_call(
        kernel,
        out_shape=[jax.ShapeDtypeStruct(shape, jnp.float32) for shape in shapes],
        in_specs=[pl.BlockSpec(memory_space=space) for space in spaces],
        out_specs=[pl.BlockSpec(memory_space=pltpu.VMEM)] * len(shapes),
        scratch_shapes=[pltpu.VMEM(shape, jnp.float32) for shape in scratch]
        + [pltpu.SemaphoreType.DMA((12,))] * (1 if far else 0),
        compiler_params=pltpu.CompilerParams(vmem_limit_bytes=LIMIT),
        cost_estimate=pl.CostEstimate(flops=flops, bytes_accessed=0, transcendentals=0),
    )(*flags, *near, *far)


def first_kernel(places, width, row, lead, rhs, far_lead, *refs):
    others, (solved, shuffled, lead_other, *held, sems) = (
        refs[: len(places) - 1],
        refs[len(places) - 1 :],
    )
    cands = rhs.shape[1]

    @pl.when(row[0] == 0)
    def _():
        copies = [
            pltpu.make_async_copy(other.at[:width], place, sems.at[at])
            for at, (other, place) in enumerate(zip(others, held))
        ]
        copies.append(
            pltpu.make_async_copy(
                far_lead.at[:, : 2 * width], lead_other, sems.at[len(copies)]
            )
        )
        for copy in copies:
            copy.start()
        for copy in copies:
            copy.wait()
        blocks = jnp.concatenate([rhs[:width]] + [place[...] for place in held], axis=1)
        inverse = jnp.concatenate([lead[:, :width], lead_other[:, :width]], axis=0)
        first = dot(inverse, blocks, 1)
        solved[...] = first
        middle = slice(width, 2 * width)
        corner = jnp.concatenate([lead[:, middle], lead_other[:, middle]], axis=0)
        total = dot(corner, first, 0)
        pieces = [total[:, at * cands : (at + 1) * cands] for at in range(len(places))]
        pieces[0] = pieces[0] - rhs[middle]
        for at, place in enumerate(places):
            shuffled[:, at * cands : (at + 1) * cands] = pieces[place]


def second_kernel(places, row, lead, far_lead, sent, got, first, bundle, *refs):
    inverse_other, sums, more, sems = refs
    width = sums.shape[0]
    cands = sums.shape[1] // len(places)

    last = slice(2 * width, 3 * width)

    @pl.when(row[0] == 0)
    def _():
        copies = [
            pltpu.make_async_copy(sent, sums, sems.at[0]),
            pltpu.make_async_copy(got, more, sems.at[1]),
            pltpu.make_async_copy(far_lead.at[:, last], inverse_other, sems.at[2]),
        ]
        for copy in copies:
            copy.start()
        for copy in copies:
            copy.wait()
        both = jnp.concatenate([lead[:, last], inverse_other[...]], axis=0)
        rest = [sums[:, place * cands : (place + 1) * cands] for place in places]
        second = dot(both, -(jnp.concatenate(rest, axis=1) + more[...]), 1)
        bundle[...] = second

    @pl.when(row[0] == 1)
    def _():
        copy = pltpu.make_async_copy(first, bundle, sems.at[3])
        copy.start()
        copy.wait()


def rows_kernel(row, held, got, flat, whole, early, beside, tail, cross, own, send, *refs):
    mine, other, base, sems = refs
    n_design, cands = base.shape
    depth = held.shape[0] // 2
    parts = [slice(at * n_design // 4, (at + 1) * n_design // 4) for at in range(4)]
    is_odd = row[0] % 2 == 1

    def fetch(at, source):
        return pltpu.make_async_copy(source, other.at[:, parts[at]], sems.at[at])

    @pl.when(row[0] > 0)
    def _():
        copies = []
        for at, part in enumerate(parts):
            copies.append(
                [
                    pltpu.make_async_copy(flat.at[:, part], mine.at[:, part], sems.at[4 + at]),
                    pltpu.make_async_copy(cross.at[part], base.at[part], sems.at[8 + at]),
                ]
            )
        sources = [
            (row[0] == 1, [beside.at[:, part] for part in parts]),
            (
                (row[0] > 1) & ~is_odd,
                [array.at[:, part] for array in (early, tail) for part in parts[:2]],
            ),
            ((row[0] > 1) & is_odd, [whole.at[:, part] for part in parts]),
        ]
        for at in range(4):
            for chosen, pieces in sources:
                pl.when(chosen)(lambda at=at, pieces=pieces: fetch(at, pieces[at]).start())
            for copy in copies[at]:
                copy.start()
        has_first = (row[0] == 1) | ((row[0] > 1) & ~is_odd)
        first = jnp.where(has_first, held[...], got[...])
        second = jnp.where(has_first, got[...], held[...])
        solved = jnp.concatenate(
            [first[:depth], second[:depth], first[depth:], second[depth:]], axis=0
        )
        solved = split(solved)
        for at, part in enumerate(parts):
            fetch(at, whole.at[:, part]).wait()
            for copy in copies[at]:
                copy.wait()
            factors = jnp.concatenate([mine[:, part], other[:, part]], axis=0)
            partial = dot(factors, solved, 0)
            own[part] = base[part] - partial[:, :cands]
            send[part] = partial[:, cands:]


def top_kernel(offsets, col, pair, *refs):
    others, out = refs[:-1], refs[-1]
    cands = out.shape[1]
    depth = pair.shape[0] // 4
    n_cols = len(offsets)
    sources = [pair[:, :cands]] + [other[...] for other in others]
    for panel in range(2):
        pieces = []
        for source in sources:
            for at in (2 * panel, 2 * panel + 1):
                pieces.append(source[at * depth : (at + 1) * depth])
        pieces = [pieces[offsets.index(at)] for at in range(n_cols)]
        bit = 1
        while bit < n_cols:
            flipped = (col[0] & bit) != 0
            pieces = [jnp.where(flipped, pieces[at ^ bit], pieces[at]) for at in range(n_cols)]
            bit *= 2
        for at, piece in enumerate(pieces):
            place = (panel * n_cols + at) * depth
            out[place : place + depth] = piece


def make_on_device(n_rows, n_cols):
    half = n_cols // 2

    def swap(array, flip, rows):
        pairs = [
            (row * n_cols + col, row * n_cols + (col ^ flip))
            for row in rows
            for col in range(n_cols)
        ]
        return lax.ppermute(array, AXES, pairs)

    def send_down(array, offset, have):
        pairs = [
            (row * n_cols + col, target(row, offset) * n_cols + col)
            for row in have
            for col in range(n_cols)
        ]
        return lax.ppermute(array, AXES, pairs)

    def target(row, offset):
        return (row + offset) ^ (1 if row < 2 and offset > 1 else 0)

    def spread(array, row_id, low, radix, have):
        digit = (row_id // low) % radix
        result = array
        for step in (2, 1, 3) if radix == 4 else range(1, radix):
            result = jnp.where(digit == step, send_down(array, step * low, have), result)
        return result, [target(row, step * low) for row in have for step in range(radix)]

    def broadcast_outer(array, row_id):
        low = n_rows
        have = [0, 1]
        while low > 2:
            radix = min(4, low // 2)
            low //= radix
            array, have = spread(array, row_id, low, radix, have)
        return array

    def swap_cores(array):
        pairs = [
            (row * n_cols + col, (row ^ 1) * n_cols + col)
            for row in range(n_rows)
            for col in range(n_cols)
        ]
        return lax.ppermute(array, AXES, pairs)

    def block(array, place, cands):
        return array[:, place * cands : (place + 1) * cands]

    def shuffle(array, flip, cands):
        return jnp.concatenate([block(array, at ^ flip, cands) for at in range(half)], axis=1)

    def on_device(cross_kernel, factor_panels, block_inverses):
        row_id = lax.axis_index("rows")
        col_id = lax.axis_index("cols")
        width = block_inverses.shape[2]
        depth = block_inverses.shape[1]
        n_design, cands = cross_kernel.shape
        count = n_design // 2
        top = [0]
        beside = [1]
        evens, odds = range(2, n_rows, 2), range(3, n_rows, 2)
        flat = factor_panels.reshape(2 * depth, n_design)

        lead = jnp.concatenate(
            [block_inverses[0], factor_panels[0, :, width : 2 * width], block_inverses[1]], axis=1
        )
        lead, rhs = lax.optimization_barrier((lead, cross_kernel))
        lead_other = swap(lead, half, top)
        rhs_others = [swap(rhs, step, top) for step in range(1, half)]
        whole = swap(flat, half, odds)
        arrived = swap(flat[:, :count], half, evens)
        lead_other, tail = lax.optimization_barrier((lead_other, flat[:, count:]))

        places = [at ^ 1 for at in range(half)]
        first, shuffled = call(
            functools.partial(first_kernel, places, width),
            [(2 * depth, half * cands), (width, half * cands)],
            6 * width * half * cands * (2 * depth + 2 * depth),
            [lead, rhs],
            [lead_other, *rhs_others],
            row_id,
            [(depth, 2 * width)] + [(width, cands)] * len(rhs_others),
        )
        shuffled, arrived, whole = lax.optimization_barrier((shuffled, arrived, whole))
        sums = got = swap(shuffled, 1, top)
        bit = 2
        while bit < half:
            update = shuffle(shuffled, 1, cands) + sums
            got = swap(shuffle(update, bit, cands), bit, top)
            sums = sums + got
            bit *= 2
        first_beside = send_down(first, 1, top)
        (bundle,) = call(
            functools.partial(second_kernel, places),
            [(2 * depth, half * cands)],
            6 * 2 * depth * width * half * cands,
            [lead],
            [lead_other, shuffled, sums, first_beside],
            row_id,
            [(depth, width)] + [(width, half * cands)] * 2,
        )
        first_beside, late = lax.optimization_barrier((first_beside, flat))
        late = swap(late, half, beside)
        held = broadcast_outer(bundle, row_id)
        tail = swap(tail, half, evens)
        held, late, tail = lax.optimization_barrier((held, late, tail))
        solved = [held, swap_cores(held)]

        pair = jnp.concatenate([first, held], axis=0)
        others = [swap(block(pair, step, cands), step, top) for step in range(1, half)]
        offsets = [at for step in range(half) for at in (step, step ^ half)]
        (top_rows,) = call(
            functools.partial(top_kernel, offsets),
            [(2 * width, cands)],
            0,
            [pair, *others],
            flag=col_id,
        )

        fresh, send = call(
            rows_kernel,
            [(n_design, cands), (n_design, (half - 1) * cands)],
            6 * n_design * 4 * depth * half * cands,
            solved,
            [flat, whole, arrived, late, tail, cross_kernel],
            row_id,
            [(2 * depth, n_design)] * 2 + [(n_design, cands)],
        )
        for step in range(1, half):
            fresh = fresh - swap(block(send, step - 1, cands), step, range(1, n_rows))
        return jnp.where(row_id == 0, top_rows, fresh)

    return on_device


def solution(mesh):
    in_specs = (P("rows", "cols"), P(None, "cols", "rows"), P(None, "cols", None))
    out_specs = P("rows", "cols")
    return jax.shard_map(
        make_on_device(mesh.shape["rows"], mesh.shape["cols"]),
        mesh=mesh,
        in_specs=in_specs,
        out_specs=out_specs,
        check_vma=False,
    )
```

```python
import functools
import jax
import jax.numpy as jnp
from jax import lax
from jax.experimental import pallas as pl
from jax.experimental.pallas import tpu as pltpu
from jax.sharding import PartitionSpec as P

AXES = ("rows", "cols")
LIMIT = 12 * 1024 * 1024


def split(array):
    high = array.astype(jnp.bfloat16)
    return high, (array - high.astype(jnp.float32)).astype(jnp.bfloat16)


def dot(left, right, left_dim):
    def one(a, b):
        return lax.dot_general(
            a, b, (((left_dim,), (0,)), ((), ())), preferred_element_type=jnp.float32
        )

    left_high, left_low = split(left)
    right_high, right_low = split(right)
    return one(left_high, right_high) + (one(left_high, right_low) + one(left_low, right_high))


def call(kernel, shapes, flops, near, far=(), flag=None, scratch=()):
    flags = [] if flag is None else [flag.astype(jnp.int32).reshape(1)]
    spaces = [pltpu.SMEM] * len(flags) + [pltpu.VMEM] * len(near) + [pltpu.HBM] * len(far)
    return pl.pallas_call(
        kernel,
        out_shape=[jax.ShapeDtypeStruct(shape, jnp.float32) for shape in shapes],
        in_specs=[pl.BlockSpec(memory_space=space) for space in spaces],
        out_specs=[pl.BlockSpec(memory_space=pltpu.VMEM)] * len(shapes),
        scratch_shapes=[pltpu.VMEM(shape, jnp.float32) for shape in scratch]
        + [pltpu.SemaphoreType.DMA((6,))] * (1 if far else 0),
        compiler_params=pltpu.CompilerParams(vmem_limit_bytes=LIMIT),
        cost_estimate=pl.CostEstimate(flops=flops, bytes_accessed=0, transcendentals=0),
    )(*flags, *near, *far)


def first_kernel(places, width, row, lead, rhs, far_lead, *refs):
    others, (solved, shuffled, lead_other, *held, sems) = (
        refs[: len(places) - 1],
        refs[len(places) - 1 :],
    )
    cands = rhs.shape[1]

    @pl.when(row[0] == 0)
    def _():
        copies = [
            pltpu.make_async_copy(other.at[:width], place, sems.at[at])
            for at, (other, place) in enumerate(zip(others, held))
        ]
        copies.append(
            pltpu.make_async_copy(
                far_lead.at[:, : 2 * width], lead_other, sems.at[len(copies)]
            )
        )
        for copy in copies:
            copy.start()
        for copy in copies:
            copy.wait()
        blocks = jnp.concatenate([rhs[:width]] + [place[...] for place in held], axis=1)
        inverse = jnp.concatenate([lead[:, :width], lead_other[:, :width]], axis=0)
        first = dot(inverse, blocks, 1)
        solved[...] = first
        middle = slice(width, 2 * width)
        corner = jnp.concatenate([lead[:, middle], lead_other[:, middle]], axis=0)
        total = dot(corner, first, 0)
        pieces = [total[:, at * cands : (at + 1) * cands] for at in range(len(places))]
        pieces[0] = pieces[0] - rhs[middle]
        for at, place in enumerate(places):
            shuffled[:, at * cands : (at + 1) * cands] = pieces[place]


def second_kernel(places, row, lead, far_lead, sent, got, first, bundle, *refs):
    inverse_other, sums, more, sems = refs
    width = sums.shape[0]
    cands = sums.shape[1] // len(places)

    last = slice(2 * width, 3 * width)

    @pl.when(row[0] == 0)
    def _():
        copies = [
            pltpu.make_async_copy(sent, sums, sems.at[0]),
            pltpu.make_async_copy(got, more, sems.at[1]),
            pltpu.make_async_copy(far_lead.at[:, last], inverse_other, sems.at[2]),
        ]
        for copy in copies:
            copy.start()
        for copy in copies:
            copy.wait()
        both = jnp.concatenate([lead[:, last], inverse_other[...]], axis=0)
        rest = [sums[:, place * cands : (place + 1) * cands] for place in places]
        second = dot(both, -(jnp.concatenate(rest, axis=1) + more[...]), 1)
        bundle[...] = second

    @pl.when(row[0] == 1)
    def _():
        copy = pltpu.make_async_copy(first, bundle, sems.at[3])
        copy.start()
        copy.wait()


def rows_kernel(row, held, got, flat, whole, early, beside, tail, cross, own, send, *refs):
    mine, other, base, sems = refs
    n_design, cands = base.shape
    depth = held.shape[0] // 2
    parts = [slice(at * n_design // 2, (at + 1) * n_design // 2) for at in range(2)]
    is_odd = row[0] % 2 == 1

    def fetch(at, source):
        return pltpu.make_async_copy(source, other.at[:, parts[at]], sems.at[at])

    @pl.when(row[0] > 0)
    def _():
        copies = []
        for at, part in enumerate(parts):
            copies.append(
                [
                    pltpu.make_async_copy(flat.at[:, part], mine.at[:, part], sems.at[2 + at]),
                    pltpu.make_async_copy(cross.at[part], base.at[part], sems.at[4 + at]),
                ]
            )
        sources = [
            (row[0] == 1, [beside.at[:, part] for part in parts]),
            ((row[0] > 1) & ~is_odd, [early, tail]),
            ((row[0] > 1) & is_odd, [whole.at[:, part] for part in parts]),
        ]
        for at in range(2):
            for chosen, pieces in sources:
                pl.when(chosen)(lambda at=at, pieces=pieces: fetch(at, pieces[at]).start())
            for copy in copies[at]:
                copy.start()
        has_first = (row[0] == 1) | ((row[0] > 1) & ~is_odd)
        first = jnp.where(has_first, held[...], got[...])
        second = jnp.where(has_first, got[...], held[...])
        solved = jnp.concatenate(
            [first[:depth], second[:depth], first[depth:], second[depth:]], axis=0
        )
        for at, part in enumerate(parts):
            fetch(at, whole.at[:, part]).wait()
            for copy in copies[at]:
                copy.wait()
            factors = jnp.concatenate([mine[:, part], other[:, part]], axis=0)
            partial = dot(solved, factors, 0)
            own[part] = base[part] - partial[:cands].T
            send[part] = partial[cands:].T


def top_kernel(offsets, col, pair, *refs):
    others, out = refs[:-1], refs[-1]
    cands = out.shape[1]
    depth = pair.shape[0] // 4
    n_cols = len(offsets)
    sources = [pair[:, :cands]] + [other[...] for other in others]
    for panel in range(2):
        pieces = []
        for source in sources:
            for at in (2 * panel, 2 * panel + 1):
                pieces.append(source[at * depth : (at + 1) * depth])
        pieces = [pieces[offsets.index(at)] for at in range(n_cols)]
        bit = 1
        while bit < n_cols:
            flipped = (col[0] & bit) != 0
            pieces = [jnp.where(flipped, pieces[at ^ bit], pieces[at]) for at in range(n_cols)]
            bit *= 2
        for at, piece in enumerate(pieces):
            place = (panel * n_cols + at) * depth
            out[place : place + depth] = piece


def make_on_device(n_rows, n_cols):
    half = n_cols // 2

    def swap(array, flip, rows):
        pairs = [
            (row * n_cols + col, row * n_cols + (col ^ flip))
            for row in rows
            for col in range(n_cols)
        ]
        return lax.ppermute(array, AXES, pairs)

    def send_down(array, offset, have):
        pairs = [
            (row * n_cols + col, target(row, offset) * n_cols + col)
            for row in have
            for col in range(n_cols)
        ]
        return lax.ppermute(array, AXES, pairs)

    def target(row, offset):
        return (row + offset) ^ (1 if row < 2 and offset > 1 else 0)

    def spread(array, row_id, low, radix, have):
        digit = (row_id // low) % radix
        result = array
        for step in (2, 1, 3) if radix == 4 else range(1, radix):
            result = jnp.where(digit == step, send_down(array, step * low, have), result)
        return result, [target(row, step * low) for row in have for step in range(radix)]

    def broadcast_outer(array, row_id):
        low = n_rows
        have = [0, 1]
        while low > 2:
            radix = min(4, low // 2)
            low //= radix
            array, have = spread(array, row_id, low, radix, have)
        return array

    def swap_cores(array):
        pairs = [
            (row * n_cols + col, (row ^ 1) * n_cols + col)
            for row in range(n_rows)
            for col in range(n_cols)
        ]
        return lax.ppermute(array, AXES, pairs)

    def block(array, place, cands):
        return array[:, place * cands : (place + 1) * cands]

    def shuffle(array, flip, cands):
        return jnp.concatenate([block(array, at ^ flip, cands) for at in range(half)], axis=1)

    def on_device(cross_kernel, factor_panels, block_inverses):
        row_id = lax.axis_index("rows")
        col_id = lax.axis_index("cols")
        width = block_inverses.shape[2]
        depth = block_inverses.shape[1]
        n_design, cands = cross_kernel.shape
        count = n_design // 2
        top = [0]
        beside = [1]
        evens, odds = range(2, n_rows, 2), range(3, n_rows, 2)
        flat = factor_panels.reshape(2 * depth, n_design)

        lead = jnp.concatenate(
            [block_inverses[0], factor_panels[0, :, width : 2 * width], block_inverses[1]], axis=1
        )
        lead, rhs = lax.optimization_barrier((lead, cross_kernel))
        lead_other = swap(lead, half, top)
        rhs_others = [swap(rhs, step, top) for step in range(1, half)]
        whole = swap(flat, half, odds)
        arrived = swap(flat[:, :count], half, evens)
        lead_other, tail = lax.optimization_barrier((lead_other, flat[:, count:]))

        places = [at ^ 1 for at in range(half)]
        first, shuffled = call(
            functools.partial(first_kernel, places, width),
            [(2 * depth, half * cands), (width, half * cands)],
            6 * width * half * cands * (2 * depth + 2 * depth),
            [lead, rhs],
            [lead_other, *rhs_others],
            row_id,
            [(depth, 2 * width)] + [(width, cands)] * len(rhs_others),
        )
        shuffled, arrived, whole = lax.optimization_barrier((shuffled, arrived, whole))
        sums = got = swap(shuffled, 1, top)
        bit = 2
        while bit < half:
            update = shuffle(shuffled, 1, cands) + sums
            got = swap(shuffle(update, bit, cands), bit, top)
            sums = sums + got
            bit *= 2
        first_beside = send_down(first, 1, top)
        (bundle,) = call(
            functools.partial(second_kernel, places),
            [(2 * depth, half * cands)],
            6 * 2 * depth * width * half * cands,
            [lead],
            [lead_other, shuffled, sums, first_beside],
            row_id,
            [(depth, width)] + [(width, half * cands)] * 2,
        )
        first_beside, late = lax.optimization_barrier((first_beside, flat))
        late = swap(late, half, beside)
        held = broadcast_outer(bundle, row_id)
        tail = swap(tail, half, evens)
        held, tail = lax.optimization_barrier((held, tail))
        solved = [held, swap_cores(held)]

        pair = jnp.concatenate([first, held], axis=0)
        others = [swap(block(pair, step, cands), step, top) for step in range(1, half)]
        offsets = [at for step in range(half) for at in (step, step ^ half)]
        (top_rows,) = call(
            functools.partial(top_kernel, offsets),
            [(2 * width, cands)],
            0,
            [pair, *others],
            flag=col_id,
        )

        fresh, send = call(
            rows_kernel,
            [(n_design, cands), (n_design, (half - 1) * cands)],
            6 * n_design * 4 * depth * half * cands,
            solved,
            [flat, whole, arrived, late, tail, cross_kernel],
            row_id,
            [(2 * depth, n_design)] * 2 + [(n_design, cands)],
        )
        for step in range(1, half):
            fresh = fresh - swap(block(send, step - 1, cands), step, range(1, n_rows))
        return jnp.where(row_id == 0, top_rows, fresh)

    return on_device


def solution(mesh):
    in_specs = (P("rows", "cols"), P(None, "cols", "rows"), P(None, "cols", None))
    out_specs = P("rows", "cols")
    return jax.shard_map(
        make_on_device(mesh.shape["rows"], mesh.shape["cols"]),
        mesh=mesh,
        in_specs=in_specs,
        out_specs=out_specs,
        check_vma=False,
    )
```

```python
import functools
import jax
import jax.numpy as jnp
from jax import lax
from jax.experimental import pallas as pl
from jax.experimental.pallas import tpu as pltpu
from jax.sharding import PartitionSpec as P

AXES = ("rows", "cols")
LIMIT = 12 * 1024 * 1024


def split(array):
    high = array.astype(jnp.bfloat16)
    return high, (array - high.astype(jnp.float32)).astype(jnp.bfloat16)


def dot(left, right, left_dim):
    def one(a, b):
        return lax.dot_general(
            a, b, (((left_dim,), (0,)), ((), ())), preferred_element_type=jnp.float32
        )

    left_high, left_low = split(left)
    right_high, right_low = split(right)
    return one(left_high, right_high) + (one(left_high, right_low) + one(left_low, right_high))


def call(kernel, shapes, flops, near, far=(), flag=None, scratch=()):
    flags = [] if flag is None else [flag.astype(jnp.int32).reshape(1)]
    spaces = [pltpu.SMEM] * len(flags) + [pltpu.VMEM] * len(near) + [pltpu.HBM] * len(far)
    return pl.pallas_call(
        kernel,
        out_shape=[jax.ShapeDtypeStruct(shape, jnp.float32) for shape in shapes],
        in_specs=[pl.BlockSpec(memory_space=space) for space in spaces],
        out_specs=[pl.BlockSpec(memory_space=pltpu.VMEM)] * len(shapes),
        scratch_shapes=[pltpu.VMEM(shape, jnp.float32) for shape in scratch]
        + [pltpu.SemaphoreType.DMA((6,))] * (1 if far else 0),
        compiler_params=pltpu.CompilerParams(vmem_limit_bytes=LIMIT),
        cost_estimate=pl.CostEstimate(flops=flops, bytes_accessed=0, transcendentals=0),
    )(*flags, *near, *far)


def first_kernel(places, width, row, lead, rhs, far_lead, *refs):
    others, (solved, shuffled, lead_other, *held, sems) = (
        refs[: len(places) - 1],
        refs[len(places) - 1 :],
    )
    cands = rhs.shape[1]

    @pl.when(row[0] == 0)
    def _():
        copies = [
            pltpu.make_async_copy(other.at[:width], place, sems.at[at])
            for at, (other, place) in enumerate(zip(others, held))
        ]
        copies.append(
            pltpu.make_async_copy(
                far_lead.at[:, : 2 * width], lead_other, sems.at[len(copies)]
            )
        )
        for copy in copies:
            copy.start()
        for copy in copies:
            copy.wait()
        blocks = jnp.concatenate([rhs[:width]] + [place[...] for place in held], axis=1)
        inverse = jnp.concatenate([lead[:, :width], lead_other[:, :width]], axis=0)
        first = dot(inverse, blocks, 1)
        solved[...] = first
        middle = slice(width, 2 * width)
        corner = jnp.concatenate([lead[:, middle], lead_other[:, middle]], axis=0)
        total = dot(corner, first, 0)
        pieces = [total[:, at * cands : (at + 1) * cands] for at in range(len(places))]
        pieces[0] = pieces[0] - rhs[middle]
        for at, place in enumerate(places):
            shuffled[:, at * cands : (at + 1) * cands] = pieces[place]


def second_kernel(places, row, lead, far_lead, sent, got, first, bundle, *refs):
    inverse_other, sums, more, sems = refs
    width = sums.shape[0]
    cands = sums.shape[1] // len(places)

    last = slice(2 * width, 3 * width)

    @pl.when(row[0] == 0)
    def _():
        copies = [
            pltpu.make_async_copy(sent, sums, sems.at[0]),
            pltpu.make_async_copy(got, more, sems.at[1]),
            pltpu.make_async_copy(far_lead.at[:, last], inverse_other, sems.at[2]),
        ]
        for copy in copies:
            copy.start()
        for copy in copies:
            copy.wait()
        both = jnp.concatenate([lead[:, last], inverse_other[...]], axis=0)
        rest = [sums[:, place * cands : (place + 1) * cands] for place in places]
        second = dot(both, -(jnp.concatenate(rest, axis=1) + more[...]), 1)
        bundle[...] = second

    @pl.when(row[0] == 1)
    def _():
        copy = pltpu.make_async_copy(first, bundle, sems.at[3])
        copy.start()
        copy.wait()


def rows_kernel(row, held, got, flat, whole, early, beside, tail, cross, own, send, *refs):
    mine, other, base, sems = refs
    n_design, cands = base.shape
    depth = held.shape[0] // 2
    parts = [slice(at * n_design // 2, (at + 1) * n_design // 2) for at in range(2)]
    is_odd = row[0] % 2 == 1

    def fetch(at, source):
        return pltpu.make_async_copy(source, other.at[:, parts[at]], sems.at[at])

    @pl.when(row[0] > 0)
    def _():
        copies = []
        for at, part in enumerate(parts):
            copies.append(
                [
                    pltpu.make_async_copy(flat.at[:, part], mine.at[:, part], sems.at[2 + at]),
                    pltpu.make_async_copy(cross.at[part], base.at[part], sems.at[4 + at]),
                ]
            )
        sources = [
            (row[0] == 1, [beside.at[:, part] for part in parts]),
            ((row[0] > 1) & ~is_odd, [early, tail]),
            ((row[0] > 1) & is_odd, [whole.at[:, part] for part in parts]),
        ]
        for at in range(2):
            for chosen, pieces in sources:
                pl.when(chosen)(lambda at=at, pieces=pieces: fetch(at, pieces[at]).start())
            for copy in copies[at]:
                copy.start()
        has_first = (row[0] == 1) | ((row[0] > 1) & ~is_odd)
        first = jnp.where(has_first, held[...], got[...])
        second = jnp.where(has_first, got[...], held[...])
        solved = jnp.concatenate(
            [first[:depth], second[:depth], first[depth:], second[depth:]], axis=0
        )
        for at, part in enumerate(parts):
            fetch(at, whole.at[:, part]).wait()
            for copy in copies[at]:
                copy.wait()
            factors = jnp.concatenate([mine[:, part], other[:, part]], axis=0)
            partial = dot(solved, factors, 0)
            own[part] = base[part] - partial[:cands].T
            send[part] = partial[cands:].T


def top_kernel(offsets, col, pair, *refs):
    others, out = refs[:-1], refs[-1]
    cands = out.shape[1]
    depth = pair.shape[0] // 4
    n_cols = len(offsets)
    sources = [pair[:, :cands]] + [other[...] for other in others]
    for panel in range(2):
        pieces = []
        for source in sources:
            for at in (2 * panel, 2 * panel + 1):
                pieces.append(source[at * depth : (at + 1) * depth])
        pieces = [pieces[offsets.index(at)] for at in range(n_cols)]
        bit = 1
        while bit < n_cols:
            flipped = (col[0] & bit) != 0
            pieces = [jnp.where(flipped, pieces[at ^ bit], pieces[at]) for at in range(n_cols)]
            bit *= 2
        for at, piece in enumerate(pieces):
            place = (panel * n_cols + at) * depth
            out[place : place + depth] = piece


def make_on_device(n_rows, n_cols):
    half = n_cols // 2

    def swap(array, flip, rows):
        pairs = [
            (row * n_cols + col, row * n_cols + (col ^ flip))
            for row in rows
            for col in range(n_cols)
        ]
        return lax.ppermute(array, AXES, pairs)

    def send_down(array, offset, have):
        pairs = [
            (row * n_cols + col, target(row, offset) * n_cols + col)
            for row in have
            for col in range(n_cols)
        ]
        return lax.ppermute(array, AXES, pairs)

    def target(row, offset):
        return (row + offset) ^ (1 if row < 2 and offset > 1 else 0)

    def spread(array, row_id, low, radix, have):
        digit = (row_id // low) % radix
        result = array
        for step in (2, 1, 3) if radix == 4 else range(1, radix):
            result = jnp.where(digit == step, send_down(array, step * low, have), result)
        return result, [target(row, step * low) for row in have for step in range(radix)]

    def broadcast_outer(array, row_id):
        low = n_rows
        have = [0, 1]
        while low > 2:
            radix = min(4, low // 2)
            low //= radix
            array, have = spread(array, row_id, low, radix, have)
        return array

    def swap_cores(array):
        pairs = [
            (row * n_cols + col, (row ^ 1) * n_cols + col)
            for row in range(n_rows)
            for col in range(n_cols)
        ]
        return lax.ppermute(array, AXES, pairs)

    def block(array, place, cands):
        return array[:, place * cands : (place + 1) * cands]

    def shuffle(array, flip, cands):
        return jnp.concatenate([block(array, at ^ flip, cands) for at in range(half)], axis=1)

    def on_device(cross_kernel, factor_panels, block_inverses):
        row_id = lax.axis_index("rows")
        col_id = lax.axis_index("cols")
        width = block_inverses.shape[2]
        depth = block_inverses.shape[1]
        n_design, cands = cross_kernel.shape
        count = n_design // 2
        top = [0]
        beside = [1]
        evens, odds = range(2, n_rows, 2), range(3, n_rows, 2)
        flat = factor_panels.reshape(2 * depth, n_design)

        lead = jnp.concatenate(
            [block_inverses[0], factor_panels[0, :, width : 2 * width], block_inverses[1]], axis=1
        )
        lead, rhs = lax.optimization_barrier((lead, cross_kernel))
        lead_other = swap(lead, half, top)
        rhs_others = [swap(rhs, step, top) for step in range(1, half)]
        whole = swap(flat, half, odds)
        arrived = swap(flat[:, :count], half, evens)
        lead_other, tail = lax.optimization_barrier((lead_other, flat[:, count:]))

        places = [at ^ 1 for at in range(half)]
        first, shuffled = call(
            functools.partial(first_kernel, places, width),
            [(2 * depth, half * cands), (width, half * cands)],
            6 * width * half * cands * (2 * depth + 2 * depth),
            [lead, rhs],
            [lead_other, *rhs_others],
            row_id,
            [(depth, 2 * width)] + [(width, cands)] * len(rhs_others),
        )
        sums = got = swap(shuffled, 1, top)
        bit = 2
        while bit < half:
            update = shuffle(shuffled, 1, cands) + sums
            got = swap(shuffle(update, bit, cands), bit, top)
            sums = sums + got
            bit *= 2
        sums, whole, arrived = lax.optimization_barrier((sums, whole, arrived))
        first_beside = send_down(first, 1, top)
        (bundle,) = call(
            functools.partial(second_kernel, places),
            [(2 * depth, half * cands)],
            6 * 2 * depth * width * half * cands,
            [lead],
            [lead_other, shuffled, sums, first_beside],
            row_id,
            [(depth, width)] + [(width, half * cands)] * 2,
        )
        first_beside, late = lax.optimization_barrier((first_beside, flat))
        late = swap(late, half, beside)
        held = broadcast_outer(bundle, row_id)
        tail = swap(tail, half, evens)
        solved = [held, swap_cores(held)]

        pair = jnp.concatenate([first, held], axis=0)
        others = [swap(block(pair, step, cands), step, top) for step in range(1, half)]
        offsets = [at for step in range(half) for at in (step, step ^ half)]
        (top_rows,) = call(
            functools.partial(top_kernel, offsets),
            [(2 * width, cands)],
            0,
            [pair, *others],
            flag=col_id,
        )

        fresh, send = call(
            rows_kernel,
            [(n_design, cands), (n_design, (half - 1) * cands)],
            6 * n_design * 4 * depth * half * cands,
            solved,
            [flat, whole, arrived, late, tail, cross_kernel],
            row_id,
            [(2 * depth, n_design)] * 2 + [(n_design, cands)],
        )
        for step in range(1, half):
            fresh = fresh - swap(block(send, step - 1, cands), step, range(1, n_rows))
        return jnp.where(row_id == 0, top_rows, fresh)

    return on_device


def solution(mesh):
    in_specs = (P("rows", "cols"), P(None, "cols", "rows"), P(None, "cols", None))
    out_specs = P("rows", "cols")
    return jax.shard_map(
        make_on_device(mesh.shape["rows"], mesh.shape["cols"]),
        mesh=mesh,
        in_specs=in_specs,
        out_specs=out_specs,
        check_vma=False,
    )
```

```python
import functools
import jax
import jax.numpy as jnp
from jax import lax
from jax.experimental import pallas as pl
from jax.experimental.pallas import tpu as pltpu
from jax.sharding import PartitionSpec as P

AXES = ("rows", "cols")
LIMIT = 12 * 1024 * 1024


def split(array):
    high = array.astype(jnp.bfloat16)
    return high, (array - high.astype(jnp.float32)).astype(jnp.bfloat16)


def dot(left, right, left_dim):
    def one(a, b):
        return lax.dot_general(
            a, b, (((left_dim,), (0,)), ((), ())), preferred_element_type=jnp.float32
        )

    left_high, left_low = split(left)
    right_high, right_low = split(right)
    return one(left_high, right_high) + (one(left_high, right_low) + one(left_low, right_high))


def call(kernel, shapes, flops, near, far=(), flag=None, scratch=()):
    flags = [] if flag is None else [flag.astype(jnp.int32).reshape(1)]
    spaces = [pltpu.SMEM] * len(flags) + [pltpu.VMEM] * len(near) + [pltpu.HBM] * len(far)
    return pl.pallas_call(
        kernel,
        out_shape=[jax.ShapeDtypeStruct(shape, jnp.float32) for shape in shapes],
        in_specs=[pl.BlockSpec(memory_space=space) for space in spaces],
        out_specs=[pl.BlockSpec(memory_space=pltpu.VMEM)] * len(shapes),
        scratch_shapes=[pltpu.VMEM(shape, jnp.float32) for shape in scratch]
        + [pltpu.SemaphoreType.DMA((6,))] * (1 if far else 0),
        compiler_params=pltpu.CompilerParams(vmem_limit_bytes=LIMIT),
        cost_estimate=pl.CostEstimate(flops=flops, bytes_accessed=0, transcendentals=0),
    )(*flags, *near, *far)


def first_kernel(places, width, row, lead, rhs, far_lead, *refs):
    others, (solved, shuffled, lead_other, *held, sems) = (
        refs[: len(places) - 1],
        refs[len(places) - 1 :],
    )
    cands = rhs.shape[1]

    @pl.when(row[0] == 0)
    def _():
        copies = [
            pltpu.make_async_copy(other.at[:width], place, sems.at[at])
            for at, (other, place) in enumerate(zip(others, held))
        ]
        copies.append(
            pltpu.make_async_copy(
                far_lead.at[:, : 2 * width], lead_other, sems.at[len(copies)]
            )
        )
        for copy in copies:
            copy.start()
        for copy in copies:
            copy.wait()
        blocks = jnp.concatenate([rhs[:width]] + [place[...] for place in held], axis=1)
        inverse = jnp.concatenate([lead[:, :width], lead_other[:, :width]], axis=0)
        first = dot(inverse, blocks, 1)
        solved[...] = first
        middle = slice(width, 2 * width)
        corner = jnp.concatenate([lead[:, middle], lead_other[:, middle]], axis=0)
        total = dot(corner, first, 0)
        pieces = [total[:, at * cands : (at + 1) * cands] for at in range(len(places))]
        pieces[0] = pieces[0] - rhs[middle]
        for at, place in enumerate(places):
            shuffled[:, at * cands : (at + 1) * cands] = pieces[place]


def second_kernel(places, row, lead, far_lead, sent, got, first, bundle, *refs):
    inverse_other, sums, more, sems = refs
    width = sums.shape[0]
    cands = sums.shape[1] // len(places)

    last = slice(2 * width, 3 * width)

    @pl.when(row[0] == 0)
    def _():
        copies = [
            pltpu.make_async_copy(sent, sums, sems.at[0]),
            pltpu.make_async_copy(got, more, sems.at[1]),
            pltpu.make_async_copy(far_lead.at[:, last], inverse_other, sems.at[2]),
        ]
        for copy in copies:
            copy.start()
        for copy in copies:
            copy.wait()
        both = jnp.concatenate([lead[:, last], inverse_other[...]], axis=0)
        rest = [sums[:, place * cands : (place + 1) * cands] for place in places]
        second = dot(both, -(jnp.concatenate(rest, axis=1) + more[...]), 1)
        bundle[...] = second

    @pl.when(row[0] == 1)
    def _():
        copy = pltpu.make_async_copy(first, bundle, sems.at[3])
        copy.start()
        copy.wait()


def rows_kernel(row, held, got, flat, whole, early, beside, tail, cross, own, send, *refs):
    mine, other, base, sems = refs
    n_design, cands = base.shape
    depth = held.shape[0] // 2
    parts = [slice(at * n_design // 2, (at + 1) * n_design // 2) for at in range(2)]
    is_odd = row[0] % 2 == 1

    def fetch(at, source):
        return pltpu.make_async_copy(source, other.at[:, parts[at]], sems.at[at])

    @pl.when(row[0] > 0)
    def _():
        copies = []
        for at, part in enumerate(parts):
            copies.append(
                [
                    pltpu.make_async_copy(flat.at[:, part], mine.at[:, part], sems.at[2 + at]),
                    pltpu.make_async_copy(cross.at[part], base.at[part], sems.at[4 + at]),
                ]
            )
        sources = [
            (row[0] == 1, [beside.at[:, part] for part in parts]),
            ((row[0] > 1) & ~is_odd, [early, tail]),
            ((row[0] > 1) & is_odd, [whole.at[:, part] for part in parts]),
        ]
        for at in range(2):
            for chosen, pieces in sources:
                pl.when(chosen)(lambda at=at, pieces=pieces: fetch(at, pieces[at]).start())
            for copy in copies[at]:
                copy.start()
        has_first = (row[0] == 1) | ((row[0] > 1) & ~is_odd)
        first = jnp.where(has_first, held[...], got[...])
        second = jnp.where(has_first, got[...], held[...])
        solved = jnp.concatenate(
            [first[:depth], second[:depth], first[depth:], second[depth:]], axis=0
        )
        for at, part in enumerate(parts):
            fetch(at, whole.at[:, part]).wait()
            for copy in copies[at]:
                copy.wait()
            factors = jnp.concatenate([mine[:, part], other[:, part]], axis=0)
            partial = dot(solved, factors, 0)
            own[part] = base[part] - partial[:cands].T
            send[part] = partial[cands:].T


def top_kernel(offsets, col, pair, *refs):
    others, out = refs[:-1], refs[-1]
    cands = out.shape[1]
    depth = pair.shape[0] // 4
    n_cols = len(offsets)
    sources = [pair[:, :cands]] + [other[...] for other in others]
    for panel in range(2):
        pieces = []
        for source in sources:
            for at in (2 * panel, 2 * panel + 1):
                pieces.append(source[at * depth : (at + 1) * depth])
        pieces = [pieces[offsets.index(at)] for at in range(n_cols)]
        bit = 1
        while bit < n_cols:
            flipped = (col[0] & bit) != 0
            pieces = [jnp.where(flipped, pieces[at ^ bit], pieces[at]) for at in range(n_cols)]
            bit *= 2
        for at, piece in enumerate(pieces):
            place = (panel * n_cols + at) * depth
            out[place : place + depth] = piece


def make_on_device(n_rows, n_cols):
    half = n_cols // 2

    def swap(array, flip, rows):
        pairs = [
            (row * n_cols + col, row * n_cols + (col ^ flip))
            for row in rows
            for col in range(n_cols)
        ]
        return lax.ppermute(array, AXES, pairs)

    def send_down(array, offset, have):
        pairs = [
            (row * n_cols + col, target(row, offset) * n_cols + col)
            for row in have
            for col in range(n_cols)
        ]
        return lax.ppermute(array, AXES, pairs)

    def target(row, offset):
        return (row + offset) ^ (1 if row < 2 and offset > 1 else 0)

    def spread(array, row_id, low, radix, have):
        digit = (row_id // low) % radix
        result = array
        for step in (2, 1, 3) if radix == 4 else range(1, radix):
            result = jnp.where(digit == step, send_down(array, step * low, have), result)
        return result, [target(row, step * low) for row in have for step in range(radix)]

    def broadcast_outer(array, row_id):
        low = n_rows
        have = [0, 1]
        while low > 2:
            radix = min(4, low // 2)
            low //= radix
            array, have = spread(array, row_id, low, radix, have)
        return array

    def swap_cores(array):
        pairs = [
            (row * n_cols + col, (row ^ 1) * n_cols + col)
            for row in range(n_rows)
            for col in range(n_cols)
        ]
        return lax.ppermute(array, AXES, pairs)

    def block(array, place, cands):
        return array[:, place * cands : (place + 1) * cands]

    def shuffle(array, flip, cands):
        return jnp.concatenate([block(array, at ^ flip, cands) for at in range(half)], axis=1)

    def on_device(cross_kernel, factor_panels, block_inverses):
        row_id = lax.axis_index("rows")
        col_id = lax.axis_index("cols")
        width = block_inverses.shape[2]
        depth = block_inverses.shape[1]
        n_design, cands = cross_kernel.shape
        count = n_design // 2
        top = [0]
        beside = [1]
        evens, odds = range(2, n_rows, 2), range(3, n_rows, 2)
        flat = factor_panels.reshape(2 * depth, n_design)

        lead = jnp.concatenate(
            [block_inverses[0], factor_panels[0, :, width : 2 * width], block_inverses[1]], axis=1
        )
        lead, rhs = lax.optimization_barrier((lead, cross_kernel))
        lead_other = swap(lead, half, top)
        rhs_others = [swap(rhs, step, top) for step in range(1, half)]
        whole = swap(flat, half, odds)
        arrived = swap(flat[:, :count], half, evens)
        lead_other, tail = lax.optimization_barrier((lead_other, flat[:, count:]))

        places = [at ^ 1 for at in range(half)]
        first, shuffled = call(
            functools.partial(first_kernel, places, width),
            [(2 * depth, half * cands), (width, half * cands)],
            6 * width * half * cands * (2 * depth + 2 * depth),
            [lead, rhs],
            [lead_other, *rhs_others],
            row_id,
            [(depth, 2 * width)] + [(width, cands)] * len(rhs_others),
        )
        shuffled, arrived, whole = lax.optimization_barrier((shuffled, arrived, whole))
        sums = got = swap(shuffled, 1, top)
        bit = 2
        while bit < half:
            update = shuffle(shuffled, 1, cands) + sums
            got = swap(shuffle(update, bit, cands), bit, top)
            sums = sums + got
            bit *= 2
        first_beside = send_down(first, 1, top)
        (bundle,) = call(
            functools.partial(second_kernel, places),
            [(2 * depth, half * cands)],
            6 * 2 * depth * width * half * cands,
            [lead],
            [lead_other, shuffled, sums, first_beside],
            row_id,
            [(depth, width)] + [(width, half * cands)] * 2,
        )
        first_beside, late = lax.optimization_barrier((first_beside, flat))
        late = swap(late, half, beside)
        held = broadcast_outer(bundle, row_id)
        tail = swap(tail, half, evens)
        solved = [held, swap_cores(held)]

        pair = jnp.concatenate([first, held], axis=0)
        others = [swap(block(pair, step, cands), step, top) for step in range(1, half)]
        offsets = [at for step in range(half) for at in (step, step ^ half)]
        (top_rows,) = call(
            functools.partial(top_kernel, offsets),
            [(2 * width, cands)],
            0,
            [pair, *others],
            flag=col_id,
        )

        fresh, send = call(
            rows_kernel,
            [(n_design, cands), (n_design, (half - 1) * cands)],
            6 * n_design * 4 * depth * half * cands,
            solved,
            [flat, whole, arrived, late, tail, cross_kernel],
            row_id,
            [(2 * depth, n_design)] * 2 + [(n_design, cands)],
        )
        for step in range(1, half):
            fresh = fresh - swap(block(send, step - 1, cands), step, range(1, n_rows))
        return jnp.where(row_id == 0, top_rows, fresh)

    return on_device


def solution(mesh):
    in_specs = (P("rows", "cols"), P(None, "cols", "rows"), P(None, "cols", None))
    out_specs = P("rows", "cols")
    return jax.shard_map(
        make_on_device(mesh.shape["rows"], mesh.shape["cols"]),
        mesh=mesh,
        in_specs=in_specs,
        out_specs=out_specs,
        check_vma=False,
    )
```

```python
import functools
import jax
import jax.numpy as jnp
from jax import lax
from jax.experimental import pallas as pl
from jax.experimental.pallas import tpu as pltpu
from jax.sharding import PartitionSpec as P

AXES = ("rows", "cols")
LIMIT = 12 * 1024 * 1024


def split(array):
    high = array.astype(jnp.bfloat16)
    return high, (array - high.astype(jnp.float32)).astype(jnp.bfloat16)


def dot(left, right, left_dim):
    def one(a, b):
        return lax.dot_general(
            a, b, (((left_dim,), (0,)), ((), ())), preferred_element_type=jnp.float32
        )

    left_high, left_low = split(left)
    right_high, right_low = split(right)
    return one(left_high, right_high) + (one(left_high, right_low) + one(left_low, right_high))


def call(kernel, shapes, flops, near, far=(), flag=None, scratch=()):
    flags = [] if flag is None else [flag.astype(jnp.int32).reshape(1)]
    spaces = [pltpu.SMEM] * len(flags) + [pltpu.VMEM] * len(near) + [pltpu.HBM] * len(far)
    return pl.pallas_call(
        kernel,
        out_shape=[jax.ShapeDtypeStruct(shape, jnp.float32) for shape in shapes],
        in_specs=[pl.BlockSpec(memory_space=space) for space in spaces],
        out_specs=[pl.BlockSpec(memory_space=pltpu.VMEM)] * len(shapes),
        scratch_shapes=[pltpu.VMEM(shape, jnp.float32) for shape in scratch]
        + [pltpu.SemaphoreType.DMA((6,))] * (1 if far else 0),
        compiler_params=pltpu.CompilerParams(vmem_limit_bytes=LIMIT),
        cost_estimate=pl.CostEstimate(flops=flops, bytes_accessed=0, transcendentals=0),
    )(*flags, *near, *far)


def first_kernel(places, width, row, lead, rhs, far_lead, *refs):
    others, (solved, shuffled, lead_other, *held, sems) = (
        refs[: len(places) - 1],
        refs[len(places) - 1 :],
    )
    cands = rhs.shape[1]

    @pl.when(row[0] == 0)
    def _():
        copies = [
            pltpu.make_async_copy(other.at[:width], place, sems.at[at])
            for at, (other, place) in enumerate(zip(others, held))
        ]
        copies.append(
            pltpu.make_async_copy(
                far_lead.at[:, : 2 * width], lead_other, sems.at[len(copies)]
            )
        )
        for copy in copies:
            copy.start()
        for copy in copies:
            copy.wait()
        blocks = jnp.concatenate([rhs[:width]] + [place[...] for place in held], axis=1)
        inverse = jnp.concatenate([lead[:, :width], lead_other[:, :width]], axis=0)
        first = dot(inverse, blocks, 1)
        solved[...] = first
        middle = slice(width, 2 * width)
        corner = jnp.concatenate([lead[:, middle], lead_other[:, middle]], axis=0)
        total = dot(corner, first, 0)
        pieces = [total[:, at * cands : (at + 1) * cands] for at in range(len(places))]
        pieces[0] = pieces[0] - rhs[middle]
        for at, place in enumerate(places):
            shuffled[:, at * cands : (at + 1) * cands] = pieces[place]


def second_kernel(places, row, lead, far_lead, sent, got, first, bundle, *refs):
    inverse_other, sums, more, sems = refs
    width = sums.shape[0]
    cands = sums.shape[1] // len(places)

    last = slice(2 * width, 3 * width)

    @pl.when(row[0] == 0)
    def _():
        copies = [
            pltpu.make_async_copy(sent, sums, sems.at[0]),
            pltpu.make_async_copy(got, more, sems.at[1]),
            pltpu.make_async_copy(far_lead.at[:, last], inverse_other, sems.at[2]),
        ]
        for copy in copies:
            copy.start()
        for copy in copies:
            copy.wait()
        both = jnp.concatenate([lead[:, last], inverse_other[...]], axis=0)
        rest = [sums[:, place * cands : (place + 1) * cands] for place in places]
        second = dot(both, -(jnp.concatenate(rest, axis=1) + more[...]), 1)
        bundle[...] = second

    @pl.when(row[0] == 1)
    def _():
        copy = pltpu.make_async_copy(first, bundle, sems.at[3])
        copy.start()
        copy.wait()


def rows_kernel(row, held, got, flat, whole, early, beside, tail, cross, own, send, *refs):
    mine, other, base, sems = refs
    n_design, cands = base.shape
    depth = held.shape[0] // 2
    parts = [slice(at * n_design // 2, (at + 1) * n_design // 2) for at in range(2)]
    is_odd = row[0] % 2 == 1

    def fetch(at, source):
        return pltpu.make_async_copy(source, other.at[:, parts[at]], sems.at[at])

    @pl.when(row[0] > 0)
    def _():
        copies = []
        for at, part in enumerate(parts):
            copies.append(
                [
                    pltpu.make_async_copy(flat.at[:, part], mine.at[:, part], sems.at[2 + at]),
                    pltpu.make_async_copy(cross.at[part], base.at[part], sems.at[4 + at]),
                ]
            )
        sources = [
            (row[0] == 1, [beside, tail]),
            ((row[0] > 1) & ~is_odd, [early, tail]),
            ((row[0] > 1) & is_odd, [whole.at[:, part] for part in parts]),
        ]
        for at in range(2):
            for chosen, pieces in sources:
                pl.when(chosen)(lambda at=at, pieces=pieces: fetch(at, pieces[at]).start())
            for copy in copies[at]:
                copy.start()
        has_first = (row[0] == 1) | ((row[0] > 1) & ~is_odd)
        first = jnp.where(has_first, held[...], got[...])
        second = jnp.where(has_first, got[...], held[...])
        solved = jnp.concatenate(
            [first[:depth], second[:depth], first[depth:], second[depth:]], axis=0
        )
        for at, part in enumerate(parts):
            fetch(at, whole.at[:, part]).wait()
            for copy in copies[at]:
                copy.wait()
            factors = jnp.concatenate([mine[:, part], other[:, part]], axis=0)
            partial = dot(solved, factors, 0)
            own[part] = base[part] - partial[:cands].T
            send[part] = partial[cands:].T


def top_kernel(offsets, col, pair, *refs):
    others, out = refs[:-1], refs[-1]
    cands = out.shape[1]
    depth = pair.shape[0] // 4
    n_cols = len(offsets)
    sources = [pair[:, :cands]] + [other[...] for other in others]
    for panel in range(2):
        pieces = []
        for source in sources:
            for at in (2 * panel, 2 * panel + 1):
                pieces.append(source[at * depth : (at + 1) * depth])
        pieces = [pieces[offsets.index(at)] for at in range(n_cols)]
        bit = 1
        while bit < n_cols:
            flipped = (col[0] & bit) != 0
            pieces = [jnp.where(flipped, pieces[at ^ bit], pieces[at]) for at in range(n_cols)]
            bit *= 2
        for at, piece in enumerate(pieces):
            place = (panel * n_cols + at) * depth
            out[place : place + depth] = piece


def make_on_device(n_rows, n_cols):
    half = n_cols // 2

    def swap(array, flip, rows):
        pairs = [
            (row * n_cols + col, row * n_cols + (col ^ flip))
            for row in rows
            for col in range(n_cols)
        ]
        return lax.ppermute(array, AXES, pairs)

    def send_down(array, offset, have):
        pairs = [
            (row * n_cols + col, target(row, offset) * n_cols + col)
            for row in have
            for col in range(n_cols)
        ]
        return lax.ppermute(array, AXES, pairs)

    def target(row, offset):
        return (row + offset) ^ (1 if row < 2 and offset > 1 else 0)

    def spread(array, row_id, low, radix, have):
        digit = (row_id // low) % radix
        result = array
        for step in (2, 1, 3) if radix == 4 else range(1, radix):
            result = jnp.where(digit == step, send_down(array, step * low, have), result)
        return result, [target(row, step * low) for row in have for step in range(radix)]

    def broadcast_outer(array, row_id):
        low = n_rows
        have = [0, 1]
        while low > 2:
            radix = min(4, low // 2)
            low //= radix
            array, have = spread(array, row_id, low, radix, have)
        return array

    def swap_cores(array):
        pairs = [
            (row * n_cols + col, (row ^ 1) * n_cols + col)
            for row in range(n_rows)
            for col in range(n_cols)
        ]
        return lax.ppermute(array, AXES, pairs)

    def block(array, place, cands):
        return array[:, place * cands : (place + 1) * cands]

    def shuffle(array, flip, cands):
        return jnp.concatenate([block(array, at ^ flip, cands) for at in range(half)], axis=1)

    def on_device(cross_kernel, factor_panels, block_inverses):
        row_id = lax.axis_index("rows")
        col_id = lax.axis_index("cols")
        width = block_inverses.shape[2]
        depth = block_inverses.shape[1]
        n_design, cands = cross_kernel.shape
        count = n_design // 2
        top = [0]
        beside = [1]
        evens, odds = range(2, n_rows, 2), range(3, n_rows, 2)
        flat = factor_panels.reshape(2 * depth, n_design)

        lead = jnp.concatenate(
            [block_inverses[0], factor_panels[0, :, width : 2 * width], block_inverses[1]], axis=1
        )
        lead, rhs = lax.optimization_barrier((lead, cross_kernel))
        lead_other = swap(lead, half, top)
        rhs_others = [swap(rhs, step, top) for step in range(1, half)]
        whole = swap(flat, half, odds)
        arrived = swap(flat[:, :count], half, evens)
        lead_other, head, tail = lax.optimization_barrier(
            (lead_other, flat[:, : n_design // 2], flat[:, count:])
        )

        places = [at ^ 1 for at in range(half)]
        first, shuffled = call(
            functools.partial(first_kernel, places, width),
            [(2 * depth, half * cands), (width, half * cands)],
            6 * width * half * cands * (2 * depth + 2 * depth),
            [lead, rhs],
            [lead_other, *rhs_others],
            row_id,
            [(depth, 2 * width)] + [(width, cands)] * len(rhs_others),
        )
        shuffled, arrived, whole = lax.optimization_barrier((shuffled, arrived, whole))
        sums = got = swap(shuffled, 1, top)
        bit = 2
        while bit < half:
            update = shuffle(shuffled, 1, cands) + sums
            got = swap(shuffle(update, bit, cands), bit, top)
            sums = sums + got
            bit *= 2
        first_beside = send_down(first, 1, top)
        (bundle,) = call(
            functools.partial(second_kernel, places),
            [(2 * depth, half * cands)],
            6 * 2 * depth * width * half * cands,
            [lead],
            [lead_other, shuffled, sums, first_beside],
            row_id,
            [(depth, width)] + [(width, half * cands)] * 2,
        )
        first_beside, head = lax.optimization_barrier((first_beside, head))
        late = swap(head, half, beside)
        held = broadcast_outer(bundle, row_id)
        held, late = lax.optimization_barrier((held, late))
        tail = swap(tail, half, [*beside, *evens])
        solved = [held, swap_cores(held)]

        pair = jnp.concatenate([first, held], axis=0)
        others = [swap(block(pair, step, cands), step, top) for step in range(1, half)]
        offsets = [at for step in range(half) for at in (step, step ^ half)]
        (top_rows,) = call(
            functools.partial(top_kernel, offsets),
            [(2 * width, cands)],
            0,
            [pair, *others],
            flag=col_id,
        )

        fresh, send = call(
            rows_kernel,
            [(n_design, cands), (n_design, (half - 1) * cands)],
            6 * n_design * 4 * depth * half * cands,
            solved,
            [flat, whole, arrived, late, tail, cross_kernel],
            row_id,
            [(2 * depth, n_design)] * 2 + [(n_design, cands)],
        )
        for step in range(1, half):
            fresh = fresh - swap(block(send, step - 1, cands), step, range(1, n_rows))
        return jnp.where(row_id == 0, top_rows, fresh)

    return on_device


def solution(mesh):
    in_specs = (P("rows", "cols"), P(None, "cols", "rows"), P(None, "cols", None))
    out_specs = P("rows", "cols")
    return jax.shard_map(
        make_on_device(mesh.shape["rows"], mesh.shape["cols"]),
        mesh=mesh,
        in_specs=in_specs,
        out_specs=out_specs,
        check_vma=False,
    )
```

```python
import functools
import jax
import jax.numpy as jnp
from jax import lax
from jax.experimental import pallas as pl
from jax.experimental.pallas import tpu as pltpu
from jax.sharding import PartitionSpec as P

AXES = ("rows", "cols")
LIMIT = 12 * 1024 * 1024


def split(array):
    high = array.astype(jnp.bfloat16)
    return high, (array - high.astype(jnp.float32)).astype(jnp.bfloat16)


def dot(left, right, left_dim):
    def one(a, b):
        return lax.dot_general(
            a, b, (((left_dim,), (0,)), ((), ())), preferred_element_type=jnp.float32
        )

    left_high, left_low = split(left)
    right_high, right_low = split(right)
    return one(left_high, right_high) + (one(left_high, right_low) + one(left_low, right_high))


def call(kernel, shapes, flops, near, far=(), flag=None, scratch=()):
    flags = [] if flag is None else [flag.astype(jnp.int32).reshape(1)]
    spaces = [pltpu.SMEM] * len(flags) + [pltpu.VMEM] * len(near) + [pltpu.HBM] * len(far)
    return pl.pallas_call(
        kernel,
        out_shape=[jax.ShapeDtypeStruct(shape, jnp.float32) for shape in shapes],
        in_specs=[pl.BlockSpec(memory_space=space) for space in spaces],
        out_specs=[pl.BlockSpec(memory_space=pltpu.VMEM)] * len(shapes),
        scratch_shapes=[pltpu.VMEM(shape, jnp.float32) for shape in scratch]
        + [pltpu.SemaphoreType.DMA((6,))] * (1 if far else 0),
        compiler_params=pltpu.CompilerParams(vmem_limit_bytes=LIMIT),
        cost_estimate=pl.CostEstimate(flops=flops, bytes_accessed=0, transcendentals=0),
    )(*flags, *near, *far)


def first_kernel(places, width, row, lead, rhs, far_lead, *refs):
    others, (solved, shuffled, lead_other, *held, sems) = (
        refs[: len(places) - 1],
        refs[len(places) - 1 :],
    )
    cands = rhs.shape[1]

    @pl.when(row[0] == 0)
    def _():
        copies = [
            pltpu.make_async_copy(other.at[:width], place, sems.at[at])
            for at, (other, place) in enumerate(zip(others, held))
        ]
        copies.append(
            pltpu.make_async_copy(
                far_lead.at[:, : 2 * width], lead_other, sems.at[len(copies)]
            )
        )
        for copy in copies:
            copy.start()
        for copy in copies:
            copy.wait()
        blocks = jnp.concatenate([rhs[:width]] + [place[...] for place in held], axis=1)
        inverse = jnp.concatenate([lead[:, :width], lead_other[:, :width]], axis=0)
        first = dot(inverse, blocks, 1)
        solved[...] = first
        middle = slice(width, 2 * width)
        corner = jnp.concatenate([lead[:, middle], lead_other[:, middle]], axis=0)
        total = dot(corner, first, 0)
        pieces = [total[:, at * cands : (at + 1) * cands] for at in range(len(places))]
        pieces[0] = pieces[0] - rhs[middle]
        for at, place in enumerate(places):
            shuffled[:, at * cands : (at + 1) * cands] = pieces[place]


def second_kernel(places, row, lead, far_lead, sent, got, first, bundle, *refs):
    inverse_other, sums, more, sems = refs
    width = sums.shape[0]
    cands = sums.shape[1] // len(places)

    last = slice(2 * width, 3 * width)

    @pl.when(row[0] == 0)
    def _():
        copies = [
            pltpu.make_async_copy(sent, sums, sems.at[0]),
            pltpu.make_async_copy(got, more, sems.at[1]),
            pltpu.make_async_copy(far_lead.at[:, last], inverse_other, sems.at[2]),
        ]
        for copy in copies:
            copy.start()
        for copy in copies:
            copy.wait()
        both = jnp.concatenate([lead[:, last], inverse_other[...]], axis=0)
        rest = [sums[:, place * cands : (place + 1) * cands] for place in places]
        second = dot(both, -(jnp.concatenate(rest, axis=1) + more[...]), 1)
        bundle[...] = second

    @pl.when(row[0] == 1)
    def _():
        copy = pltpu.make_async_copy(first, bundle, sems.at[3])
        copy.start()
        copy.wait()


def rows_kernel(row, held, got, flat, whole, early, beside, tail, cross, own, send, *refs):
    mine, other, base, sems = refs
    n_design, cands = base.shape
    depth = held.shape[0] // 2
    parts = [slice(at * n_design // 2, (at + 1) * n_design // 2) for at in range(2)]
    is_odd = row[0] % 2 == 1

    def fetch(at, source):
        return pltpu.make_async_copy(source, other.at[:, parts[at]], sems.at[at])

    @pl.when(row[0] > 0)
    def _():
        copies = []
        for at, part in enumerate(parts):
            copies.append(
                [
                    pltpu.make_async_copy(flat.at[:, part], mine.at[:, part], sems.at[2 + at]),
                    pltpu.make_async_copy(cross.at[part], base.at[part], sems.at[4 + at]),
                ]
            )
        sources = [
            (row[0] == 1, [beside.at[:, part] for part in parts]),
            ((row[0] > 1) & ~is_odd, [early, tail]),
            ((row[0] > 1) & is_odd, [whole.at[:, part] for part in parts]),
        ]
        for at in range(2):
            for chosen, pieces in sources:
                pl.when(chosen)(lambda at=at, pieces=pieces: fetch(at, pieces[at]).start())
            for copy in copies[at]:
                copy.start()
        has_first = (row[0] == 1) | ((row[0] > 1) & ~is_odd)
        first = jnp.where(has_first, held[...], got[...])
        second = jnp.where(has_first, got[...], held[...])
        solved = jnp.concatenate(
            [first[:depth], second[:depth], first[depth:], second[depth:]], axis=0
        )
        for at, part in enumerate(parts):
            fetch(at, whole.at[:, part]).wait()
            for copy in copies[at]:
                copy.wait()
            factors = jnp.concatenate([mine[:, part], other[:, part]], axis=0)
            partial = dot(solved, factors, 0)
            own[part] = base[part] - partial[:cands].T
            send[part] = partial[cands:].T


def top_kernel(offsets, col, pair, *refs):
    others, out = refs[:-1], refs[-1]
    cands = out.shape[1]
    depth = pair.shape[0] // 4
    n_cols = len(offsets)
    sources = [pair[:, :cands]] + [other[...] for other in others]
    for panel in range(2):
        pieces = []
        for source in sources:
            for at in (2 * panel, 2 * panel + 1):
                pieces.append(source[at * depth : (at + 1) * depth])
        pieces = [pieces[offsets.index(at)] for at in range(n_cols)]
        bit = 1
        while bit < n_cols:
            flipped = (col[0] & bit) != 0
            pieces = [jnp.where(flipped, pieces[at ^ bit], pieces[at]) for at in range(n_cols)]
            bit *= 2
        for at, piece in enumerate(pieces):
            place = (panel * n_cols + at) * depth
            out[place : place + depth] = piece


def make_on_device(n_rows, n_cols):
    half = n_cols // 2

    def swap(array, flip, rows):
        pairs = [
            (row * n_cols + col, row * n_cols + (col ^ flip))
            for row in rows
            for col in range(n_cols)
        ]
        return lax.ppermute(array, AXES, pairs)

    def send_down(array, offset, have):
        pairs = [
            (row * n_cols + col, target(row, offset) * n_cols + col)
            for row in have
            for col in range(n_cols)
        ]
        return lax.ppermute(array, AXES, pairs)

    def target(row, offset):
        return (row + offset) ^ (1 if row < 2 and offset > 1 else 0)

    def spread(array, row_id, low, radix, have):
        digit = (row_id // low) % radix
        result = array
        for step in (2, 1, 3) if radix == 4 else range(1, radix):
            result = jnp.where(digit == step, send_down(array, step * low, have), result)
        return result, [target(row, step * low) for row in have for step in range(radix)]

    def broadcast_outer(array, row_id):
        low = n_rows
        have = [0, 1]
        while low > 2:
            radix = min(4, low // 2)
            low //= radix
            array, have = spread(array, row_id, low, radix, have)
        return array

    def swap_cores(array):
        pairs = [
            (row * n_cols + col, (row ^ 1) * n_cols + col)
            for row in range(n_rows)
            for col in range(n_cols)
        ]
        return lax.ppermute(array, AXES, pairs)

    def block(array, place, cands):
        return array[:, place * cands : (place + 1) * cands]

    def shuffle(array, flip, cands):
        return jnp.concatenate([block(array, at ^ flip, cands) for at in range(half)], axis=1)

    def on_device(cross_kernel, factor_panels, block_inverses):
        row_id = lax.axis_index("rows")
        col_id = lax.axis_index("cols")
        width = block_inverses.shape[2]
        depth = block_inverses.shape[1]
        n_design, cands = cross_kernel.shape
        count = n_design // 2
        top = [0]
        beside = [1]
        evens, odds = range(2, n_rows, 2), range(3, n_rows, 2)
        flat = factor_panels.reshape(2 * depth, n_design)

        lead = jnp.concatenate(
            [block_inverses[0], factor_panels[0, :, width : 2 * width], block_inverses[1]], axis=1
        )
        lead, rhs = lax.optimization_barrier((lead, cross_kernel))
        lead_other = swap(lead, half, top)
        rhs_others = [swap(rhs, step, top) for step in range(1, half)]
        whole = swap(flat, half, odds)
        arrived = swap(flat[:, :count], half, evens)
        lead_other, tail = lax.optimization_barrier((lead_other, flat[:, count:]))

        places = [at ^ 1 for at in range(half)]
        first, shuffled = call(
            functools.partial(first_kernel, places, width),
            [(2 * depth, half * cands), (width, half * cands)],
            6 * width * half * cands * (2 * depth + 2 * depth),
            [lead, rhs],
            [lead_other, *rhs_others],
            row_id,
            [(depth, 2 * width)] + [(width, cands)] * len(rhs_others),
        )
        shuffled, first, arrived, whole = lax.optimization_barrier(
            (shuffled, first, arrived, whole)
        )
        sums = got = swap(shuffled, 1, top)
        bit = 2
        while bit < half:
            update = shuffle(shuffled, 1, cands) + sums
            got = swap(shuffle(update, bit, cands), bit, top)
            sums = sums + got
            bit *= 2
        first_beside = send_down(first, 1, top)
        (bundle,) = call(
            functools.partial(second_kernel, places),
            [(2 * depth, half * cands)],
            6 * 2 * depth * width * half * cands,
            [lead],
            [lead_other, shuffled, sums, first_beside],
            row_id,
            [(depth, width)] + [(width, half * cands)] * 2,
        )
        first_beside, late = lax.optimization_barrier((first_beside, flat))
        late = swap(late, half, beside)
        held = broadcast_outer(bundle, row_id)
        held, late = lax.optimization_barrier((held, late))
        tail = swap(tail, half, evens)
        solved = [held, swap_cores(held)]

        pair = jnp.concatenate([first, held], axis=0)
        others = [swap(block(pair, step, cands), step, top) for step in range(1, half)]
        offsets = [at for step in range(half) for at in (step, step ^ half)]
        (top_rows,) = call(
            functools.partial(top_kernel, offsets),
            [(2 * width, cands)],
            0,
            [pair, *others],
            flag=col_id,
        )

        fresh, send = call(
            rows_kernel,
            [(n_design, cands), (n_design, (half - 1) * cands)],
            6 * n_design * 4 * depth * half * cands,
            solved,
            [flat, whole, arrived, late, tail, cross_kernel],
            row_id,
            [(2 * depth, n_design)] * 2 + [(n_design, cands)],
        )
        for step in range(1, half):
            fresh = fresh - swap(block(send, step - 1, cands), step, range(1, n_rows))
        return jnp.where(row_id == 0, top_rows, fresh)

    return on_device


def solution(mesh):
    in_specs = (P("rows", "cols"), P(None, "cols", "rows"), P(None, "cols", None))
    out_specs = P("rows", "cols")
    return jax.shard_map(
        make_on_device(mesh.shape["rows"], mesh.shape["cols"]),
        mesh=mesh,
        in_specs=in_specs,
        out_specs=out_specs,
        check_vma=False,
    )
```

```python
import functools
import jax
import jax.numpy as jnp
from jax import lax
from jax.experimental import pallas as pl
from jax.experimental.pallas import tpu as pltpu
from jax.sharding import PartitionSpec as P

AXES = ("rows", "cols")
CUT = 5
LIMIT = 12 * 1024 * 1024


def split(array):
    high = array.astype(jnp.bfloat16)
    return high, (array - high.astype(jnp.float32)).astype(jnp.bfloat16)


def dot(left, right, left_dim):
    def one(a, b):
        return lax.dot_general(
            a, b, (((left_dim,), (0,)), ((), ())), preferred_element_type=jnp.float32
        )

    left_high, left_low = split(left)
    right_high, right_low = split(right)
    return one(left_high, right_high) + (one(left_high, right_low) + one(left_low, right_high))


def call(kernel, shapes, flops, near, far=(), flag=None, scratch=()):
    flags = [] if flag is None else [flag.astype(jnp.int32).reshape(1)]
    spaces = [pltpu.SMEM] * len(flags) + [pltpu.VMEM] * len(near) + [pltpu.HBM] * len(far)
    return pl.pallas_call(
        kernel,
        out_shape=[jax.ShapeDtypeStruct(shape, jnp.float32) for shape in shapes],
        in_specs=[pl.BlockSpec(memory_space=space) for space in spaces],
        out_specs=[pl.BlockSpec(memory_space=pltpu.VMEM)] * len(shapes),
        scratch_shapes=[pltpu.VMEM(shape, jnp.float32) for shape in scratch]
        + [pltpu.SemaphoreType.DMA((6,))] * (1 if far else 0),
        compiler_params=pltpu.CompilerParams(vmem_limit_bytes=LIMIT),
        cost_estimate=pl.CostEstimate(flops=flops, bytes_accessed=0, transcendentals=0),
    )(*flags, *near, *far)


def first_kernel(places, width, row, lead, rhs, far_lead, *refs):
    others, (solved, shuffled, lead_other, *held, sems) = (
        refs[: len(places) - 1],
        refs[len(places) - 1 :],
    )
    cands = rhs.shape[1]

    @pl.when(row[0] == 0)
    def _():
        copies = [
            pltpu.make_async_copy(other.at[:width], place, sems.at[at])
            for at, (other, place) in enumerate(zip(others, held))
        ]
        copies.append(
            pltpu.make_async_copy(
                far_lead.at[:, : 2 * width], lead_other, sems.at[len(copies)]
            )
        )
        for copy in copies:
            copy.start()
        for copy in copies:
            copy.wait()
        blocks = jnp.concatenate([rhs[:width]] + [place[...] for place in held], axis=1)
        inverse = jnp.concatenate([lead[:, :width], lead_other[:, :width]], axis=0)
        first = dot(inverse, blocks, 1)
        solved[...] = first
        middle = slice(width, 2 * width)
        corner = jnp.concatenate([lead[:, middle], lead_other[:, middle]], axis=0)
        total = dot(corner, first, 0)
        pieces = [total[:, at * cands : (at + 1) * cands] for at in range(len(places))]
        pieces[0] = pieces[0] - rhs[middle]
        for at, place in enumerate(places):
            shuffled[:, at * cands : (at + 1) * cands] = pieces[place]


def second_kernel(places, row, lead, far_lead, sent, got, first, bundle, *refs):
    inverse_other, sums, more, sems = refs
    width = sums.shape[0]
    cands = sums.shape[1] // len(places)

    last = slice(2 * width, 3 * width)

    @pl.when(row[0] == 0)
    def _():
        copies = [
            pltpu.make_async_copy(sent, sums, sems.at[0]),
            pltpu.make_async_copy(got, more, sems.at[1]),
            pltpu.make_async_copy(far_lead.at[:, last], inverse_other, sems.at[2]),
        ]
        for copy in copies:
            copy.start()
        for copy in copies:
            copy.wait()
        both = jnp.concatenate([lead[:, last], inverse_other[...]], axis=0)
        rest = [sums[:, place * cands : (place + 1) * cands] for place in places]
        second = dot(both, -(jnp.concatenate(rest, axis=1) + more[...]), 1)
        bundle[...] = second

    @pl.when(row[0] == 1)
    def _():
        copy = pltpu.make_async_copy(first, bundle, sems.at[3])
        copy.start()
        copy.wait()


def rows_kernel(rows, row, held, got, flat, whole, early, beside, tail, cross, own, send, *refs):
    mine, other, base, sems = refs
    cands = base.shape[1]
    depth = held.shape[0] // 2
    start, stop = rows
    middle = early.shape[1]
    is_odd = row[0] % 2 == 1

    def fetch(source, low, high):
        place = other.at[:, low - start : high - start]
        return pltpu.make_async_copy(source, place, sems.at[0])

    pieces = []
    if start < middle:
        low, high = start, min(stop, middle)
        pieces.append((early.at[:, low:high], low, high))
    if stop > middle:
        low, high = max(start, middle), stop
        pieces.append((tail.at[:, low - middle : high - middle], low, high))

    @pl.when(row[0] > 0)
    def _():
        part = slice(start, stop)
        arrivals = fetch(whole.at[:, part], start, stop)
        copies = [
            pltpu.make_async_copy(flat.at[:, part], mine, sems.at[1]),
            pltpu.make_async_copy(cross.at[part], base, sems.at[2]),
        ]
        pl.when((row[0] > 1) & is_odd)(arrivals.start)
        pl.when(row[0] == 1)(fetch(beside.at[:, part], start, stop).start)
        for piece in pieces:
            pl.when((row[0] > 1) & ~is_odd)(fetch(*piece).start)
        for copy in copies:
            copy.start()
        has_first = (row[0] == 1) | ((row[0] > 1) & ~is_odd)
        first = jnp.where(has_first, held[...], got[...])
        second = jnp.where(has_first, got[...], held[...])
        solved = jnp.concatenate(
            [first[:depth], second[:depth], first[depth:], second[depth:]], axis=0
        )
        for copy in [arrivals, *copies]:
            copy.wait()
        factors = jnp.concatenate([mine[...], other[...]], axis=0)
        partial = dot(solved, factors, 0)
        own[...] = base[...] - partial[:cands].T
        send[...] = partial[cands:].T


def top_kernel(offsets, col, pair, *refs):
    others, out = refs[:-1], refs[-1]
    cands = out.shape[1]
    depth = pair.shape[0] // 4
    n_cols = len(offsets)
    sources = [pair[:, :cands]] + [other[...] for other in others]
    for panel in range(2):
        pieces = []
        for source in sources:
            for at in (2 * panel, 2 * panel + 1):
                pieces.append(source[at * depth : (at + 1) * depth])
        pieces = [pieces[offsets.index(at)] for at in range(n_cols)]
        bit = 1
        while bit < n_cols:
            flipped = (col[0] & bit) != 0
            pieces = [jnp.where(flipped, pieces[at ^ bit], pieces[at]) for at in range(n_cols)]
            bit *= 2
        for at, piece in enumerate(pieces):
            place = (panel * n_cols + at) * depth
            out[place : place + depth] = piece


def make_on_device(n_rows, n_cols):
    half = n_cols // 2

    def swap(array, flip, rows):
        pairs = [
            (row * n_cols + col, row * n_cols + (col ^ flip))
            for row in rows
            for col in range(n_cols)
        ]
        return lax.ppermute(array, AXES, pairs)

    def send_down(array, offset, have):
        pairs = [
            (row * n_cols + col, target(row, offset) * n_cols + col)
            for row in have
            for col in range(n_cols)
        ]
        return lax.ppermute(array, AXES, pairs)

    def target(row, offset):
        return (row + offset) ^ (1 if row < 2 and offset > 1 else 0)

    def spread(array, row_id, low, radix, have):
        digit = (row_id // low) % radix
        result = array
        for step in (2, 1, 3) if radix == 4 else range(1, radix):
            result = jnp.where(digit == step, send_down(array, step * low, have), result)
        return result, [target(row, step * low) for row in have for step in range(radix)]

    def broadcast_outer(array, row_id):
        low = n_rows
        have = [0, 1]
        while low > 2:
            radix = min(4, low // 2)
            low //= radix
            array, have = spread(array, row_id, low, radix, have)
        return array

    def swap_cores(array):
        pairs = [
            (row * n_cols + col, (row ^ 1) * n_cols + col)
            for row in range(n_rows)
            for col in range(n_cols)
        ]
        return lax.ppermute(array, AXES, pairs)

    def block(array, place, cands):
        return array[:, place * cands : (place + 1) * cands]

    def shuffle(array, flip, cands):
        return jnp.concatenate([block(array, at ^ flip, cands) for at in range(half)], axis=1)

    def on_device(cross_kernel, factor_panels, block_inverses):
        row_id = lax.axis_index("rows")
        col_id = lax.axis_index("cols")
        width = block_inverses.shape[2]
        depth = block_inverses.shape[1]
        n_design, cands = cross_kernel.shape
        count = n_design // 2
        top = [0]
        beside = [1]
        evens, odds = range(2, n_rows, 2), range(3, n_rows, 2)
        flat = factor_panels.reshape(2 * depth, n_design)

        lead = jnp.concatenate(
            [block_inverses[0], factor_panels[0, :, width : 2 * width], block_inverses[1]], axis=1
        )
        lead, rhs = lax.optimization_barrier((lead, cross_kernel))
        lead_other = swap(lead, half, top)
        rhs_others = [swap(rhs, step, top) for step in range(1, half)]
        whole = swap(flat, half, odds)
        arrived = swap(flat[:, :count], half, evens)
        lead_other, tail = lax.optimization_barrier((lead_other, flat[:, count:]))

        places = [at ^ 1 for at in range(half)]
        first, shuffled = call(
            functools.partial(first_kernel, places, width),
            [(2 * depth, half * cands), (width, half * cands)],
            6 * width * half * cands * (2 * depth + 2 * depth),
            [lead, rhs],
            [lead_other, *rhs_others],
            row_id,
            [(depth, 2 * width)] + [(width, cands)] * len(rhs_others),
        )
        shuffled, first, arrived, whole = lax.optimization_barrier(
            (shuffled, first, arrived, whole)
        )
        sums = got = swap(shuffled, 1, top)
        bit = 2
        while bit < half:
            update = shuffle(shuffled, 1, cands) + sums
            got = swap(shuffle(update, bit, cands), bit, top)
            sums = sums + got
            bit *= 2
        first_beside = send_down(first, 1, top)
        (bundle,) = call(
            functools.partial(second_kernel, places),
            [(2 * depth, half * cands)],
            6 * 2 * depth * width * half * cands,
            [lead],
            [lead_other, shuffled, sums, first_beside],
            row_id,
            [(depth, width)] + [(width, half * cands)] * 2,
        )
        first_beside, late = lax.optimization_barrier((first_beside, flat))
        late = swap(late, half, beside)
        held = broadcast_outer(bundle, row_id)
        held, late = lax.optimization_barrier((held, late))
        tail = swap(tail, half, evens)
        solved = [held, swap_cores(held)]

        pair = jnp.concatenate([first, held], axis=0)
        others = [swap(block(pair, step, cands), step, top) for step in range(1, half)]
        offsets = [at for step in range(half) for at in (step, step ^ half)]
        (top_rows,) = call(
            functools.partial(top_kernel, offsets),
            [(2 * width, cands)],
            0,
            [pair, *others],
            flag=col_id,
        )

        fresh = []
        for rows in ((0, CUT * n_design // 8), (CUT * n_design // 8, n_design)):
            size = rows[1] - rows[0]
            own, send = call(
                functools.partial(rows_kernel, rows),
                [(size, cands), (size, (half - 1) * cands)],
                6 * size * 4 * depth * half * cands,
                solved,
                [flat, whole, arrived, late, tail, cross_kernel],
                row_id,
                [(2 * depth, size)] * 2 + [(size, cands)],
            )
            solved[0], send = lax.optimization_barrier((solved[0], send))
            for step in range(1, half):
                own = own - swap(block(send, step - 1, cands), step, range(1, n_rows))
            fresh.append(own)
        fresh = jnp.concatenate(fresh, axis=0)
        return jnp.where(row_id == 0, top_rows, fresh)

    return on_device


def solution(mesh):
    in_specs = (P("rows", "cols"), P(None, "cols", "rows"), P(None, "cols", None))
    out_specs = P("rows", "cols")
    return jax.shard_map(
        make_on_device(mesh.shape["rows"], mesh.shape["cols"]),
        mesh=mesh,
        in_specs=in_specs,
        out_specs=out_specs,
        check_vma=False,
    )
```

```python
import functools
import jax
import jax.numpy as jnp
from jax import lax
from jax.experimental import pallas as pl
from jax.experimental.pallas import tpu as pltpu
from jax.sharding import PartitionSpec as P

AXES = ("rows", "cols")
LIMIT = 12 * 1024 * 1024


def split(array):
    high = array.astype(jnp.bfloat16)
    return high, (array - high.astype(jnp.float32)).astype(jnp.bfloat16)


def dot(left, right, left_dim):
    def one(a, b):
        return lax.dot_general(
            a, b, (((left_dim,), (0,)), ((), ())), preferred_element_type=jnp.float32
        )

    left_high, left_low = split(left)
    right_high, right_low = split(right)
    return one(left_high, right_high) + (one(left_high, right_low) + one(left_low, right_high))


def call(kernel, shapes, flops, near, far=(), flag=None, scratch=()):
    flags = [] if flag is None else [flag.astype(jnp.int32).reshape(1)]
    spaces = [pltpu.SMEM] * len(flags) + [pltpu.VMEM] * len(near) + [pltpu.HBM] * len(far)
    return pl.pallas_call(
        kernel,
        out_shape=[jax.ShapeDtypeStruct(shape, jnp.float32) for shape in shapes],
        in_specs=[pl.BlockSpec(memory_space=space) for space in spaces],
        out_specs=[pl.BlockSpec(memory_space=pltpu.VMEM)] * len(shapes),
        scratch_shapes=[pltpu.VMEM(shape, jnp.float32) for shape in scratch]
        + [pltpu.SemaphoreType.DMA((6,))] * (1 if far else 0),
        compiler_params=pltpu.CompilerParams(vmem_limit_bytes=LIMIT),
        cost_estimate=pl.CostEstimate(flops=flops, bytes_accessed=0, transcendentals=0),
    )(*flags, *near, *far)


def first_kernel(places, width, row, lead, rhs, far_lead, *refs):
    others, (solved, shuffled, lead_other, *held, sems) = (
        refs[: len(places) - 1],
        refs[len(places) - 1 :],
    )
    cands = rhs.shape[1]

    @pl.when(row[0] == 0)
    def _():
        copies = [
            pltpu.make_async_copy(other.at[:width], place, sems.at[at])
            for at, (other, place) in enumerate(zip(others, held))
        ]
        copies.append(
            pltpu.make_async_copy(
                far_lead.at[:, : 2 * width], lead_other, sems.at[len(copies)]
            )
        )
        for copy in copies:
            copy.start()
        for copy in copies:
            copy.wait()
        blocks = jnp.concatenate([rhs[:width]] + [place[...] for place in held], axis=1)
        inverse = jnp.concatenate([lead[:, :width], lead_other[:, :width]], axis=0)
        first = dot(inverse, blocks, 1)
        solved[...] = first
        middle = slice(width, 2 * width)
        corner = jnp.concatenate([lead[:, middle], lead_other[:, middle]], axis=0)
        total = dot(corner, first, 0)
        pieces = [total[:, at * cands : (at + 1) * cands] for at in range(len(places))]
        pieces[0] = pieces[0] - rhs[middle]
        for at, place in enumerate(places):
            shuffled[:, at * cands : (at + 1) * cands] = pieces[place]


def second_kernel(places, row, lead, far_lead, sent, got, first, bundle, *refs):
    inverse_other, sums, more, sems = refs
    width = sums.shape[0]
    cands = sums.shape[1] // len(places)

    last = slice(2 * width, 3 * width)

    @pl.when(row[0] == 0)
    def _():
        copies = [
            pltpu.make_async_copy(sent, sums, sems.at[0]),
            pltpu.make_async_copy(got, more, sems.at[1]),
            pltpu.make_async_copy(far_lead.at[:, last], inverse_other, sems.at[2]),
        ]
        for copy in copies:
            copy.start()
        for copy in copies:
            copy.wait()
        both = jnp.concatenate([lead[:, last], inverse_other[...]], axis=0)
        rest = [sums[:, place * cands : (place + 1) * cands] for place in places]
        second = dot(both, -(jnp.concatenate(rest, axis=1) + more[...]), 1)
        bundle[...] = second

    @pl.when(row[0] == 1)
    def _():
        copy = pltpu.make_async_copy(first, bundle, sems.at[3])
        copy.start()
        copy.wait()


def rows_kernel(row, held, got, mine, base, whole, early, beside, tail, own, send, *refs):
    other, sems = refs
    n_design, cands = base.shape
    depth = held.shape[0] // 2
    parts = [slice(at * n_design // 2, (at + 1) * n_design // 2) for at in range(2)]
    is_odd = row[0] % 2 == 1

    def fetch(at, source):
        return pltpu.make_async_copy(source, other.at[:, parts[at]], sems.at[at])

    @pl.when(row[0] > 0)
    def _():
        sources = [
            (row[0] == 1, [beside.at[:, part] for part in parts]),
            ((row[0] > 1) & ~is_odd, [early, tail]),
            ((row[0] > 1) & is_odd, [whole.at[:, part] for part in parts]),
        ]
        for at in range(2):
            for chosen, pieces in sources:
                pl.when(chosen)(lambda at=at, pieces=pieces: fetch(at, pieces[at]).start())
        has_first = (row[0] == 1) | ((row[0] > 1) & ~is_odd)
        first = jnp.where(has_first, held[...], got[...])
        second = jnp.where(has_first, got[...], held[...])
        solved = jnp.concatenate(
            [first[:depth], second[:depth], first[depth:], second[depth:]], axis=0
        )
        for at, part in enumerate(parts):
            fetch(at, whole.at[:, part]).wait()
            factors = jnp.concatenate([mine[:, part], other[:, part]], axis=0)
            partial = dot(solved, factors, 0)
            own[part] = base[part] - partial[:cands].T
            send[part] = partial[cands:].T


def top_kernel(offsets, col, pair, *refs):
    others, out = refs[:-1], refs[-1]
    cands = out.shape[1]
    depth = pair.shape[0] // 4
    n_cols = len(offsets)
    sources = [pair[:, :cands]] + [other[...] for other in others]
    for panel in range(2):
        pieces = []
        for source in sources:
            for at in (2 * panel, 2 * panel + 1):
                pieces.append(source[at * depth : (at + 1) * depth])
        pieces = [pieces[offsets.index(at)] for at in range(n_cols)]
        bit = 1
        while bit < n_cols:
            flipped = (col[0] & bit) != 0
            pieces = [jnp.where(flipped, pieces[at ^ bit], pieces[at]) for at in range(n_cols)]
            bit *= 2
        for at, piece in enumerate(pieces):
            place = (panel * n_cols + at) * depth
            out[place : place + depth] = piece


def make_on_device(n_rows, n_cols):
    half = n_cols // 2

    def swap(array, flip, rows):
        pairs = [
            (row * n_cols + col, row * n_cols + (col ^ flip))
            for row in rows
            for col in range(n_cols)
        ]
        return lax.ppermute(array, AXES, pairs)

    def send_down(array, offset, have):
        pairs = [
            (row * n_cols + col, target(row, offset) * n_cols + col)
            for row in have
            for col in range(n_cols)
        ]
        return lax.ppermute(array, AXES, pairs)

    def target(row, offset):
        return (row + offset) ^ (1 if row < 2 and offset > 1 else 0)

    def spread(array, row_id, low, radix, have):
        digit = (row_id // low) % radix
        result = array
        for step in (2, 1, 3) if radix == 4 else range(1, radix):
            result = jnp.where(digit == step, send_down(array, step * low, have), result)
        return result, [target(row, step * low) for row in have for step in range(radix)]

    def broadcast_outer(array, row_id):
        low = n_rows
        have = [0, 1]
        while low > 2:
            radix = min(4, low // 2)
            low //= radix
            array, have = spread(array, row_id, low, radix, have)
        return array

    def swap_cores(array):
        pairs = [
            (row * n_cols + col, (row ^ 1) * n_cols + col)
            for row in range(n_rows)
            for col in range(n_cols)
        ]
        return lax.ppermute(array, AXES, pairs)

    def block(array, place, cands):
        return array[:, place * cands : (place + 1) * cands]

    def shuffle(array, flip, cands):
        return jnp.concatenate([block(array, at ^ flip, cands) for at in range(half)], axis=1)

    def on_device(cross_kernel, factor_panels, block_inverses):
        row_id = lax.axis_index("rows")
        col_id = lax.axis_index("cols")
        width = block_inverses.shape[2]
        depth = block_inverses.shape[1]
        n_design, cands = cross_kernel.shape
        count = n_design // 2
        top = [0]
        beside = [1]
        evens, odds = range(2, n_rows, 2), range(3, n_rows, 2)
        flat = factor_panels.reshape(2 * depth, n_design)

        lead = jnp.concatenate(
            [block_inverses[0], factor_panels[0, :, width : 2 * width], block_inverses[1]], axis=1
        )
        lead, rhs = lax.optimization_barrier((lead, cross_kernel))
        lead_other = swap(lead, half, top)
        rhs_others = [swap(rhs, step, top) for step in range(1, half)]
        whole = swap(flat, half, odds)
        arrived = swap(flat[:, :count], half, evens)
        lead_other, tail = lax.optimization_barrier((lead_other, flat[:, count:]))

        places = [at ^ 1 for at in range(half)]
        first, shuffled = call(
            functools.partial(first_kernel, places, width),
            [(2 * depth, half * cands), (width, half * cands)],
            6 * width * half * cands * (2 * depth + 2 * depth),
            [lead, rhs],
            [lead_other, *rhs_others],
            row_id,
            [(depth, 2 * width)] + [(width, cands)] * len(rhs_others),
        )
        shuffled, first, arrived, whole = lax.optimization_barrier(
            (shuffled, first, arrived, whole)
        )
        sums = got = swap(shuffled, 1, top)
        bit = 2
        while bit < half:
            update = shuffle(shuffled, 1, cands) + sums
            got = swap(shuffle(update, bit, cands), bit, top)
            sums = sums + got
            bit *= 2
        first_beside = send_down(first, 1, top)
        (bundle,) = call(
            functools.partial(second_kernel, places),
            [(2 * depth, half * cands)],
            6 * 2 * depth * width * half * cands,
            [lead],
            [lead_other, shuffled, sums, first_beside],
            row_id,
            [(depth, width)] + [(width, half * cands)] * 2,
        )
        first_beside, late = lax.optimization_barrier((first_beside, flat))
        late = swap(late, half, beside)
        held = broadcast_outer(bundle, row_id)
        held, late = lax.optimization_barrier((held, late))
        tail = swap(tail, half, evens)
        solved = [held, swap_cores(held)]

        pair = jnp.concatenate([first, held], axis=0)
        others = [swap(block(pair, step, cands), step, top) for step in range(1, half)]
        offsets = [at for step in range(half) for at in (step, step ^ half)]
        (top_rows,) = call(
            functools.partial(top_kernel, offsets),
            [(2 * width, cands)],
            0,
            [pair, *others],
            flag=col_id,
        )

        fresh, send = call(
            rows_kernel,
            [(n_design, cands), (n_design, (half - 1) * cands)],
            6 * n_design * 4 * depth * half * cands,
            [*solved, flat, cross_kernel],
            [whole, arrived, late, tail],
            row_id,
            [(2 * depth, n_design)],
        )
        for step in range(1, half):
            fresh = fresh - swap(block(send, step - 1, cands), step, range(1, n_rows))
        return jnp.where(row_id == 0, top_rows, fresh)

    return on_device


def solution(mesh):
    in_specs = (P("rows", "cols"), P(None, "cols", "rows"), P(None, "cols", None))
    out_specs = P("rows", "cols")
    return jax.shard_map(
        make_on_device(mesh.shape["rows"], mesh.shape["cols"]),
        mesh=mesh,
        in_specs=in_specs,
        out_specs=out_specs,
        check_vma=False,
    )
```

```python
import functools
import jax
import jax.numpy as jnp
from jax import lax
from jax.experimental import pallas as pl
from jax.experimental.pallas import tpu as pltpu
from jax.sharding import PartitionSpec as P

AXES = ("rows", "cols")
LIMIT = 12 * 1024 * 1024


def split(array):
    high = array.astype(jnp.bfloat16)
    return high, (array - high.astype(jnp.float32)).astype(jnp.bfloat16)


def dot(left, right, left_dim):
    def one(a, b):
        return lax.dot_general(
            a, b, (((left_dim,), (0,)), ((), ())), preferred_element_type=jnp.float32
        )

    left_high, left_low = split(left)
    right_high, right_low = split(right)
    return one(left_high, right_high) + (one(left_high, right_low) + one(left_low, right_high))


def call(kernel, shapes, flops, near, far=(), flag=None, scratch=()):
    flags = [] if flag is None else [flag.astype(jnp.int32).reshape(1)]
    spaces = [pltpu.SMEM] * len(flags) + [pltpu.VMEM] * len(near) + [pltpu.HBM] * len(far)
    return pl.pallas_call(
        kernel,
        out_shape=[jax.ShapeDtypeStruct(shape, jnp.float32) for shape in shapes],
        in_specs=[pl.BlockSpec(memory_space=space) for space in spaces],
        out_specs=[pl.BlockSpec(memory_space=pltpu.VMEM)] * len(shapes),
        scratch_shapes=[pltpu.VMEM(shape, jnp.float32) for shape in scratch]
        + [pltpu.SemaphoreType.DMA((6,))] * (1 if far else 0),
        compiler_params=pltpu.CompilerParams(vmem_limit_bytes=LIMIT),
        cost_estimate=pl.CostEstimate(flops=flops, bytes_accessed=0, transcendentals=0),
    )(*flags, *near, *far)


def first_kernel(places, width, row, lead, rhs, far_lead, *refs):
    others, (solved, shuffled, lead_other, *held, sems) = (
        refs[: len(places) - 1],
        refs[len(places) - 1 :],
    )
    cands = rhs.shape[1]

    @pl.when(row[0] == 0)
    def _():
        copies = [
            pltpu.make_async_copy(other.at[:width], place, sems.at[at])
            for at, (other, place) in enumerate(zip(others, held))
        ]
        copies.append(
            pltpu.make_async_copy(
                far_lead.at[:, : 2 * width], lead_other, sems.at[len(copies)]
            )
        )
        for copy in copies:
            copy.start()
        for copy in copies:
            copy.wait()
        blocks = jnp.concatenate([rhs[:width]] + [place[...] for place in held], axis=1)
        inverse = jnp.concatenate([lead[:, :width], lead_other[:, :width]], axis=0)
        first = dot(inverse, blocks, 1)
        solved[...] = first
        middle = slice(width, 2 * width)
        corner = jnp.concatenate([lead[:, middle], lead_other[:, middle]], axis=0)
        total = dot(corner, first, 0)
        pieces = [total[:, at * cands : (at + 1) * cands] for at in range(len(places))]
        pieces[0] = pieces[0] - rhs[middle]
        for at, place in enumerate(places):
            shuffled[:, at * cands : (at + 1) * cands] = pieces[place]


def second_kernel(places, row, lead, far_lead, sent, got, first, bundle, *refs):
    inverse_other, sums, more, sems = refs
    width = sums.shape[0]
    cands = sums.shape[1] // len(places)

    last = slice(2 * width, 3 * width)

    @pl.when(row[0] == 0)
    def _():
        copies = [
            pltpu.make_async_copy(sent, sums, sems.at[0]),
            pltpu.make_async_copy(got, more, sems.at[1]),
            pltpu.make_async_copy(far_lead.at[:, last], inverse_other, sems.at[2]),
        ]
        for copy in copies:
            copy.start()
        for copy in copies:
            copy.wait()
        both = jnp.concatenate([lead[:, last], inverse_other[...]], axis=0)
        rest = [sums[:, place * cands : (place + 1) * cands] for place in places]
        second = dot(both, -(jnp.concatenate(rest, axis=1) + more[...]), 1)
        bundle[...] = second

    @pl.when(row[0] == 1)
    def _():
        copy = pltpu.make_async_copy(first, bundle, sems.at[3])
        copy.start()
        copy.wait()


def rows_kernel(row, held, got, flat, whole, early, beside, tail, cross, own, send, *refs):
    mine, other, base, sems = refs
    n_design, cands = base.shape
    depth = held.shape[0] // 2
    parts = [slice(at * n_design // 2, (at + 1) * n_design // 2) for at in range(2)]
    is_odd = row[0] % 2 == 1

    def fetch(at, source):
        return pltpu.make_async_copy(source, other.at[:, parts[at]], sems.at[at])

    @pl.when(row[0] > 0)
    def _():
        copies = []
        for at, part in enumerate(parts):
            copies.append(
                [
                    pltpu.make_async_copy(flat.at[:, part], mine.at[:, part], sems.at[2 + at]),
                    pltpu.make_async_copy(cross.at[part], base.at[part], sems.at[4 + at]),
                ]
            )
        sources = [
            (row[0] == 1, [beside.at[:, part] for part in parts]),
            ((row[0] > 1) & ~is_odd, [early, tail]),
            ((row[0] > 1) & is_odd, [whole.at[:, part] for part in parts]),
        ]
        for at in range(2):
            for chosen, pieces in sources:
                pl.when(chosen)(lambda at=at, pieces=pieces: fetch(at, pieces[at]).start())
            for copy in copies[at]:
                copy.start()
        has_first = (row[0] == 1) | ((row[0] > 1) & ~is_odd)
        first = jnp.where(has_first, held[...], got[...])
        second = jnp.where(has_first, got[...], held[...])
        solved = jnp.concatenate(
            [first[:depth], second[:depth], first[depth:], second[depth:]], axis=0
        )
        for at, part in enumerate(parts):
            fetch(at, whole.at[:, part]).wait()
            for copy in copies[at]:
                copy.wait()
            factors = jnp.concatenate([mine[:, part], other[:, part]], axis=0)
            partial = dot(solved, factors, 0)
            own[part] = base[part] - partial[:cands].T
            send[part] = partial[cands:].T


def top_kernel(offsets, col, pair, *refs):
    others, out = refs[:-1], refs[-1]
    cands = out.shape[1]
    depth = pair.shape[0] // 4
    n_cols = len(offsets)
    sources = [pair[:, :cands]] + [other[...] for other in others]
    for panel in range(2):
        pieces = []
        for source in sources:
            for at in (2 * panel, 2 * panel + 1):
                pieces.append(source[at * depth : (at + 1) * depth])
        pieces = [pieces[offsets.index(at)] for at in range(n_cols)]
        bit = 1
        while bit < n_cols:
            flipped = (col[0] & bit) != 0
            pieces = [jnp.where(flipped, pieces[at ^ bit], pieces[at]) for at in range(n_cols)]
            bit *= 2
        for at, piece in enumerate(pieces):
            place = (panel * n_cols + at) * depth
            out[place : place + depth] = piece


def make_on_device(n_rows, n_cols):
    half = n_cols // 2

    def swap(array, flip, rows):
        pairs = [
            (row * n_cols + col, row * n_cols + (col ^ flip))
            for row in rows
            for col in range(n_cols)
        ]
        return lax.ppermute(array, AXES, pairs)

    def send_down(array, offset, have):
        pairs = [
            (row * n_cols + col, target(row, offset) * n_cols + col)
            for row in have
            for col in range(n_cols)
        ]
        return lax.ppermute(array, AXES, pairs)

    def target(row, offset):
        return (row + offset) ^ (1 if row < 2 and offset > 1 else 0)

    def spread(array, row_id, low, radix, have):
        digit = (row_id // low) % radix
        result = array
        for step in (2, 3, 1) if radix == 4 else range(1, radix):
            result = jnp.where(digit == step, send_down(array, step * low, have), result)
        return result, [target(row, step * low) for row in have for step in range(radix)]

    def broadcast_outer(array, row_id):
        low = n_rows
        have = [0, 1]
        while low > 2:
            radix = min(4, low // 2)
            low //= radix
            array, have = spread(array, row_id, low, radix, have)
        return array

    def swap_cores(array):
        pairs = [
            (row * n_cols + col, (row ^ 1) * n_cols + col)
            for row in range(n_rows)
            for col in range(n_cols)
        ]
        return lax.ppermute(array, AXES, pairs)

    def block(array, place, cands):
        return array[:, place * cands : (place + 1) * cands]

    def shuffle(array, flip, cands):
        return jnp.concatenate([block(array, at ^ flip, cands) for at in range(half)], axis=1)

    def on_device(cross_kernel, factor_panels, block_inverses):
        row_id = lax.axis_index("rows")
        col_id = lax.axis_index("cols")
        width = block_inverses.shape[2]
        depth = block_inverses.shape[1]
        n_design, cands = cross_kernel.shape
        count = n_design // 2
        top = [0]
        beside = [1]
        evens, odds = range(2, n_rows, 2), range(3, n_rows, 2)
        flat = factor_panels.reshape(2 * depth, n_design)

        lead = jnp.concatenate(
            [block_inverses[0], factor_panels[0, :, width : 2 * width], block_inverses[1]], axis=1
        )
        lead, rhs = lax.optimization_barrier((lead, cross_kernel))
        lead_other = swap(lead, half, top)
        rhs_others = [swap(rhs, step, top) for step in range(1, half)]
        whole = swap(flat, half, odds)
        arrived = swap(flat[:, :count], half, evens)
        lead_other, tail = lax.optimization_barrier((lead_other, flat[:, count:]))

        places = [at ^ 1 for at in range(half)]
        first, shuffled = call(
            functools.partial(first_kernel, places, width),
            [(2 * depth, half * cands), (width, half * cands)],
            6 * width * half * cands * (2 * depth + 2 * depth),
            [lead, rhs],
            [lead_other, *rhs_others],
            row_id,
            [(depth, 2 * width)] + [(width, cands)] * len(rhs_others),
        )
        shuffled, first, arrived, whole = lax.optimization_barrier(
            (shuffled, first, arrived, whole)
        )
        sums = got = swap(shuffled, 1, top)
        bit = 2
        while bit < half:
            update = shuffle(shuffled, 1, cands) + sums
            got = swap(shuffle(update, bit, cands), bit, top)
            sums = sums + got
            bit *= 2
        first_beside = send_down(first, 1, top)
        (bundle,) = call(
            functools.partial(second_kernel, places),
            [(2 * depth, half * cands)],
            6 * 2 * depth * width * half * cands,
            [lead],
            [lead_other, shuffled, sums, first_beside],
            row_id,
            [(depth, width)] + [(width, half * cands)] * 2,
        )
        first_beside, late = lax.optimization_barrier((first_beside, flat))
        late = swap(late, half, beside)
        held = broadcast_outer(bundle, row_id)
        held, late = lax.optimization_barrier((held, late))
        tail = swap(tail, half, evens)
        solved = [held, swap_cores(held)]

        pair = jnp.concatenate([first, held], axis=0)
        others = [swap(block(pair, step, cands), step, top) for step in range(1, half)]
        offsets = [at for step in range(half) for at in (step, step ^ half)]
        (top_rows,) = call(
            functools.partial(top_kernel, offsets),
            [(2 * width, cands)],
            0,
            [pair, *others],
            flag=col_id,
        )

        fresh, send = call(
            rows_kernel,
            [(n_design, cands), (n_design, (half - 1) * cands)],
            6 * n_design * 4 * depth * half * cands,
            solved,
            [flat, whole, arrived, late, tail, cross_kernel],
            row_id,
            [(2 * depth, n_design)] * 2 + [(n_design, cands)],
        )
        for step in range(1, half):
            fresh = fresh - swap(block(send, step - 1, cands), step, range(1, n_rows))
        return jnp.where(row_id == 0, top_rows, fresh)

    return on_device


def solution(mesh):
    in_specs = (P("rows", "cols"), P(None, "cols", "rows"), P(None, "cols", None))
    out_specs = P("rows", "cols")
    return jax.shard_map(
        make_on_device(mesh.shape["rows"], mesh.shape["cols"]),
        mesh=mesh,
        in_specs=in_specs,
        out_specs=out_specs,
        check_vma=False,
    )
```

```python
import functools
import jax
import jax.numpy as jnp
from jax import lax
from jax.experimental import pallas as pl
from jax.experimental.pallas import tpu as pltpu
from jax.sharding import PartitionSpec as P

AXES = ("rows", "cols")
LIMIT = 12 * 1024 * 1024


def split(array):
    high = array.astype(jnp.bfloat16)
    return high, (array - high.astype(jnp.float32)).astype(jnp.bfloat16)


def dot(left, right, left_dim):
    def one(a, b):
        return lax.dot_general(
            a, b, (((left_dim,), (0,)), ((), ())), preferred_element_type=jnp.float32
        )

    left_high, left_low = split(left)
    right_high, right_low = split(right)
    both = one(jnp.concatenate([left_high, left_low], axis=1 - left_dim), right_high)
    count = both.shape[0] // 2
    return both[:count] + (one(left_high, right_low) + both[count:])


def call(kernel, shapes, flops, near, far=(), flag=None, scratch=()):
    flags = [] if flag is None else [flag.astype(jnp.int32).reshape(1)]
    spaces = [pltpu.SMEM] * len(flags) + [pltpu.VMEM] * len(near) + [pltpu.HBM] * len(far)
    return pl.pallas_call(
        kernel,
        out_shape=[jax.ShapeDtypeStruct(shape, jnp.float32) for shape in shapes],
        in_specs=[pl.BlockSpec(memory_space=space) for space in spaces],
        out_specs=[pl.BlockSpec(memory_space=pltpu.VMEM)] * len(shapes),
        scratch_shapes=[pltpu.VMEM(shape, jnp.float32) for shape in scratch]
        + [pltpu.SemaphoreType.DMA((6,))] * (1 if far else 0),
        compiler_params=pltpu.CompilerParams(vmem_limit_bytes=LIMIT),
        cost_estimate=pl.CostEstimate(flops=flops, bytes_accessed=0, transcendentals=0),
    )(*flags, *near, *far)


def first_kernel(places, width, row, lead, rhs, far_lead, *refs):
    others, (solved, shuffled, lead_other, *held, sems) = (
        refs[: len(places) - 1],
        refs[len(places) - 1 :],
    )
    cands = rhs.shape[1]

    @pl.when(row[0] == 0)
    def _():
        copies = [
            pltpu.make_async_copy(other.at[:width], place, sems.at[at])
            for at, (other, place) in enumerate(zip(others, held))
        ]
        copies.append(
            pltpu.make_async_copy(
                far_lead.at[:, : 2 * width], lead_other, sems.at[len(copies)]
            )
        )
        for copy in copies:
            copy.start()
        for copy in copies:
            copy.wait()
        blocks = jnp.concatenate([rhs[:width]] + [place[...] for place in held], axis=1)
        inverse = jnp.concatenate([lead[:, :width], lead_other[:, :width]], axis=0)
        first = dot(inverse, blocks, 1)
        solved[...] = first
        middle = slice(width, 2 * width)
        corner = jnp.concatenate([lead[:, middle], lead_other[:, middle]], axis=0)
        total = dot(corner, first, 0)
        pieces = [total[:, at * cands : (at + 1) * cands] for at in range(len(places))]
        pieces[0] = pieces[0] - rhs[middle]
        for at, place in enumerate(places):
            shuffled[:, at * cands : (at + 1) * cands] = pieces[place]


def second_kernel(places, row, lead, far_lead, sent, got, first, bundle, *refs):
    inverse_other, sums, more, sems = refs
    width = sums.shape[0]
    cands = sums.shape[1] // len(places)

    last = slice(2 * width, 3 * width)

    @pl.when(row[0] == 0)
    def _():
        copies = [
            pltpu.make_async_copy(sent, sums, sems.at[0]),
            pltpu.make_async_copy(got, more, sems.at[1]),
            pltpu.make_async_copy(far_lead.at[:, last], inverse_other, sems.at[2]),
        ]
        for copy in copies:
            copy.start()
        for copy in copies:
            copy.wait()
        both = jnp.concatenate([lead[:, last], inverse_other[...]], axis=0)
        rest = [sums[:, place * cands : (place + 1) * cands] for place in places]
        second = dot(both, -(jnp.concatenate(rest, axis=1) + more[...]), 1)
        bundle[...] = second

    @pl.when(row[0] == 1)
    def _():
        copy = pltpu.make_async_copy(first, bundle, sems.at[3])
        copy.start()
        copy.wait()


def rows_kernel(row, held, got, flat, whole, early, beside, tail, cross, own, send, *refs):
    mine, other, base, sems = refs
    n_design, cands = base.shape
    depth = held.shape[0] // 2
    parts = [slice(at * n_design // 2, (at + 1) * n_design // 2) for at in range(2)]
    is_odd = row[0] % 2 == 1

    def fetch(at, source):
        return pltpu.make_async_copy(source, other.at[:, parts[at]], sems.at[at])

    @pl.when(row[0] > 0)
    def _():
        copies = []
        for at, part in enumerate(parts):
            copies.append(
                [
                    pltpu.make_async_copy(flat.at[:, part], mine.at[:, part], sems.at[2 + at]),
                    pltpu.make_async_copy(cross.at[part], base.at[part], sems.at[4 + at]),
                ]
            )
        sources = [
            (row[0] == 1, [beside.at[:, part] for part in parts]),
            ((row[0] > 1) & ~is_odd, [early, tail]),
            ((row[0] > 1) & is_odd, [whole.at[:, part] for part in parts]),
        ]
        for at in range(2):
            for chosen, pieces in sources:
                pl.when(chosen)(lambda at=at, pieces=pieces: fetch(at, pieces[at]).start())
            for copy in copies[at]:
                copy.start()
        has_first = (row[0] == 1) | ((row[0] > 1) & ~is_odd)
        first = jnp.where(has_first, held[...], got[...])
        second = jnp.where(has_first, got[...], held[...])
        solved = jnp.concatenate(
            [first[:depth], second[:depth], first[depth:], second[depth:]], axis=0
        )
        for at, part in enumerate(parts):
            fetch(at, whole.at[:, part]).wait()
            for copy in copies[at]:
                copy.wait()
            factors = jnp.concatenate([mine[:, part], other[:, part]], axis=0)
            partial = dot(solved, factors, 0)
            own[part] = base[part] - partial[:cands].T
            send[part] = partial[cands:].T


def top_kernel(offsets, col, pair, *refs):
    others, out = refs[:-1], refs[-1]
    cands = out.shape[1]
    depth = pair.shape[0] // 4
    n_cols = len(offsets)
    sources = [pair[:, :cands]] + [other[...] for other in others]
    for panel in range(2):
        pieces = []
        for source in sources:
            for at in (2 * panel, 2 * panel + 1):
                pieces.append(source[at * depth : (at + 1) * depth])
        pieces = [pieces[offsets.index(at)] for at in range(n_cols)]
        bit = 1
        while bit < n_cols:
            flipped = (col[0] & bit) != 0
            pieces = [jnp.where(flipped, pieces[at ^ bit], pieces[at]) for at in range(n_cols)]
            bit *= 2
        for at, piece in enumerate(pieces):
            place = (panel * n_cols + at) * depth
            out[place : place + depth] = piece


def make_on_device(n_rows, n_cols):
    half = n_cols // 2

    def swap(array, flip, rows):
        pairs = [
            (row * n_cols + col, row * n_cols + (col ^ flip))
            for row in rows
            for col in range(n_cols)
        ]
        return lax.ppermute(array, AXES, pairs)

    def send_down(array, offset, have):
        pairs = [
            (row * n_cols + col, target(row, offset) * n_cols + col)
            for row in have
            for col in range(n_cols)
        ]
        return lax.ppermute(array, AXES, pairs)

    def target(row, offset):
        return (row + offset) ^ (1 if row < 2 and offset > 1 else 0)

    def spread(array, row_id, low, radix, have):
        digit = (row_id // low) % radix
        result = array
        for step in (2, 1, 3) if radix == 4 else range(1, radix):
            result = jnp.where(digit == step, send_down(array, step * low, have), result)
        return result, [target(row, step * low) for row in have for step in range(radix)]

    def broadcast_outer(array, row_id):
        low = n_rows
        have = [0, 1]
        while low > 2:
            radix = min(4, low // 2)
            low //= radix
            array, have = spread(array, row_id, low, radix, have)
        return array

    def swap_cores(array):
        pairs = [
            (row * n_cols + col, (row ^ 1) * n_cols + col)
            for row in range(n_rows)
            for col in range(n_cols)
        ]
        return lax.ppermute(array, AXES, pairs)

    def block(array, place, cands):
        return array[:, place * cands : (place + 1) * cands]

    def shuffle(array, flip, cands):
        return jnp.concatenate([block(array, at ^ flip, cands) for at in range(half)], axis=1)

    def on_device(cross_kernel, factor_panels, block_inverses):
        row_id = lax.axis_index("rows")
        col_id = lax.axis_index("cols")
        width = block_inverses.shape[2]
        depth = block_inverses.shape[1]
        n_design, cands = cross_kernel.shape
        count = n_design // 2
        top = [0]
        beside = [1]
        evens, odds = range(2, n_rows, 2), range(3, n_rows, 2)
        flat = factor_panels.reshape(2 * depth, n_design)

        lead = jnp.concatenate(
            [block_inverses[0], factor_panels[0, :, width : 2 * width], block_inverses[1]], axis=1
        )
        lead, rhs = lax.optimization_barrier((lead, cross_kernel))
        lead_other = swap(lead, half, top)
        rhs_others = [swap(rhs, step, top) for step in range(1, half)]
        whole = swap(flat, half, odds)
        arrived = swap(flat[:, :count], half, evens)
        lead_other, tail = lax.optimization_barrier((lead_other, flat[:, count:]))

        places = [at ^ 1 for at in range(half)]
        first, shuffled = call(
            functools.partial(first_kernel, places, width),
            [(2 * depth, half * cands), (width, half * cands)],
            6 * width * half * cands * (2 * depth + 2 * depth),
            [lead, rhs],
            [lead_other, *rhs_others],
            row_id,
            [(depth, 2 * width)] + [(width, cands)] * len(rhs_others),
        )
        shuffled, first, arrived, whole = lax.optimization_barrier(
            (shuffled, first, arrived, whole)
        )
        sums = got = swap(shuffled, 1, top)
        bit = 2
        while bit < half:
            update = shuffle(shuffled, 1, cands) + sums
            got = swap(shuffle(update, bit, cands), bit, top)
            sums = sums + got
            bit *= 2
        first_beside = send_down(first, 1, top)
        (bundle,) = call(
            functools.partial(second_kernel, places),
            [(2 * depth, half * cands)],
            6 * 2 * depth * width * half * cands,
            [lead],
            [lead_other, shuffled, sums, first_beside],
            row_id,
            [(depth, width)] + [(width, half * cands)] * 2,
        )
        first_beside, late = lax.optimization_barrier((first_beside, flat))
        late = swap(late, half, beside)
        held = broadcast_outer(bundle, row_id)
        held, late = lax.optimization_barrier((held, late))
        tail = swap(tail, half, evens)
        solved = [held, swap_cores(held)]

        pair = jnp.concatenate([first, held], axis=0)
        others = [swap(block(pair, step, cands), step, top) for step in range(1, half)]
        offsets = [at for step in range(half) for at in (step, step ^ half)]
        (top_rows,) = call(
            functools.partial(top_kernel, offsets),
            [(2 * width, cands)],
            0,
            [pair, *others],
            flag=col_id,
        )

        fresh, send = call(
            rows_kernel,
            [(n_design, cands), (n_design, (half - 1) * cands)],
            6 * n_design * 4 * depth * half * cands,
            solved,
            [flat, whole, arrived, late, tail, cross_kernel],
            row_id,
            [(2 * depth, n_design)] * 2 + [(n_design, cands)],
        )
        for step in range(1, half):
            fresh = fresh - swap(block(send, step - 1, cands), step, range(1, n_rows))
        return jnp.where(row_id == 0, top_rows, fresh)

    return on_device


def solution(mesh):
    in_specs = (P("rows", "cols"), P(None, "cols", "rows"), P(None, "cols", None))
    out_specs = P("rows", "cols")
    return jax.shard_map(
        make_on_device(mesh.shape["rows"], mesh.shape["cols"]),
        mesh=mesh,
        in_specs=in_specs,
        out_specs=out_specs,
        check_vma=False,
    )
```

```python
import functools
import jax
import jax.numpy as jnp
from jax import lax
from jax.experimental import pallas as pl
from jax.experimental.pallas import tpu as pltpu
from jax.sharding import PartitionSpec as P

AXES = ("rows", "cols")
LIMIT = 12 * 1024 * 1024


def split(array):
    high = array.astype(jnp.bfloat16)
    return high, (array - high.astype(jnp.float32)).astype(jnp.bfloat16)


def dot(left, right, left_dim):
    def one(a, b):
        return lax.dot_general(
            a, b, (((left_dim,), (0,)), ((), ())), preferred_element_type=jnp.float32
        )

    left_high, left_low = split(left)
    right_high, right_low = split(right)
    return one(left_high, right_high) + (one(left_high, right_low) + one(left_low, right_high))


def call(kernel, shapes, flops, near, far=(), flag=None, scratch=()):
    flags = [] if flag is None else [flag.astype(jnp.int32).reshape(1)]
    spaces = [pltpu.SMEM] * len(flags) + [pltpu.VMEM] * len(near) + [pltpu.HBM] * len(far)
    return pl.pallas_call(
        kernel,
        out_shape=[jax.ShapeDtypeStruct(shape, jnp.float32) for shape in shapes],
        in_specs=[pl.BlockSpec(memory_space=space) for space in spaces],
        out_specs=[pl.BlockSpec(memory_space=pltpu.VMEM)] * len(shapes),
        scratch_shapes=[pltpu.VMEM(shape, jnp.float32) for shape in scratch]
        + [pltpu.SemaphoreType.DMA((6,))] * (1 if far else 0),
        compiler_params=pltpu.CompilerParams(vmem_limit_bytes=LIMIT),
        cost_estimate=pl.CostEstimate(flops=flops, bytes_accessed=0, transcendentals=0),
    )(*flags, *near, *far)


def first_kernel(places, width, row, lead, rhs, far_lead, *refs):
    others, (solved, shuffled, lead_other, *held, sems) = (
        refs[: len(places) - 1],
        refs[len(places) - 1 :],
    )
    cands = rhs.shape[1]

    @pl.when(row[0] == 0)
    def _():
        copies = [
            pltpu.make_async_copy(other.at[:width], place, sems.at[at])
            for at, (other, place) in enumerate(zip(others, held))
        ]
        copies.append(
            pltpu.make_async_copy(
                far_lead.at[:, : 2 * width], lead_other, sems.at[len(copies)]
            )
        )
        for copy in copies:
            copy.start()
        for copy in copies:
            copy.wait()
        blocks = jnp.concatenate([rhs[:width]] + [place[...] for place in held], axis=1)
        inverse = jnp.concatenate([lead[:, :width], lead_other[:, :width]], axis=0)
        first = dot(inverse, blocks, 1)
        solved[...] = first
        middle = slice(width, 2 * width)
        corner = jnp.concatenate([lead[:, middle], lead_other[:, middle]], axis=0)
        total = dot(corner, first, 0)
        pieces = [total[:, at * cands : (at + 1) * cands] for at in range(len(places))]
        pieces[0] = pieces[0] - rhs[middle]
        for at, place in enumerate(places):
            shuffled[:, at * cands : (at + 1) * cands] = pieces[place]


def second_kernel(places, row, lead, far_lead, sent, got, first, bundle, *refs):
    inverse_other, sums, more, sems = refs
    width = sums.shape[0]
    cands = sums.shape[1] // len(places)

    last = slice(2 * width, 3 * width)

    @pl.when(row[0] == 0)
    def _():
        copies = [
            pltpu.make_async_copy(sent, sums, sems.at[0]),
            pltpu.make_async_copy(got, more, sems.at[1]),
            pltpu.make_async_copy(far_lead.at[:, last], inverse_other, sems.at[2]),
        ]
        for copy in copies:
            copy.start()
        for copy in copies:
            copy.wait()
        both = jnp.concatenate([lead[:, last], inverse_other[...]], axis=0)
        rest = [sums[:, place * cands : (place + 1) * cands] for place in places]
        second = dot(both, -(jnp.concatenate(rest, axis=1) + more[...]), 1)
        bundle[...] = second

    @pl.when(row[0] == 1)
    def _():
        copy = pltpu.make_async_copy(first, bundle, sems.at[3])
        copy.start()
        copy.wait()


def rows_kernel(row, held, got, flat, whole, early, beside, tail, cross, own, send, *refs):
    mine, other, base, sems = refs
    n_design, cands = base.shape
    depth = held.shape[0] // 2
    parts = [slice(at * n_design // 2, (at + 1) * n_design // 2) for at in range(2)]
    is_odd = row[0] % 2 == 1

    def fetch(at, source):
        return pltpu.make_async_copy(source, other.at[:, parts[at]], sems.at[at])

    @pl.when(row[0] > 0)
    def _():
        copies = []
        for at, part in enumerate(parts):
            copies.append(
                [
                    pltpu.make_async_copy(flat.at[:, part], mine.at[:, part], sems.at[2 + at]),
                    pltpu.make_async_copy(cross.at[part], base.at[part], sems.at[4 + at]),
                ]
            )
        sources = [
            (row[0] == 1, [beside.at[:, part] for part in parts]),
            ((row[0] > 1) & ~is_odd, [early, tail]),
            ((row[0] > 1) & is_odd, [whole.at[:, part] for part in parts]),
        ]
        for at in range(2):
            for chosen, pieces in sources:
                pl.when(chosen)(lambda at=at, pieces=pieces: fetch(at, pieces[at]).start())
            for copy in copies[at]:
                copy.start()
        has_first = (row[0] == 1) | ((row[0] > 1) & ~is_odd)
        first = jnp.where(has_first, held[...], got[...])
        second = jnp.where(has_first, got[...], held[...])
        solved = jnp.concatenate(
            [first[:depth], second[:depth], first[depth:], second[depth:]], axis=0
        )
        for at, part in enumerate(parts):
            fetch(at, whole.at[:, part]).wait()
            for copy in copies[at]:
                copy.wait()
            factors = jnp.concatenate([mine[:, part], other[:, part]], axis=0)
            partial = dot(solved, factors, 0)
            own[part] = base[part] - partial[:cands].T
            send[part] = partial[cands:].T


def top_kernel(offsets, col, pair, *refs):
    others, out = refs[:-1], refs[-1]
    cands = out.shape[1]
    depth = pair.shape[0] // 4
    n_cols = len(offsets)
    sources = [pair[:, :cands]] + [other[...] for other in others]
    for panel in range(2):
        pieces = []
        for source in sources:
            for at in (2 * panel, 2 * panel + 1):
                pieces.append(source[at * depth : (at + 1) * depth])
        pieces = [pieces[offsets.index(at)] for at in range(n_cols)]
        bit = 1
        while bit < n_cols:
            flipped = (col[0] & bit) != 0
            pieces = [jnp.where(flipped, pieces[at ^ bit], pieces[at]) for at in range(n_cols)]
            bit *= 2
        for at, piece in enumerate(pieces):
            place = (panel * n_cols + at) * depth
            out[place : place + depth] = piece


def make_on_device(n_rows, n_cols):
    half = n_cols // 2

    def swap(array, flip, rows):
        pairs = [
            (row * n_cols + col, row * n_cols + (col ^ flip))
            for row in rows
            for col in range(n_cols)
        ]
        return lax.ppermute(array, AXES, pairs)

    def send_down(array, offset, have):
        pairs = [
            (row * n_cols + col, target(row, offset) * n_cols + col)
            for row in have
            for col in range(n_cols)
        ]
        return lax.ppermute(array, AXES, pairs)

    def target(row, offset):
        return (row + offset) ^ (1 if row < 2 and offset > 1 else 0)

    def spread(array, row_id, low, radix, have):
        digit = (row_id // low) % radix
        result = array
        for step in (3, 1, 2) if radix == 4 else range(1, radix):
            result = jnp.where(digit == step, send_down(array, step * low, have), result)
        return result, [target(row, step * low) for row in have for step in range(radix)]

    def broadcast_outer(array, row_id):
        low = n_rows
        have = [0, 1]
        while low > 2:
            radix = min(4, low // 2)
            low //= radix
            array, have = spread(array, row_id, low, radix, have)
        return array

    def swap_cores(array):
        pairs = [
            (row * n_cols + col, (row ^ 1) * n_cols + col)
            for row in range(n_rows)
            for col in range(n_cols)
        ]
        return lax.ppermute(array, AXES, pairs)

    def block(array, place, cands):
        return array[:, place * cands : (place + 1) * cands]

    def shuffle(array, flip, cands):
        return jnp.concatenate([block(array, at ^ flip, cands) for at in range(half)], axis=1)

    def on_device(cross_kernel, factor_panels, block_inverses):
        row_id = lax.axis_index("rows")
        col_id = lax.axis_index("cols")
        width = block_inverses.shape[2]
        depth = block_inverses.shape[1]
        n_design, cands = cross_kernel.shape
        count = n_design // 2
        top = [0]
        beside = [1]
        evens, odds = range(2, n_rows, 2), range(3, n_rows, 2)
        flat = factor_panels.reshape(2 * depth, n_design)

        lead = jnp.concatenate(
            [block_inverses[0], factor_panels[0, :, width : 2 * width], block_inverses[1]], axis=1
        )
        lead, rhs = lax.optimization_barrier((lead, cross_kernel))
        lead_other = swap(lead, half, top)
        rhs_others = [swap(rhs, step, top) for step in range(1, half)]
        whole = swap(flat, half, odds)
        arrived = swap(flat[:, :count], half, evens)
        lead_other, tail = lax.optimization_barrier((lead_other, flat[:, count:]))

        places = [at ^ 1 for at in range(half)]
        first, shuffled = call(
            functools.partial(first_kernel, places, width),
            [(2 * depth, half * cands), (width, half * cands)],
            6 * width * half * cands * (2 * depth + 2 * depth),
            [lead, rhs],
            [lead_other, *rhs_others],
            row_id,
            [(depth, 2 * width)] + [(width, cands)] * len(rhs_others),
        )
        shuffled, first, arrived, whole = lax.optimization_barrier(
            (shuffled, first, arrived, whole)
        )
        sums = got = swap(shuffled, 1, top)
        bit = 2
        while bit < half:
            update = shuffle(shuffled, 1, cands) + sums
            got = swap(shuffle(update, bit, cands), bit, top)
            sums = sums + got
            bit *= 2
        first_beside = send_down(first, 1, top)
        (bundle,) = call(
            functools.partial(second_kernel, places),
            [(2 * depth, half * cands)],
            6 * 2 * depth * width * half * cands,
            [lead],
            [lead_other, shuffled, sums, first_beside],
            row_id,
            [(depth, width)] + [(width, half * cands)] * 2,
        )
        first_beside, late = lax.optimization_barrier((first_beside, flat))
        late = swap(late, half, beside)
        held = broadcast_outer(bundle, row_id)
        held, late = lax.optimization_barrier((held, late))
        tail = swap(tail, half, evens)
        solved = [held, swap_cores(held)]

        pair = jnp.concatenate([first, held], axis=0)
        others = [swap(block(pair, step, cands), step, top) for step in range(1, half)]
        offsets = [at for step in range(half) for at in (step, step ^ half)]
        (top_rows,) = call(
            functools.partial(top_kernel, offsets),
            [(2 * width, cands)],
            0,
            [pair, *others],
            flag=col_id,
        )

        fresh, send = call(
            rows_kernel,
            [(n_design, cands), (n_design, (half - 1) * cands)],
            6 * n_design * 4 * depth * half * cands,
            solved,
            [flat, whole, arrived, late, tail, cross_kernel],
            row_id,
            [(2 * depth, n_design)] * 2 + [(n_design, cands)],
        )
        for step in range(1, half):
            fresh = fresh - swap(block(send, step - 1, cands), step, range(1, n_rows))
        return jnp.where(row_id == 0, top_rows, fresh)

    return on_device


def solution(mesh):
    in_specs = (P("rows", "cols"), P(None, "cols", "rows"), P(None, "cols", None))
    out_specs = P("rows", "cols")
    return jax.shard_map(
        make_on_device(mesh.shape["rows"], mesh.shape["cols"]),
        mesh=mesh,
        in_specs=in_specs,
        out_specs=out_specs,
        check_vma=False,
    )
```
